32 devices in a mesh: seq: 8 (over z, y), head: 4 (over x, core).
Axes of the slice: x: 2, y: 2, z: 4, core: 2. Of those that a mesh axis runs over, the one named last changes fastest.
Arguments:
- queries: bfloat16 [1536, 4096], P('seq', 'head'), may hold values from -125 to 125
- key_vectors: bfloat16 [1536, 4096], P('seq', 'head'), may hold values from -21 to 21
- values: bfloat16 [1536, 4096], P('seq', 'head'), may hold values from -6 to 6
- cotangent: bfloat16 [1536, 4096], P('seq', 'head'), may hold values from -6 to 6
- cluster: int32 [1536, 1], P('seq'), may hold values from 0 to 1; in each aligned block of 192 rows (0 to 191, 192 to 383, ...) at most 192 rows name the same one
- block_pattern: int32 [2, 12, 12], replicated, may hold values from 0 to 1, as said below
Outputs:
- attended: bfloat16 [1536, 4096], P('seq', 'head')
- query_grad: bfloat16 [1536, 4096], P('seq', 'head')
- key_grad: bfloat16 [1536, 4096], P('seq', 'head')
- value_grad: bfloat16 [1536, 4096], P('seq', 'head')
The draws below stay inside these ranges and needn't reach their ends.
Inputs may be any that keep to these rules, and one draw needn't show every extreme that they name: Within the rows of one device no cluster is named by more than 192 rows, and in every draw some cluster is named by exactly 192 rows of some device. Every diagonal entry block_pattern[g, b, b] is 1.
All inputs are finite; a program needn't handle non-finite values.
Results may differ from the reference program's by a relative error of at most 0.0061.
Values may be sent and summed in bfloat16 or wider, within the bound.
No kernel may reach another device: no remote copies, remote signals or barrier semaphores. Data moves between devices by JAX's collectives and lax.ppermute only.
A program may use at most 128 MiB of HBM per device.

```python
import math
import jax
import jax.numpy as jnp
import numpy as np
from jax import lax

HEADS = 32
HEAD_DIM = 128
T_DEV = 192
GS = 4
BLK = 128
SEQ = 1536
GROUPS = 2
CAP = 192
NB = 12


def draw_queries(key, part):
    first_key = jax.random.fold_in(key, 0)
    shape_full = (SEQ, HEADS * HEAD_DIM)
    return jnp.clip(jax.random.normal(first_key, shape_full, jnp.float32), -6.0, 6.0).astype(jnp.bfloat16)


def draw_key_vectors(key, part):
    first_key = jax.random.fold_in(key, 0)
    feature_total = HEADS * HEAD_DIM
    shape_full = (SEQ, feature_total)
    column_scale = 1.0 + 2.0 * jnp.arange(feature_total, dtype=jnp.float32) / feature_total
    return (jnp.clip(jax.random.normal(first_key, shape_full, jnp.float32), -6.0, 6.0) * column_scale[None, :]).astype(jnp.bfloat16)


def draw_block_pattern(key, part):
    random_bits = jax.random.randint(key, (GROUPS, NB, NB), 0, 2)
    diagonal_mask = jnp.arange(NB)[:, None] == jnp.arange(NB)[None, :]
    return jnp.where(diagonal_mask[None, :, :], 1, random_bits).astype(jnp.int32)


def block_scale(stream_key, extent, cuts, least, top_value):
    gain, own = 1.0, jax.random.fold_in(stream_key, 6)
    for position, parts in cuts:
        steps = jnp.exp(jax.random.uniform(jax.random.fold_in(own, position), (parts,), jnp.float32, least / len(cuts), top_value / len(cuts)))
        gain = gain * jnp.repeat(steps, extent[position] // parts).reshape([-1 if axis == position else 1 for axis in range(len(extent))])
    return gain


def assign_block(own_key, own, number, rows, number_of, top, most, skew):
    ranking = jax.random.permutation(own_key, number_of)
    heavy_load, ordinary = shares(number_of, rows * top, most, skew, True), shares(number_of, rows * top, most, skew, False)
    places = jnp.arange(number_of)

    def named(sizes, rotation):
        used = int((sizes > 0).sum())
        fixed = max(1, used // 4)
        passed = fixed + (places - fixed + rotation * (used - fixed)) % max(1, number_of - fixed)
        return jnp.zeros((number_of,), jnp.int32).at[ranking[jnp.where(places < fixed, places, passed)]].set(jnp.asarray(sizes, jnp.int32))

    sizes = jnp.where(number % 4 == 0, named(heavy_load, number // 4), named(ordinary, number - number // 4 - 1))
    mixed = jax.random.permutation(jax.random.fold_in(own, 3), number_of)
    giver, sink = mixed[0:number_of // 2 * 2:2], mixed[1:number_of // 2 * 2:2]
    margin = jnp.minimum(sizes[giver] - 1, most - sizes[sink]) // 2
    margin = jnp.where((giver == ranking[0]) | (sink == ranking[0]) | (sizes[sink] == 0), 0, jnp.maximum(margin, 0))
    passed = jax.random.randint(jax.random.fold_in(own, 4), (number_of // 2,), 0, 1 << 20) % (margin + 1)
    sizes = sizes.at[giver].add(-passed).at[sink].add(passed)
    labels = jnp.searchsorted(jnp.cumsum(sizes), jnp.arange(rows * top), side="right").astype(jnp.int32)
    grid = labels.reshape(top, rows).T
    grid = grid[jax.random.permutation(jax.random.fold_in(own, 1), rows)]
    rotation = jax.random.randint(jax.random.fold_in(own, 2), (rows, 1), 0, top)
    return jnp.take_along_axis(grid, (jnp.arange(top)[None, :] + rotation) % top, axis=1)


def shares(amount, total, limit, skew, full):
    portions = [(1 << 20) // math.isqrt(grade ** skew) + 1 for grade in range(1, amount + 1)]
    largest = limit if full else min(limit, max(-(-total // amount), total * portions[0] // sum(portions)))
    least = 1 if total - largest >= amount - 1 else 0
    given, surplus = [largest] + [least] * (amount - 1), total - largest - least * (amount - 1)
    while surplus > 0:
        movable = [i for i in range(1, amount) if given[i] < largest] or [i for i in range(1, amount) if given[i] < limit]
        whole, remaining = sum([portions[i] for i in movable]), surplus
        for i in movable:
            addition = min(limit - given[i], max(1, remaining * portions[i] // whole), surplus)
            given[i] = given[i] + addition
            surplus = surplus - addition
    return np.array(given)


def gaussian(stream_key, dims, spread, bound, cuts=(), kind=jnp.bfloat16):
    factor_of = block_scale(stream_key, dims, cuts, -0.22, 0.18) if cuts else 1.0
    drawn = jax.random.normal(stream_key, dims, jnp.float32) * spread * factor_of
    return jnp.minimum(jnp.maximum(drawn, -bound), bound).astype(kind)


def setup_inputs(seed: int = 0) -> dict:
    streams_of = jax.random.split(jax.random.key(seed), 7)
    queries = draw_queries(jax.random.fold_in(streams_of[6], 71), 0)
    key_vectors = draw_key_vectors(jax.random.fold_in(streams_of[6], 71), 0)
    values = gaussian(streams_of[2], (SEQ, HEADS * HEAD_DIM), 1.0, 6.0, ((0, 8), (1, 4)))
    cotangent = gaussian(streams_of[3], (SEQ, HEADS * HEAD_DIM), 1.0, 6.0, ((0, 8), (1, 4)))
    cluster_keys = jax.random.split(jax.random.fold_in(streams_of[4], 1), SEQ // T_DEV)
    cluster_turns = jax.random.permutation(jax.random.fold_in(streams_of[4], 3), SEQ // T_DEV)
    cluster = jax.vmap(lambda own, number: assign_block(jax.random.fold_in(streams_of[4], 2), own, number, T_DEV, GROUPS, 1, CAP, 2))(cluster_keys, cluster_turns).reshape((SEQ, 1))
    block_pattern = draw_block_pattern(jax.random.fold_in(streams_of[6], 71), 0)
    return {"queries": queries, "key_vectors": key_vectors, "values": values, "cotangent": cotangent, "cluster": cluster, "block_pattern": block_pattern}


NEG_FILL = -1e+30
EPSILON = 1e-05

def contract_last(left_side, right_side):
    return lax.dot_general(left_side, right_side, (((1,), (1,)), ((), ())), preferred_element_type=jnp.float32)

def contract_first(left_side, right_side):
    return lax.dot_general(left_side, right_side, (((0,), (0,)), ((), ())), preferred_element_type=jnp.float32)

def head_terms(query_rows, key_rows, value_rows, grad_rows, visible, score_scale):
    scores = jnp.where(visible, contract_last(query_rows, key_rows) * score_scale, NEG_FILL)
    row_max = lax.optimization_barrier(jnp.max(scores, axis=1, keepdims=True))
    weights = jnp.where(visible, jnp.exp(scores - row_max), 0.0)
    row_total = jnp.maximum(lax.optimization_barrier(jnp.sum(weights, axis=1, keepdims=True)), 1.0)
    probabilities = weights / row_total
    prob_half = probabilities.astype(jnp.bfloat16)
    attended = jnp.dot(prob_half, value_rows, preferred_element_type=jnp.float32).astype(jnp.bfloat16)
    prob_grad = contract_last(grad_rows, value_rows)
    row_delta = lax.optimization_barrier(jnp.sum(probabilities * prob_grad, axis=1, keepdims=True))
    score_grad = (probabilities * (prob_grad - row_delta)).astype(jnp.bfloat16)
    query_grad = (jnp.dot(score_grad, key_rows, preferred_element_type=jnp.float32) * score_scale).astype(jnp.bfloat16)
    key_grad = (contract_first(score_grad, query_rows) * score_scale).astype(jnp.bfloat16)
    value_grad = contract_first(prob_half, grad_rows).astype(jnp.bfloat16)
    return (attended, query_grad, key_grad, value_grad)

def reference(queries, key_vectors, values, cotangent, cluster, block_pattern):
    features = HEADS * HEAD_DIM
    score_scale = HEAD_DIM ** (-0.5)
    key_float = key_vectors.astype(jnp.float32)
    key_rms = jnp.sqrt(lax.optimization_barrier(jnp.mean(key_float * key_float, axis=1, keepdims=True)) + EPSILON)
    normed_float = key_float / key_rms
    normed = normed_float.astype(jnp.bfloat16)
    cluster_ids = cluster[:, 0].astype(jnp.int32)
    order = jnp.argsort(cluster_ids, stable=True).astype(jnp.int32)
    counts = lax.optimization_barrier(jnp.sum((cluster_ids[:, None] == jnp.arange(GROUPS, dtype=jnp.int32)[None, :]).astype(jnp.int32), axis=0))
    starts = (jnp.cumsum(counts) - counts).astype(jnp.int32)
    longest = GS * 2 * T_DEV
    padded = jnp.concatenate([order, jnp.full((longest,), SEQ, jnp.int32)])
    empty_half = jnp.zeros((SEQ, features), jnp.bfloat16)

    def per_cluster(running, cluster_index):
        taken = lax.dynamic_slice_in_dim(padded, starts[cluster_index], longest)
        present = jnp.arange(longest, dtype=jnp.int32) < counts[cluster_index]
        target = jnp.where(present, taken, SEQ).astype(jnp.int32)
        safe_rows = jnp.minimum(target, SEQ - 1)
        blocks = safe_rows // BLK
        pattern = lax.dynamic_index_in_dim(block_pattern, cluster_index, 0, keepdims=False)
        allowed = jnp.take(pattern[blocks], blocks, axis=1) == 1
        visible = allowed & (target[None, :] <= target[:, None]) & present[:, None] & present[None, :]
        query_rows = queries[safe_rows]
        key_rows = normed[safe_rows]
        value_rows = values[safe_rows]
        grad_rows = cotangent[safe_rows]

        def per_head(head_index):
            column_start = head_index * HEAD_DIM
            return head_terms(lax.dynamic_slice_in_dim(query_rows, column_start, HEAD_DIM, 1), lax.dynamic_slice_in_dim(key_rows, column_start, HEAD_DIM, 1), lax.dynamic_slice_in_dim(value_rows, column_start, HEAD_DIM, 1), lax.dynamic_slice_in_dim(grad_rows, column_start, HEAD_DIM, 1), visible, score_scale)
        results = lax.map(per_head, jnp.arange(HEADS, dtype=jnp.int32))
        updated = []
        for stored, result in zip(running, results):
            flat_result = jnp.transpose(result, (1, 0, 2)).reshape(longest, features)
            updated.append(stored.at[target].set(flat_result, mode='drop'))
        return (tuple(updated), None)
    finals, unused = lax.scan(per_cluster, (empty_half, empty_half, empty_half, empty_half), jnp.arange(GROUPS, dtype=jnp.int32))
    attended, query_grad, normed_grad, value_grad = finals
    grad_float = normed_grad.astype(jnp.float32)
    inner = lax.optimization_barrier(jnp.sum(normed_float * grad_float, axis=1, keepdims=True)) / features
    key_grad = ((grad_float - normed_float * inner) / key_rms).astype(jnp.bfloat16)
    return (attended, query_grad, key_grad, value_grad)
```

```python
import functools

import jax
import jax.numpy as jnp
from jax import lax
from jax.experimental import pallas as pl
from jax.experimental.pallas import tpu as pltpu
from jax.sharding import PartitionSpec as P

HEADS = 32
HEAD_DIM = 128
GS = 4
BLK = 128


NEG_FILL = -1e30
EPSILON = 1e-05
LOG2_E = 1.4426950408889634
LANES = 128
ID_ROWS = 16
QUERY_TILE = 256
VMEM_BYTES = 48 << 20


def contract_last(left_side, right_side):
    return lax.dot_general(
        left_side, right_side, (((1,), (1,)), ((), ())), preferred_element_type=jnp.float32
    )


def contract_first(left_side, right_side):
    return lax.dot_general(
        left_side, right_side, (((0,), (0,)), ((), ())), preferred_element_type=jnp.float32
    )


def visible_mask(pattern, query_pos, query_live, key_pos, key_live):
    pattern_rows = pattern[query_pos // BLK]
    allowed = jnp.take(pattern_rows, key_pos // BLK, axis=1) == 1
    causal = key_pos[None, :] <= query_pos[:, None]
    return allowed & causal & query_live[:, None] & key_live[None, :]


def cluster_ranks(table, cluster_index):
    source_count, tok_count = table.shape
    in_cluster = table == cluster_index
    token_iota = jnp.arange(tok_count, dtype=jnp.int32)
    earlier_table = (token_iota[:, None] < token_iota[None, :]).astype(jnp.bfloat16)
    earlier = jnp.dot(
        in_cluster.astype(jnp.bfloat16), earlier_table, preferred_element_type=jnp.float32
    ).astype(jnp.int32)
    global_pos = (
        jnp.arange(source_count, dtype=jnp.int32)[:, None] * tok_count + token_iota[None, :]
    )
    return (in_cluster, earlier, global_pos)


def code_positions(slot_code, global_pos, capacity):
    matches = slot_code[:, :, None] == jnp.arange(capacity, dtype=jnp.int32)[None, None, :]
    positions = jnp.sum(jnp.where(matches, global_pos[:, :, None], 0), axis=1)
    occupied = jnp.any(matches, axis=1)
    return (positions, occupied)


def rank_positions(table, cluster_index, capacity):
    in_cluster, earlier, global_pos = cluster_ranks(table, cluster_index)
    rank_code = jnp.where(in_cluster, earlier, -1)
    positions, occupied = code_positions(rank_code, global_pos, capacity)
    return (positions.reshape(-1), occupied.reshape(-1))


def dispatch_rows(outgoing):
    return lax.all_to_all(outgoing, "seq", split_axis=1, concat_axis=1, tiled=True)


def combine_rows(outgoing):
    return lax.all_to_all(outgoing, "seq", split_axis=1, concat_axis=1, tiled=True)


def forward_heads(query_slots, key_slots, value_slots, grad_slots, visible, score_scale):
    query_count, features = query_slots.shape
    key_count = key_slots.shape[0]
    head_count = features // HEAD_DIM
    attended = jnp.zeros((query_count, features), jnp.bfloat16)
    query_grad = jnp.zeros((query_count, features), jnp.bfloat16)
    side_result = jnp.zeros((2, key_count, features), jnp.float32)

    def one_head(head_index, running):
        attended_acc, query_acc, side_acc = running
        column_start = head_index * HEAD_DIM
        query_rows = lax.dynamic_slice_in_dim(query_slots, column_start, HEAD_DIM, 1)
        key_rows = lax.dynamic_slice_in_dim(key_slots, column_start, HEAD_DIM, 1)
        value_rows = lax.dynamic_slice_in_dim(value_slots, column_start, HEAD_DIM, 1)
        grad_rows = lax.dynamic_slice_in_dim(grad_slots, column_start, HEAD_DIM, 1)
        scores = jnp.where(visible, contract_last(query_rows, key_rows) * score_scale, NEG_FILL)
        row_max = jnp.max(scores, axis=1, keepdims=True)
        weights = jnp.where(visible, jnp.exp(scores - row_max), 0.0)
        row_total = jnp.maximum(jnp.sum(weights, axis=1, keepdims=True), 1.0)
        probabilities = weights / row_total
        prob_half = probabilities.astype(jnp.bfloat16)
        attended_head = jnp.dot(prob_half, value_rows, preferred_element_type=jnp.float32).astype(
            jnp.bfloat16
        )
        prob_grad = contract_last(grad_rows, value_rows)
        row_delta = jnp.sum(probabilities * prob_grad, axis=1, keepdims=True)
        score_grad = (probabilities * (prob_grad - row_delta)).astype(jnp.bfloat16)
        query_head = (
            jnp.dot(score_grad, key_rows, preferred_element_type=jnp.float32) * score_scale
        ).astype(jnp.bfloat16)
        attended_acc = lax.dynamic_update_slice_in_dim(attended_acc, attended_head, column_start, 1)
        query_acc = lax.dynamic_update_slice_in_dim(query_acc, query_head, column_start, 1)
        key_part = contract_first(score_grad, query_rows)
        value_part = contract_first(prob_half, grad_rows)
        side_acc = lax.dynamic_update_slice_in_dim(
            side_acc, jnp.stack([key_part, value_part]), column_start, 2
        )
        return (attended_acc, query_acc, side_acc)

    return lax.fori_loop(0, head_count, one_head, (attended, query_grad, side_result))


def per_device(queries, key_vectors, values, cotangent, cluster, block_pattern):
    seq_count = lax.axis_size("seq")
    tok_count, features = queries.shape
    slot_count = 2 * tok_count // seq_count
    group_count = seq_count // GS
    score_scale = HEAD_DIM ** (-0.5)
    my_index = lax.axis_index("seq")
    group_index = my_index // GS
    key_float = key_vectors.astype(jnp.float32)
    square_sum = lax.psum(jnp.sum(key_float * key_float, axis=1), "head")
    key_rms = jnp.sqrt(square_sum / (HEADS * HEAD_DIM) + EPSILON)[:, None]
    normed_float = key_float / key_rms
    normed = normed_float.astype(jnp.bfloat16)
    own_ids = cluster[:, 0]
    everyone = lax.all_gather(own_ids, "seq", axis=0, tiled=True)
    table = everyone.reshape(seq_count, tok_count)
    token_iota = jnp.arange(tok_count, dtype=jnp.int32)
    onehot_own = (own_ids[:, None] == jnp.arange(group_count, dtype=jnp.int32)[None, :]).astype(
        jnp.bfloat16
    )
    before_table = (token_iota[:, None] > token_iota[None, :]).astype(jnp.bfloat16)
    before = jnp.dot(before_table, onehot_own, preferred_element_type=jnp.float32)
    own_rank = jnp.sum(before * onehot_own.astype(jnp.float32), axis=1).astype(jnp.int32)
    pattern = lax.dynamic_index_in_dim(block_pattern, group_index, 0, keepdims=False)
    stacked_inputs = jnp.stack([queries, normed, values, cotangent])
    quarter = features // GS
    capacity = GS * slot_count
    split_inputs = stacked_inputs.reshape(4, tok_count, GS, quarter)
    placed = (
        jnp.zeros((4, group_count, capacity, GS, quarter), jnp.bfloat16)
        .at[:, own_ids, own_rank]
        .set(split_inputs)
    )
    outgoing = placed.transpose(0, 1, 3, 2, 4).reshape(4, seq_count * capacity, quarter)
    arrived = dispatch_rows(outgoing)
    flat_positions, flat_present = rank_positions(table, group_index, capacity)
    visible = visible_mask(pattern, flat_positions, flat_present, flat_positions, flat_present)
    attended, query_grad, both_terms = forward_heads(
        arrived[0], arrived[1], arrived[2], arrived[3], visible, score_scale
    )
    normed_grad = (both_terms[0] * score_scale).astype(jnp.bfloat16)
    value_slots = both_terms[1].astype(jnp.bfloat16)
    outgoing_back = jnp.stack([attended, query_grad, normed_grad, value_slots])
    returned = combine_rows(outgoing_back)
    arranged = returned.reshape(4, group_count, GS, capacity, quarter).transpose(1, 3, 0, 2, 4)
    home_rows = arranged[own_ids, own_rank].transpose(1, 0, 2, 3).reshape(4, tok_count, features)
    grad_float = home_rows[2].astype(jnp.float32)
    inner = lax.psum(jnp.sum(normed_float * grad_float, axis=1), "head")
    key_grad = (
        (grad_float - normed_float * (inner / (HEADS * HEAD_DIM))[:, None]) / key_rms
    ).astype(jnp.bfloat16)
    return (home_rows[0], home_rows[1], key_grad, home_rows[3])


def row_to_column(row, count):
    lanes = row.shape[1]
    diagonal = lax.broadcasted_iota(jnp.int32, (lanes, lanes), 0) == lax.broadcasted_iota(
        jnp.int32, (lanes, lanes), 1
    )
    spread = jnp.where(diagonal, jnp.broadcast_to(row, (lanes, lanes)), 0.0)
    return jnp.sum(spread, axis=1, keepdims=True)[:count]


def column_of(rows_ref, first_row, count):
    pieces = []
    for start in range(0, count, LANES):
        row = rows_ref[first_row + start // LANES : first_row + start // LANES + 1, :LANES]
        pieces.append(row_to_column(row.astype(jnp.float32), min(LANES, count - start)))
    return jnp.concatenate(pieces, axis=0)


def store_as_rows(out_ref, column):
    count = column.shape[0]
    out_ref[...] = jnp.zeros_like(out_ref)
    for start in range(0, count, LANES):
        size = min(LANES, count - start)
        diagonal = lax.broadcasted_iota(jnp.int32, (size, LANES), 0) == lax.broadcasted_iota(
            jnp.int32, (size, LANES), 1
        )
        spread = jnp.where(diagonal, column[start : start + size], 0.0)
        out_ref[start // LANES : start // LANES + 1, :] = jnp.sum(spread, axis=0, keepdims=True)


def pack_kernel(count, me_ref, query_ref, value_ref, grad_ref, ids_ref, *out_refs):
    tokens = query_ref.shape[0]
    width = query_ref.shape[1] // count
    for distance in range(count):
        start = pl.multiple_of((me_ref[0] ^ distance) * width, LANES)
        out_ref = out_refs[distance]
        for place, source_ref in enumerate((query_ref, value_ref, grad_ref)):
            out_ref[place * tokens : (place + 1) * tokens, :] = source_ref[:, pl.ds(start, width)]
        out_ref[3 * tokens :, :LANES] = ids_ref[...]
        if width > LANES:
            out_ref[3 * tokens :, LANES:] = jnp.zeros(
                (ID_ROWS, width - LANES), jnp.bfloat16
            )


def pack_keys_kernel(count, me_ref, key_ref, rms_ref, *out_refs):
    tokens = key_ref.shape[0]
    width = key_ref.shape[1] // count
    rms = column_of(rms_ref, 0, tokens)
    for distance in range(count):
        start = pl.multiple_of((me_ref[0] ^ distance) * width, LANES)
        key_float = key_ref[:, pl.ds(start, width)].astype(jnp.float32)
        out_refs[distance][...] = (key_float / rms).astype(jnp.bfloat16)


def attention_kernel(count, tokens, cluster_count, block_count, me_ref, pattern_ref, *refs):
    packed_refs, key_refs = refs[:count], refs[count : 2 * count]
    main_refs, key_grad_refs = refs[2 * count : 3 * count], refs[3 * count : 4 * count]
    (query_all, key_all, value_all, grad_all, ids_all, attended_all, query_grad_all,
     key_grad_all, value_grad_all) = refs[4 * count :]
    width = key_refs[0].shape[1]
    seq_len = count * tokens
    score_scale = HEAD_DIM ** (-0.5)
    exponent_scale = score_scale * LOG2_E
    tile = QUERY_TILE if seq_len % QUERY_TILE == 0 else BLK

    def rows_of(distance):
        return pl.ds(pl.multiple_of((me_ref[0] ^ distance) * tokens, 16), tokens)

    for distance in range(count):
        ids_all[rows_of(distance), :] = column_of(packed_refs[distance], 3 * tokens, tokens)
    lane = lax.broadcasted_iota(jnp.int32, (1, LANES), 1)
    lane_cluster = jnp.zeros((1, LANES), jnp.int32)
    for index in range(1, cluster_count + 1):
        lane_cluster = lane_cluster + (lane >= index * block_count).astype(jnp.int32)
    lane_block = lane - lane_cluster * block_count
    lane_cluster = lane_cluster.astype(jnp.float32)
    for block in range(block_count):
        rows = slice(block * BLK, (block + 1) * BLK)
        same = ids_all[rows, :] == lane_cluster
        allowed = pattern_ref[block : block + 1, :] == 1.0
        query_all[rows, HEAD_DIM:] = jnp.where(same & allowed, 0.0, NEG_FILL).astype(jnp.bfloat16)
        key_all[rows, HEAD_DIM:] = jnp.where(same & (lane_block == block), 1.0, 0.0).astype(
            jnp.bfloat16
        )
    for head in range(width // HEAD_DIM):
        columns = slice(head * HEAD_DIM, (head + 1) * HEAD_DIM)
        for distance in range(count):
            rows = rows_of(distance)
            query_all[rows, :HEAD_DIM] = packed_refs[distance][:tokens, columns]
            value_all[rows, :] = packed_refs[distance][tokens : 2 * tokens, columns]
            grad_all[rows, :] = packed_refs[distance][2 * tokens : 3 * tokens, columns]
            key_all[rows, :HEAD_DIM] = key_refs[distance][:, columns]
        for first in range(0, seq_len, tile):
            rows = slice(first, first + tile)
            limit = first + tile
            scores = contract_last(query_all[rows, :], key_all[:limit, :])
            column_index = lax.broadcasted_iota(jnp.int32, (tile, limit), 1)
            row_index = lax.broadcasted_iota(jnp.int32, (tile, limit), 0) + first
            scores = jnp.where(column_index <= row_index, scores, NEG_FILL)
            row_max = jnp.max(scores, axis=1, keepdims=True)
            weights = jnp.exp2((scores - row_max) * exponent_scale)
            row_total = jnp.maximum(jnp.sum(weights, axis=1, keepdims=True), 1.0)
            probabilities = weights * (1.0 / row_total)
            prob_grad = contract_last(grad_all[rows, :], value_all[:limit, :])
            row_delta = jnp.sum(probabilities * prob_grad, axis=1, keepdims=True)
            prob_half = probabilities.astype(jnp.bfloat16)
            score_grad = (probabilities * (prob_grad - row_delta)).astype(jnp.bfloat16)
            attended_all[rows, :] = jnp.dot(
                prob_half, value_all[:limit, :], preferred_element_type=jnp.float32
            ).astype(jnp.bfloat16)
            query_grad_all[rows, :] = (
                jnp.dot(
                    score_grad, key_all[:limit, :HEAD_DIM], preferred_element_type=jnp.float32
                )
                * score_scale
            ).astype(jnp.bfloat16)
            key_part = contract_first(score_grad, query_all[rows, :HEAD_DIM])
            value_part = contract_first(prob_half, grad_all[rows, :])
            if first:
                key_grad_all[:first, :] += key_part[:first]
                value_grad_all[:first, :] += value_part[:first]
            key_grad_all[rows, :] = key_part[first:]
            value_grad_all[rows, :] = value_part[first:]
        for distance in range(count):
            rows = rows_of(distance)
            main_refs[distance][:tokens, columns] = attended_all[rows, :]
            main_refs[distance][tokens : 2 * tokens, columns] = query_grad_all[rows, :]
            main_refs[distance][2 * tokens :, columns] = value_grad_all[rows, :].astype(
                jnp.bfloat16
            )
            key_grad_refs[distance][:, columns] = (key_grad_all[rows, :] * score_scale).astype(
                jnp.bfloat16
            )


def inner_kernel(count, me_ref, key_ref, rms_ref, *refs):
    grad_refs, out_ref = refs[:count], refs[count]
    tokens = key_ref.shape[0]
    width = key_ref.shape[1] // count
    total = jnp.zeros((tokens, width), jnp.float32)
    for distance in range(count):
        start = pl.multiple_of((me_ref[0] ^ distance) * width, LANES)
        key_float = key_ref[:, pl.ds(start, width)].astype(jnp.float32)
        total = total + key_float * grad_refs[distance][...].astype(jnp.float32)
    column = jnp.sum(total, axis=1, keepdims=True) / column_of(rms_ref, 0, tokens)
    store_as_rows(out_ref, column)


def final_kernel(count, feature_total, me_ref, key_ref, rms_ref, inner_ref, *refs):
    grad_refs, main_refs = refs[:count], refs[count : 2 * count]
    attended_ref, query_ref, key_out_ref, value_ref = refs[2 * count :]
    tokens = key_ref.shape[0]
    width = key_ref.shape[1] // count
    rms = column_of(rms_ref, 0, tokens)
    inner = column_of(inner_ref, 0, tokens) / feature_total
    for distance in range(count):
        columns = pl.ds(pl.multiple_of((me_ref[0] ^ distance) * width, LANES), width)
        normed_float = key_ref[:, columns].astype(jnp.float32) / rms
        grad_float = grad_refs[distance][...].astype(jnp.float32)
        key_out_ref[:, columns] = ((grad_float - normed_float * inner) / rms).astype(jnp.bfloat16)
        attended_ref[:, columns] = main_refs[distance][:tokens, :]
        query_ref[:, columns] = main_refs[distance][tokens : 2 * tokens, :]
        value_ref[:, columns] = main_refs[distance][2 * tokens :, :]


def lane_rows(vector, row_count):
    return jnp.pad(vector, (0, row_count * LANES - vector.shape[0])).reshape(row_count, LANES)


def call(kernel, out_shapes, scalars, arrays, scratch=(), vmem=VMEM_BYTES):
    return pl.pallas_call(
        kernel,
        out_shape=out_shapes,
        in_specs=[pl.BlockSpec(memory_space=pltpu.SMEM)] * len(scalars)
        + [pl.BlockSpec(memory_space=pltpu.VMEM)] * len(arrays),
        out_specs=jax.tree.map(lambda shape: pl.BlockSpec(memory_space=pltpu.VMEM), out_shapes),
        scratch_shapes=list(scratch),
        compiler_params=pltpu.CompilerParams(vmem_limit_bytes=vmem),
    )(*scalars, *arrays)


def swap(blocks):
    count = len(blocks)
    return [blocks[0]] + [
        lax.ppermute(blocks[d], "seq", [(i, i ^ d) for i in range(count)])
        for d in range(1, count)
    ]


def all_heads_apart(queries, key_vectors, values, cotangent, cluster, block_pattern):
    count = lax.axis_size("seq")
    tokens, features = queries.shape
    width = features // count
    cluster_count, block_count, _ = block_pattern.shape
    seq_len = count * tokens
    row_count = -(-tokens // LANES)
    me = lax.axis_index("seq").astype(jnp.int32).reshape(1)
    half = lambda rows, columns: jax.ShapeDtypeStruct((rows, columns), jnp.bfloat16)
    ids = lane_rows(cluster[:, 0], ID_ROWS).astype(jnp.bfloat16)
    packed = call(
        functools.partial(pack_kernel, count),
        [half(3 * tokens + ID_ROWS, width)] * count,
        [me],
        [queries, values, cotangent, ids],
    )
    packed = swap(packed)
    key_float = key_vectors.astype(jnp.float32)
    square_sum = lax.psum(jnp.sum(key_float * key_float, axis=1), "head")
    feature_total = HEADS * HEAD_DIM
    key_rms = lane_rows(jnp.sqrt(square_sum / feature_total + EPSILON), row_count)
    keys = call(
        functools.partial(pack_keys_kernel, count),
        [half(tokens, width)] * count,
        [me],
        [key_vectors, key_rms],
    )
    keys = swap(keys)
    pattern_rows = block_pattern.transpose(1, 0, 2).reshape(block_count, -1).astype(jnp.float32)
    pattern_rows = jnp.pad(pattern_rows, ((0, 0), (0, LANES - cluster_count * block_count)))
    results = call(
        functools.partial(attention_kernel, count, tokens, cluster_count, block_count),
        [half(3 * tokens, width)] * count + [half(tokens, width)] * count,
        [me],
        [pattern_rows] + packed + keys,
        [
            pltpu.VMEM((seq_len, 2 * HEAD_DIM), jnp.bfloat16),
            pltpu.VMEM((seq_len, 2 * HEAD_DIM), jnp.bfloat16),
            pltpu.VMEM((seq_len, HEAD_DIM), jnp.bfloat16),
            pltpu.VMEM((seq_len, HEAD_DIM), jnp.bfloat16),
            pltpu.VMEM((seq_len, 1), jnp.float32),
            pltpu.VMEM((seq_len, HEAD_DIM), jnp.bfloat16),
            pltpu.VMEM((seq_len, HEAD_DIM), jnp.bfloat16),
            pltpu.VMEM((seq_len, HEAD_DIM), jnp.float32),
            pltpu.VMEM((seq_len, HEAD_DIM), jnp.float32),
        ],
    )
    key_grads = swap(results[count:])
    main = swap(results[:count])
    inner = call(
        functools.partial(inner_kernel, count),
        jax.ShapeDtypeStruct((row_count, LANES), jnp.float32),
        [me],
        [key_vectors, key_rms] + key_grads,
    )
    inner = lax.psum(inner, "head")
    return tuple(
        call(
            functools.partial(final_kernel, count, feature_total),
            [half(tokens, features)] * 4,
            [me],
            [key_vectors, key_rms, inner] + key_grads + main,
        )
    )


def per_device_any(queries, key_vectors, values, cotangent, cluster, block_pattern):
    count = lax.axis_size("seq")
    features = queries.shape[1]
    cluster_count, block_count, _ = block_pattern.shape
    spread = features % (count * HEAD_DIM) == 0 and count & (count - 1) == 0
    chosen = all_heads_apart if spread and cluster_count * block_count <= LANES else per_device
    return chosen(queries, key_vectors, values, cotangent, cluster, block_pattern)


def solution(mesh):
    in_specs = (
        P("seq", "head"),
        P("seq", "head"),
        P("seq", "head"),
        P("seq", "head"),
        P("seq", None),
        P(),
    )
    out_specs = (P("seq", "head"), P("seq", "head"), P("seq", "head"), P("seq", "head"))
    return jax.shard_map(
        per_device_any, mesh=mesh, in_specs=in_specs, out_specs=out_specs, check_vma=False
    )
```

```python
import functools

import jax
import jax.numpy as jnp
from jax import lax
from jax.experimental import pallas as pl
from jax.experimental.pallas import tpu as pltpu
from jax.sharding import PartitionSpec as P

HEADS = 32
HEAD_DIM = 128
GS = 4
BLK = 128


NEG_FILL = -1e30
EPSILON = 1e-05
SCORE_SCALE = HEAD_DIM ** (-0.5)
EXPONENT_SCALE = SCORE_SCALE * 1.4426950408889634
LANES = 128
ID_ROWS = 16
QUERY_TILE = 256
VMEM_BYTES = 48 << 20


def contract_last(left_side, right_side):
    return lax.dot_general(
        left_side, right_side, (((1,), (1,)), ((), ())), preferred_element_type=jnp.float32
    )


def contract_first(left_side, right_side):
    return lax.dot_general(
        left_side, right_side, (((0,), (0,)), ((), ())), preferred_element_type=jnp.float32
    )


def visible_mask(pattern, query_pos, query_live, key_pos, key_live):
    pattern_rows = pattern[query_pos // BLK]
    allowed = jnp.take(pattern_rows, key_pos // BLK, axis=1) == 1
    causal = key_pos[None, :] <= query_pos[:, None]
    return allowed & causal & query_live[:, None] & key_live[None, :]


def cluster_ranks(table, cluster_index):
    source_count, tok_count = table.shape
    in_cluster = table == cluster_index
    token_iota = jnp.arange(tok_count, dtype=jnp.int32)
    earlier_table = (token_iota[:, None] < token_iota[None, :]).astype(jnp.bfloat16)
    earlier = jnp.dot(
        in_cluster.astype(jnp.bfloat16), earlier_table, preferred_element_type=jnp.float32
    ).astype(jnp.int32)
    global_pos = (
        jnp.arange(source_count, dtype=jnp.int32)[:, None] * tok_count + token_iota[None, :]
    )
    return (in_cluster, earlier, global_pos)


def code_positions(slot_code, global_pos, capacity):
    matches = slot_code[:, :, None] == jnp.arange(capacity, dtype=jnp.int32)[None, None, :]
    positions = jnp.sum(jnp.where(matches, global_pos[:, :, None], 0), axis=1)
    occupied = jnp.any(matches, axis=1)
    return (positions, occupied)


def rank_positions(table, cluster_index, capacity):
    in_cluster, earlier, global_pos = cluster_ranks(table, cluster_index)
    rank_code = jnp.where(in_cluster, earlier, -1)
    positions, occupied = code_positions(rank_code, global_pos, capacity)
    return (positions.reshape(-1), occupied.reshape(-1))


def dispatch_rows(outgoing):
    return lax.all_to_all(outgoing, "seq", split_axis=1, concat_axis=1, tiled=True)


def combine_rows(outgoing):
    return lax.all_to_all(outgoing, "seq", split_axis=1, concat_axis=1, tiled=True)


def forward_heads(query_slots, key_slots, value_slots, grad_slots, visible, score_scale):
    query_count, features = query_slots.shape
    key_count = key_slots.shape[0]
    head_count = features // HEAD_DIM
    attended = jnp.zeros((query_count, features), jnp.bfloat16)
    query_grad = jnp.zeros((query_count, features), jnp.bfloat16)
    side_result = jnp.zeros((2, key_count, features), jnp.float32)

    def one_head(head_index, running):
        attended_acc, query_acc, side_acc = running
        column_start = head_index * HEAD_DIM
        query_rows = lax.dynamic_slice_in_dim(query_slots, column_start, HEAD_DIM, 1)
        key_rows = lax.dynamic_slice_in_dim(key_slots, column_start, HEAD_DIM, 1)
        value_rows = lax.dynamic_slice_in_dim(value_slots, column_start, HEAD_DIM, 1)
        grad_rows = lax.dynamic_slice_in_dim(grad_slots, column_start, HEAD_DIM, 1)
        scores = jnp.where(visible, contract_last(query_rows, key_rows) * score_scale, NEG_FILL)
        row_max = jnp.max(scores, axis=1, keepdims=True)
        weights = jnp.where(visible, jnp.exp(scores - row_max), 0.0)
        row_total = jnp.maximum(jnp.sum(weights, axis=1, keepdims=True), 1.0)
        probabilities = weights / row_total
        prob_half = probabilities.astype(jnp.bfloat16)
        attended_head = jnp.dot(prob_half, value_rows, preferred_element_type=jnp.float32).astype(
            jnp.bfloat16
        )
        prob_grad = contract_last(grad_rows, value_rows)
        row_delta = jnp.sum(probabilities * prob_grad, axis=1, keepdims=True)
        score_grad = (probabilities * (prob_grad - row_delta)).astype(jnp.bfloat16)
        query_head = (
            jnp.dot(score_grad, key_rows, preferred_element_type=jnp.float32) * score_scale
        ).astype(jnp.bfloat16)
        attended_acc = lax.dynamic_update_slice_in_dim(attended_acc, attended_head, column_start, 1)
        query_acc = lax.dynamic_update_slice_in_dim(query_acc, query_head, column_start, 1)
        key_part = contract_first(score_grad, query_rows)
        value_part = contract_first(prob_half, grad_rows)
        side_acc = lax.dynamic_update_slice_in_dim(
            side_acc, jnp.stack([key_part, value_part]), column_start, 2
        )
        return (attended_acc, query_acc, side_acc)

    return lax.fori_loop(0, head_count, one_head, (attended, query_grad, side_result))


def per_device(queries, key_vectors, values, cotangent, cluster, block_pattern):
    seq_count = lax.axis_size("seq")
    tok_count, features = queries.shape
    slot_count = 2 * tok_count // seq_count
    group_count = seq_count // GS
    score_scale = HEAD_DIM ** (-0.5)
    my_index = lax.axis_index("seq")
    group_index = my_index // GS
    key_float = key_vectors.astype(jnp.float32)
    square_sum = lax.psum(jnp.sum(key_float * key_float, axis=1), "head")
    key_rms = jnp.sqrt(square_sum / (HEADS * HEAD_DIM) + EPSILON)[:, None]
    normed_float = key_float / key_rms
    normed = normed_float.astype(jnp.bfloat16)
    own_ids = cluster[:, 0]
    everyone = lax.all_gather(own_ids, "seq", axis=0, tiled=True)
    table = everyone.reshape(seq_count, tok_count)
    token_iota = jnp.arange(tok_count, dtype=jnp.int32)
    onehot_own = (own_ids[:, None] == jnp.arange(group_count, dtype=jnp.int32)[None, :]).astype(
        jnp.bfloat16
    )
    before_table = (token_iota[:, None] > token_iota[None, :]).astype(jnp.bfloat16)
    before = jnp.dot(before_table, onehot_own, preferred_element_type=jnp.float32)
    own_rank = jnp.sum(before * onehot_own.astype(jnp.float32), axis=1).astype(jnp.int32)
    pattern = lax.dynamic_index_in_dim(block_pattern, group_index, 0, keepdims=False)
    stacked_inputs = jnp.stack([queries, normed, values, cotangent])
    quarter = features // GS
    capacity = GS * slot_count
    split_inputs = stacked_inputs.reshape(4, tok_count, GS, quarter)
    placed = (
        jnp.zeros((4, group_count, capacity, GS, quarter), jnp.bfloat16)
        .at[:, own_ids, own_rank]
        .set(split_inputs)
    )
    outgoing = placed.transpose(0, 1, 3, 2, 4).reshape(4, seq_count * capacity, quarter)
    arrived = dispatch_rows(outgoing)
    flat_positions, flat_present = rank_positions(table, group_index, capacity)
    visible = visible_mask(pattern, flat_positions, flat_present, flat_positions, flat_present)
    attended, query_grad, both_terms = forward_heads(
        arrived[0], arrived[1], arrived[2], arrived[3], visible, score_scale
    )
    normed_grad = (both_terms[0] * score_scale).astype(jnp.bfloat16)
    value_slots = both_terms[1].astype(jnp.bfloat16)
    outgoing_back = jnp.stack([attended, query_grad, normed_grad, value_slots])
    returned = combine_rows(outgoing_back)
    arranged = returned.reshape(4, group_count, GS, capacity, quarter).transpose(1, 3, 0, 2, 4)
    home_rows = arranged[own_ids, own_rank].transpose(1, 0, 2, 3).reshape(4, tok_count, features)
    grad_float = home_rows[2].astype(jnp.float32)
    inner = lax.psum(jnp.sum(normed_float * grad_float, axis=1), "head")
    key_grad = (
        (grad_float - normed_float * (inner / (HEADS * HEAD_DIM))[:, None]) / key_rms
    ).astype(jnp.bfloat16)
    return (home_rows[0], home_rows[1], key_grad, home_rows[3])


def row_to_column(row, count):
    lanes = row.shape[1]
    diagonal = lax.broadcasted_iota(jnp.int32, (lanes, lanes), 0) == lax.broadcasted_iota(
        jnp.int32, (lanes, lanes), 1
    )
    spread = jnp.where(diagonal, jnp.broadcast_to(row, (lanes, lanes)), 0.0)
    return jnp.sum(spread, axis=1, keepdims=True)[:count]


def column_of(rows_ref, first_row, count):
    pieces = []
    for start in range(0, count, LANES):
        row = rows_ref[first_row + start // LANES : first_row + start // LANES + 1, :LANES]
        pieces.append(row_to_column(row.astype(jnp.float32), min(LANES, count - start)))
    return jnp.concatenate(pieces, axis=0)


def store_as_rows(out_ref, first_row, column):
    count = column.shape[0]
    for start in range(0, count, LANES):
        size = min(LANES, count - start)
        diagonal = lax.broadcasted_iota(jnp.int32, (size, LANES), 0) == lax.broadcasted_iota(
            jnp.int32, (size, LANES), 1
        )
        spread = jnp.where(diagonal, column[start : start + size], 0.0)
        row = first_row + start // LANES
        out_ref[row : row + 1, :] = jnp.sum(spread, axis=0, keepdims=True)


def block_rows(index, size):
    return pl.ds(pl.multiple_of(index * size, 16), size)


def pack_kernel(half_count, query_ref, value_ref, grad_ref, ids_ref, out_ref, sems):
    tokens, features = query_ref.shape
    width = features // half_count
    stride = 3 * tokens + ID_ROWS
    copies = []
    for place, source_ref in enumerate((query_ref, value_ref, grad_ref)):
        for owner in range(half_count):
            copies.append(
                pltpu.make_async_copy(
                    source_ref.at[:, owner * width : (owner + 1) * width],
                    out_ref.at[pl.ds(owner * stride + place * tokens, tokens), :],
                    sems.at[place * half_count + owner],
                )
            )
    for copy in copies:
        copy.start()
    for owner in range(half_count):
        rows = slice(owner * stride + 3 * tokens, (owner + 1) * stride)
        out_ref[rows, :LANES] = ids_ref[...]
        out_ref[rows, LANES:] = jnp.zeros((ID_ROWS, width - LANES), jnp.bfloat16)
    for copy in copies:
        copy.wait()


def pack_keys_kernel(
    half_count, me_ref, query_ref, value_ref, grad_ref, key_ref, rms_ref, ids_ref, *out_refs
):
    tokens, features = key_ref.shape
    width = features // half_count
    single = width // 2
    is_high = me_ref[0] >= half_count
    inside = me_ref[0] & (half_count - 1)
    key_refs, cross_refs = out_refs[:half_count], out_refs[half_count:]
    rms = column_of(rms_ref, 0, tokens)

    def normed_columns(first, size):
        return (key_ref[:, pl.ds(first, size)].astype(jnp.float32) / rms).astype(jnp.bfloat16)

    for distance in range(half_count):
        first = pl.multiple_of((inside ^ distance) * width, LANES)
        cross_ref = cross_refs[distance]
        key_refs[distance][...] = normed_columns(first, width)
        cross_ref[2 * tokens :, :LANES] = ids_ref[...]
        if single > LANES:
            cross_ref[2 * tokens :, LANES:] = jnp.zeros((ID_ROWS, single - LANES), jnp.bfloat16)

        @pl.when(is_high)
        def send_down():
            second = pl.multiple_of(first + single, LANES)
            cross_ref[:tokens, :] = query_ref[:, pl.ds(second, single)]
            cross_ref[tokens : 2 * tokens, :] = grad_ref[:, pl.ds(second, single)]

        @pl.when(jnp.logical_not(is_high))
        def send_up():
            cross_ref[:tokens, :] = normed_columns(first, single)
            cross_ref[tokens : 2 * tokens, :] = value_ref[:, pl.ds(first, single)]


class Slots:
    def __init__(self, shape, me_ref, pattern_ref, packed_ref, key_refs, cross_refs):
        self.tokens, self.half_count, self.cluster_count, self.block_count = shape
        self.half_len = self.tokens * self.half_count
        self.half_blocks = self.half_len // BLK
        self.is_high = me_ref[0] >= self.half_count
        self.inside = me_ref[0] & (self.half_count - 1)
        self.pattern_ref, self.packed_ref = pattern_ref, packed_ref
        self.key_refs, self.cross_refs = key_refs, cross_refs
        lane = lax.broadcasted_iota(jnp.int32, (1, LANES), 1)
        lane_cluster = jnp.zeros((1, LANES), jnp.int32)
        for index in range(1, self.cluster_count + 1):
            lane_cluster = lane_cluster + (lane >= index * self.block_count).astype(jnp.int32)
        self.lane_block = lane - lane_cluster * self.block_count
        self.lane_cluster = lane_cluster.astype(jnp.float32)

    def own_ids(self, ids_all):
        stride = 3 * self.tokens + ID_ROWS
        for source in range(self.half_count):
            ids_all[source * self.tokens : (source + 1) * self.tokens, :] = column_of(
                self.packed_ref, source * stride + 3 * self.tokens, self.tokens
            )

    def cross_ids(self, ids_all):
        for distance in range(self.half_count):
            ids_all[block_rows(self.inside ^ distance, self.tokens), :] = column_of(
                self.cross_refs[distance], 2 * self.tokens, self.tokens
            )

    def query_features(self, ids_all, target, high):
        for block in range(self.half_blocks):
            rows = slice(block * BLK, (block + 1) * BLK)
            place = block + high * self.half_blocks
            allowed = self.pattern_ref[pl.ds(place, 1), :] == 1.0
            same = ids_all[rows, :] == self.lane_cluster
            target[rows, HEAD_DIM:] = jnp.where(same & allowed, 0.0, NEG_FILL).astype(jnp.bfloat16)

    def key_features(self, ids_all, target, high):
        for block in range(self.half_blocks):
            rows = slice(block * BLK, (block + 1) * BLK)
            place = block + high * self.half_blocks
            same = ids_all[rows, :] == self.lane_cluster
            target[rows, HEAD_DIM:] = jnp.where(same & (self.lane_block == place), 1.0, 0.0).astype(
                jnp.bfloat16
            )

    def own(self, column, query_all, key_all, value_all, grad_all):
        columns = slice(column, column + HEAD_DIM)
        stride = 3 * self.tokens + ID_ROWS
        for source in range(self.half_count):
            rows = slice(source * self.tokens, (source + 1) * self.tokens)
            for place, target in enumerate((query_all, value_all, grad_all)):
                first = source * stride + place * self.tokens
                target[rows, :HEAD_DIM] = self.packed_ref[first : first + self.tokens, columns]
        for distance in range(self.half_count):
            rows = block_rows(self.inside ^ distance, self.tokens)
            key_all[rows, :HEAD_DIM] = self.key_refs[distance][:, columns]

    def cross(self, column, first_all, second_all):
        columns = slice(column, column + HEAD_DIM)
        for distance in range(self.half_count):
            rows = block_rows(self.inside ^ distance, self.tokens)
            cross_ref = self.cross_refs[distance]
            first_all[rows, :HEAD_DIM] = cross_ref[: self.tokens, columns]
            second_all[rows, :] = cross_ref[self.tokens : 2 * self.tokens, columns]


def tile_scores(query_tile, pieces):
    results = []
    for key_all, _, limit, first in pieces:
        scores = contract_last(query_tile, key_all[:limit, :])
        if first is not None:
            column_index = lax.broadcasted_iota(jnp.int32, scores.shape, 1)
            row_index = lax.broadcasted_iota(jnp.int32, scores.shape, 0) + first
            scores = jnp.where(column_index <= row_index, scores, NEG_FILL)
        results.append(scores)
    return results


def tile_stats(scores, prob_grads):
    row_max = functools.reduce(
        jnp.maximum, [jnp.max(part, axis=1, keepdims=True) for part in scores]
    )
    weights = [jnp.exp2((part - row_max) * EXPONENT_SCALE) for part in scores]
    row_total = sum(jnp.sum(part, axis=1, keepdims=True) for part in weights)
    row_delta = sum(
        jnp.sum(part * grad, axis=1, keepdims=True) for part, grad in zip(weights, prob_grads)
    )
    return weights, row_max, row_total, row_delta


def tile_backward(query_tile, grad_tile, pieces, sums, stats, is_first):
    scores = tile_scores(query_tile, pieces)
    prob_grads = [contract_last(grad_tile, piece[1][: piece[2], :]) for piece in pieces]
    if stats is None:
        weights, _, row_total, row_delta = tile_stats(scores, prob_grads)
        inverse = 1.0 / jnp.maximum(row_total, 1.0)
        row_delta = row_delta * inverse
    else:
        row_max, inverse, row_delta = stats
        weights = [jnp.exp2((part - row_max) * EXPONENT_SCALE) for part in scores]
    attended, query_grad = 0.0, 0.0
    for index, (key_all, value_all, limit, first) in enumerate(pieces):
        probabilities = weights[index] * inverse
        prob_half = probabilities.astype(jnp.bfloat16)
        score_grad = (probabilities * (prob_grads[index] - row_delta)).astype(jnp.bfloat16)
        attended += jnp.dot(prob_half, value_all[:limit, :], preferred_element_type=jnp.float32)
        query_grad += jnp.dot(
            score_grad, key_all[:limit, :HEAD_DIM], preferred_element_type=jnp.float32
        )
        key_part = contract_first(score_grad, query_tile[:, :HEAD_DIM])
        value_part = contract_first(prob_half, grad_tile)
        key_sum, value_sum = sums[index]
        fresh = 0 if is_first else (limit if first is None else first)
        if fresh:
            key_sum[:fresh, :] += key_part[:fresh]
            value_sum[:fresh, :] += value_part[:fresh]
        if fresh < limit:
            key_sum[fresh:limit, :] = key_part[fresh:]
            value_sum[fresh:limit, :] = value_part[fresh:]
    return attended.astype(jnp.bfloat16), (query_grad * SCORE_SCALE).astype(jnp.bfloat16)


def own_tiles(half_len):
    tile = QUERY_TILE if half_len % QUERY_TILE == 0 else BLK
    return [(first, slice(first, first + tile), first + tile) for first in range(0, half_len, tile)]


def stats_kernel(shape, stat_rows, me_ref, pattern_ref, packed_ref, *refs):
    half_count = shape[1]
    key_refs, cross_refs = refs[:half_count], refs[half_count : 2 * half_count]
    out_ref, query_all, key_all, value_all, grad_all, other_query, other_grad, ids = refs[
        2 * half_count :
    ]
    slots = Slots(shape, me_ref, pattern_ref, packed_ref, key_refs, cross_refs)
    single = packed_ref.shape[1] // 2
    out_ref[...] = jnp.zeros_like(out_ref)
    slots.own_ids(ids)
    slots.key_features(ids, key_all, slots.is_high.astype(jnp.int32))

    @pl.when(slots.is_high)
    def _():
        slots.query_features(ids, query_all, 1)

    @pl.when(jnp.logical_not(slots.is_high))
    def _():
        slots.cross_ids(ids)
        slots.query_features(ids, other_query, 1)

    for head in range(single // HEAD_DIM):
        slots.own(single + head * HEAD_DIM, query_all, key_all, value_all, grad_all)
        first_row = 3 * stat_rows * head

        def note(first, found):
            for place, column in enumerate(found[1:]):
                store_as_rows(
                    out_ref, first_row + place * stat_rows + first // LANES, column
                )

        @pl.when(slots.is_high)
        def _():
            for first, rows, limit in own_tiles(slots.half_len):
                pieces = [(key_all, value_all, limit, first)]
                scores = tile_scores(query_all[rows, :], pieces)
                prob_grad = contract_last(grad_all[rows, :], value_all[:limit, :])
                note(first, tile_stats(scores, [prob_grad]))

        @pl.when(jnp.logical_not(slots.is_high))
        def _():
            slots.cross(head * HEAD_DIM, other_query, other_grad)
            for first, rows, _ in own_tiles(slots.half_len):
                pieces = [(key_all, value_all, slots.half_len, None)]
                scores = tile_scores(other_query[rows, :], pieces)
                prob_grad = contract_last(other_grad[rows, :], value_all[...])
                note(first, tile_stats(scores, [prob_grad]))


def store_own(slots, result_ref, key_refs, column, results, key_sum, value_sum):
    attended, query_grad = results
    tokens = slots.tokens
    columns = slice(column, column + HEAD_DIM)
    stride = result_ref.shape[0] // slots.half_count
    for source in range(slots.half_count):
        rows = slice(source * tokens, (source + 1) * tokens)
        first = source * stride
        result_ref[first : first + tokens, columns] = attended[rows, :]
        result_ref[first + tokens : first + 2 * tokens, columns] = query_grad[rows, :]
        result_ref[first + 2 * tokens : first + 3 * tokens, columns] = value_sum[rows, :].astype(
            jnp.bfloat16
        )
    for distance in range(slots.half_count):
        rows = block_rows(slots.inside ^ distance, tokens)
        key_refs[distance][:, columns] = (key_sum[rows, :] * SCORE_SCALE).astype(jnp.bfloat16)


def first_head_kernel(shape, me_ref, pattern_ref, packed_ref, *refs):
    half_count = shape[1]
    key_refs, cross_refs = refs[:half_count], refs[half_count : 2 * half_count]
    refs = refs[2 * half_count :]
    result_ref, key_out_refs, cross_out_refs = (
        refs[0], refs[1 : 1 + half_count], refs[1 + half_count : 1 + 2 * half_count]
    )
    (query_all, key_all, value_all, grad_all, other_key, other_value, ids, attended, query_grad,
     key_sum, value_sum, other_key_sum, other_value_sum) = refs[1 + 2 * half_count :]
    slots = Slots(shape, me_ref, pattern_ref, packed_ref, key_refs, cross_refs)
    single = packed_ref.shape[1] // 2
    high = slots.is_high.astype(jnp.int32)
    slots.own_ids(ids)
    slots.key_features(ids, key_all, high)
    slots.query_features(ids, query_all, high)

    @pl.when(slots.is_high)
    def _():
        slots.cross_ids(ids)
        slots.key_features(ids, other_key, 0)

    for head in range(single // HEAD_DIM):
        column = head * HEAD_DIM
        slots.own(column, query_all, key_all, value_all, grad_all)

        def run(others, other_sums):
            for first, rows, limit in own_tiles(slots.half_len):
                attended[rows, :], query_grad[rows, :] = tile_backward(
                    query_all[rows, :],
                    grad_all[rows, :],
                    others + [(key_all, value_all, limit, first)],
                    other_sums + [(key_sum, value_sum)],
                    None,
                    first == 0,
                )

        @pl.when(slots.is_high)
        def _():
            slots.cross(column, other_key, other_value)
            run(
                [(other_key, other_value, slots.half_len, None)],
                [(other_key_sum, other_value_sum)],
            )
            for distance in range(half_count):
                rows = block_rows(slots.inside ^ distance, slots.tokens)
                columns = slice(column, column + HEAD_DIM)
                target = cross_out_refs[distance]
                target[: slots.tokens, columns] = (other_key_sum[rows, :] * SCORE_SCALE).astype(
                    jnp.bfloat16
                )
                target[slots.tokens :, columns] = other_value_sum[rows, :].astype(jnp.bfloat16)

        @pl.when(jnp.logical_not(slots.is_high))
        def _():
            run([], [])
            for distance in range(half_count):
                cross_out_refs[distance][...] = jnp.zeros_like(cross_out_refs[distance])

        store_own(slots, result_ref, key_out_refs, column, (attended, query_grad), key_sum, value_sum)


def second_head_kernel(shape, stat_rows, me_ref, pattern_ref, packed_ref, *refs):
    half_count = shape[1]
    key_refs, cross_refs = refs[:half_count], refs[half_count : 2 * half_count]
    own_stats_ref, other_stats_ref, first_result_ref = refs[2 * half_count : 2 * half_count + 3]
    refs = refs[2 * half_count + 3 :]
    first_key_refs, first_cross_refs = refs[:half_count], refs[half_count : 2 * half_count]
    refs = refs[2 * half_count :]
    result_ref, key_out_refs, cross_out_refs = (
        refs[0], refs[1 : 1 + half_count], refs[1 + half_count : 1 + 2 * half_count]
    )
    (query_all, key_all, value_all, grad_all, other_query, other_grad, ids, attended, query_grad,
     key_sum, value_sum, other_attended, other_query_grad) = refs[1 + 2 * half_count :]
    slots = Slots(shape, me_ref, pattern_ref, packed_ref, key_refs, cross_refs)
    single = packed_ref.shape[1] // 2
    high = slots.is_high.astype(jnp.int32)
    slots.own_ids(ids)
    slots.key_features(ids, key_all, high)
    slots.query_features(ids, query_all, high)

    @pl.when(jnp.logical_not(slots.is_high))
    def _():
        slots.cross_ids(ids)
        slots.query_features(ids, other_query, 1)

    result_ref[:, :single] = first_result_ref[...]
    for distance in range(half_count):
        key_out_refs[distance][:, :single] = first_key_refs[distance][...]

    def joint_stats(head, first, size):
        found = [
            [
                column_of(
                    ref, 3 * stat_rows * head + place * stat_rows + first // LANES, size
                )
                for place in range(3)
            ]
            for ref in (own_stats_ref, other_stats_ref)
        ]
        (own_max, own_total, own_delta), (far_max, far_total, far_delta) = found
        row_max = jnp.maximum(own_max, far_max)
        own_part = jnp.exp2((own_max - row_max) * EXPONENT_SCALE)
        far_part = jnp.exp2((far_max - row_max) * EXPONENT_SCALE)
        inverse = 1.0 / jnp.maximum(own_total * own_part + far_total * far_part, 1.0)
        return row_max, inverse, (own_delta * own_part + far_delta * far_part) * inverse

    for head in range(single // HEAD_DIM):
        column = head * HEAD_DIM
        slots.own(single + column, query_all, key_all, value_all, grad_all)

        def run(joint):
            for first, rows, limit in own_tiles(slots.half_len):
                attended[rows, :], query_grad[rows, :] = tile_backward(
                    query_all[rows, :],
                    grad_all[rows, :],
                    [(key_all, value_all, limit, first)],
                    [(key_sum, value_sum)],
                    joint_stats(head, first, limit - first) if joint else None,
                    first == 0,
                )

        @pl.when(slots.is_high)
        def _():
            run(True)
            for distance in range(half_count):
                cross_out_refs[distance][...] = first_cross_refs[distance][...]

        @pl.when(jnp.logical_not(slots.is_high))
        def _():
            slots.cross(column, other_query, other_grad)
            run(False)
            for first, rows, limit in own_tiles(slots.half_len):
                other_attended[rows, :], other_query_grad[rows, :] = tile_backward(
                    other_query[rows, :],
                    other_grad[rows, :],
                    [(key_all, value_all, slots.half_len, None)],
                    [(key_sum, value_sum)],
                    joint_stats(head, first, limit - first),
                    False,
                )
            for distance in range(half_count):
                rows = block_rows(slots.inside ^ distance, slots.tokens)
                columns = slice(column, column + HEAD_DIM)
                target = cross_out_refs[distance]
                target[: slots.tokens, columns] = other_attended[rows, :]
                target[slots.tokens :, columns] = other_query_grad[rows, :]

        store_own(
            slots, result_ref, key_out_refs, single + column, (attended, query_grad), key_sum,
            value_sum,
        )


def normed_grad_of(half_count, me_ref, key_grad_refs, cross_refs, distance, tokens):
    single = key_grad_refs[distance].shape[1] // 2
    is_low = me_ref[0] < half_count
    grad_float = key_grad_refs[distance][...].astype(jnp.float32)
    far = jnp.where(is_low, cross_refs[distance][:tokens, :].astype(jnp.float32), 0.0)
    return jnp.concatenate([grad_float[:, :single] + far, grad_float[:, single:]], axis=1)


def inner_kernel(half_count, me_ref, key_ref, rms_ref, *refs):
    key_grad_refs, cross_refs = refs[:half_count], refs[half_count : 2 * half_count]
    out_ref = refs[2 * half_count]
    tokens, features = key_ref.shape
    width = features // half_count
    inside = me_ref[0] & (half_count - 1)
    total = jnp.zeros((tokens, width), jnp.float32)
    for distance in range(half_count):
        start = pl.multiple_of((inside ^ distance) * width, LANES)
        key_float = key_ref[:, pl.ds(start, width)].astype(jnp.float32)
        total = total + key_float * normed_grad_of(
            half_count, me_ref, key_grad_refs, cross_refs, distance, tokens
        )
    column = jnp.sum(total, axis=1, keepdims=True) / column_of(rms_ref, 0, tokens)
    out_ref[...] = jnp.zeros_like(out_ref)
    store_as_rows(out_ref, 0, column)


def final_kernel(half_count, feature_total, me_ref, key_ref, rms_ref, inner_ref, *refs):
    key_grad_refs, cross_refs = refs[:half_count], refs[half_count : 2 * half_count]
    result_ref, attended_ref, query_ref, key_out_ref, value_ref = refs[2 * half_count :]
    tokens, features = key_ref.shape
    width = features // half_count
    single = width // 2
    is_high = me_ref[0] >= half_count
    inside = me_ref[0] & (half_count - 1)
    rms = column_of(rms_ref, 0, tokens)
    inner = column_of(inner_ref, 0, tokens) / feature_total
    for owner in range(half_count):
        columns = slice(owner * width, (owner + 1) * width)
        for place, target in enumerate((attended_ref, query_ref, value_ref)):
            first = (owner * 3 + place) * tokens
            target[:, columns] = result_ref[first : first + tokens, :]
    for distance in range(half_count):
        start = pl.multiple_of((inside ^ distance) * width, LANES)
        columns = pl.ds(start, width)
        normed_float = key_ref[:, columns].astype(jnp.float32) / rms
        grad_float = normed_grad_of(
            half_count, me_ref, key_grad_refs, cross_refs, distance, tokens
        )
        key_out_ref[:, columns] = ((grad_float - normed_float * inner) / rms).astype(jnp.bfloat16)
        cross_ref = cross_refs[distance]

        def add(target, columns, first):
            far = cross_ref[first : first + tokens, :].astype(jnp.float32)
            target[:, columns] = (target[:, columns].astype(jnp.float32) + far).astype(jnp.bfloat16)

        @pl.when(is_high)
        def _():
            second = pl.ds(pl.multiple_of(start + single, LANES), single)
            add(attended_ref, second, 0)
            add(query_ref, second, tokens)

        @pl.when(jnp.logical_not(is_high))
        def _():
            add(value_ref, pl.ds(start, single), tokens)


def lane_rows(vector, row_count):
    return jnp.pad(vector, (0, row_count * LANES - vector.shape[0])).reshape(row_count, LANES)


def half_array(rows, columns):
    return jax.ShapeDtypeStruct((rows, columns), jnp.bfloat16)


def call(kernel, out_shapes, scalars, arrays, scratch=(), in_hbm=0):
    vmem, anywhere = pl.BlockSpec(memory_space=pltpu.VMEM), pl.BlockSpec(memory_space=pl.ANY)
    return pl.pallas_call(
        kernel,
        out_shape=out_shapes,
        in_specs=[pl.BlockSpec(memory_space=pltpu.SMEM)] * len(scalars)
        + [anywhere] * in_hbm
        + [vmem] * (len(arrays) - in_hbm),
        out_specs=jax.tree.map(lambda shape: vmem, out_shapes),
        scratch_shapes=list(scratch),
        compiler_params=pltpu.CompilerParams(vmem_limit_bytes=VMEM_BYTES),
    )(*scalars, *arrays)


def swap(block, distance):
    count = lax.axis_size("seq")
    return lax.ppermute(block, "seq", [(i, i ^ distance) for i in range(count)])


def swap_inside(blocks):
    return [blocks[0]] + [swap(block, d) for d, block in enumerate(blocks) if d]


def swap_across(blocks):
    return [swap(block, len(blocks) + d) for d, block in enumerate(blocks)]


def exchange_inside(rows):
    count = lax.axis_size("seq")
    groups = [list(range(count // 2)), list(range(count // 2, count))]
    return lax.all_to_all(
        rows, "seq", split_axis=0, concat_axis=0, tiled=True, axis_index_groups=groups
    )


def by_halves(queries, key_vectors, values, cotangent, cluster, block_pattern):
    count = lax.axis_size("seq")
    half_count = count // 2
    tokens, features = queries.shape
    width = features // half_count
    single = width // 2
    cluster_count, block_count, _ = block_pattern.shape
    half_len = half_count * tokens
    shape = (tokens, half_count, cluster_count, block_count)
    row_count = -(-tokens // LANES)
    stat_rows = -(-half_len // LANES)
    me = lax.axis_index("seq").astype(jnp.int32).reshape(1)
    ids = lane_rows(cluster[:, 0], ID_ROWS).astype(jnp.bfloat16)
    packed = call(
        functools.partial(pack_kernel, half_count),
        half_array(half_count * (3 * tokens + ID_ROWS), width),
        [],
        [queries, values, cotangent, ids],
        [pltpu.SemaphoreType.DMA((3 * half_count,))],
        in_hbm=3,
    )
    packed = exchange_inside(packed)
    key_float = key_vectors.astype(jnp.float32)
    square_sum = lax.psum(jnp.sum(key_float * key_float, axis=1), "head")
    feature_total = HEADS * HEAD_DIM
    key_rms = lane_rows(jnp.sqrt(square_sum / feature_total + EPSILON), row_count)
    sent = call(
        functools.partial(pack_keys_kernel, half_count),
        [half_array(tokens, width)] * half_count
        + [half_array(2 * tokens + ID_ROWS, single)] * half_count,
        [me],
        [queries, values, cotangent, key_vectors, key_rms, ids],
    )
    cross = swap_across(sent[half_count:])
    keys = swap_inside(sent[:half_count])
    pattern_rows = block_pattern.transpose(1, 0, 2).reshape(block_count, -1).astype(jnp.float32)
    pattern_rows = jnp.pad(pattern_rows, ((0, 0), (0, LANES - cluster_count * block_count)))
    inputs = [pattern_rows, packed] + keys + cross
    wide = pltpu.VMEM((half_len, 2 * HEAD_DIM), jnp.bfloat16)
    slim = pltpu.VMEM((half_len, HEAD_DIM), jnp.bfloat16)
    sums = pltpu.VMEM((half_len, HEAD_DIM), jnp.float32)
    ids_column = pltpu.VMEM((half_len, 1), jnp.float32)
    stats = call(
        functools.partial(stats_kernel, shape, stat_rows),
        jax.ShapeDtypeStruct((3 * stat_rows * (single // HEAD_DIM), LANES), jnp.float32),
        [me],
        inputs,
        [wide, wide, slim, slim, wide, slim, ids_column],
    )
    far_stats = swap(stats, half_count)
    first = call(
        functools.partial(first_head_kernel, shape),
        [half_array(3 * half_len, single)]
        + [half_array(tokens, single)] * half_count
        + [half_array(2 * tokens, single)] * half_count,
        [me],
        inputs,
        [wide, wide, slim, slim, wide, slim, ids_column, slim, slim, sums, sums, sums, sums],
    )
    results = call(
        functools.partial(second_head_kernel, shape, stat_rows),
        [half_array(3 * half_len, width)]
        + [half_array(tokens, width)] * half_count
        + [half_array(2 * tokens, single)] * half_count,
        [me],
        inputs + [stats, far_stats] + list(first),
        [wide, wide, slim, slim, wide, slim, ids_column, slim, slim, sums, sums, slim, slim],
    )
    key_grads = swap_inside(results[1 : 1 + half_count])
    far_parts = swap_across(results[1 + half_count :])
    main = exchange_inside(results[0])
    inner = call(
        functools.partial(inner_kernel, half_count),
        jax.ShapeDtypeStruct((row_count, LANES), jnp.float32),
        [me],
        [key_vectors, key_rms] + key_grads + far_parts,
    )
    inner = lax.psum(inner, "head")
    return tuple(
        call(
            functools.partial(final_kernel, half_count, feature_total),
            [half_array(tokens, features)] * 4,
            [me],
            [key_vectors, key_rms, inner] + key_grads + far_parts + [main],
        )
    )


def per_device_any(queries, key_vectors, values, cotangent, cluster, block_pattern):
    count = lax.axis_size("seq")
    tokens, features = queries.shape
    cluster_count, block_count, _ = block_pattern.shape
    fits = (
        count % 2 == 0
        and count & (count - 1) == 0
        and features % (count * HEAD_DIM) == 0
        and tokens % ID_ROWS == 0
        and tokens * count % (2 * BLK) == 0
        and cluster_count * block_count <= LANES
    )
    chosen = by_halves if fits else per_device
    return chosen(queries, key_vectors, values, cotangent, cluster, block_pattern)


def solution(mesh):
    in_specs = (
        P("seq", "head"),
        P("seq", "head"),
        P("seq", "head"),
        P("seq", "head"),
        P("seq", None),
        P(),
    )
    out_specs = (P("seq", "head"), P("seq", "head"), P("seq", "head"), P("seq", "head"))
    return jax.shard_map(
        per_device_any, mesh=mesh, in_specs=in_specs, out_specs=out_specs, check_vma=False
    )
```

```python
import functools

import jax
import jax.numpy as jnp
from jax import lax
from jax.experimental import pallas as pl
from jax.experimental.pallas import tpu as pltpu
from jax.sharding import PartitionSpec as P

HEADS = 32
HEAD_DIM = 128
GS = 4
BLK = 128


NEG_FILL = -1e30
EPSILON = 1e-05
SCORE_SCALE = HEAD_DIM ** (-0.5)
EXPONENT_SCALE = SCORE_SCALE * 1.4426950408889634
LANES = 128
ID_ROWS = 16
QUERY_TILE = 256
VMEM_BYTES = 32 << 20
PACK_VMEM_BYTES = 60 << 20


def contract_last(left_side, right_side):
    return lax.dot_general(
        left_side, right_side, (((1,), (1,)), ((), ())), preferred_element_type=jnp.float32
    )


def contract_first(left_side, right_side):
    return lax.dot_general(
        left_side, right_side, (((0,), (0,)), ((), ())), preferred_element_type=jnp.float32
    )


def visible_mask(pattern, query_pos, query_live, key_pos, key_live):
    pattern_rows = pattern[query_pos // BLK]
    allowed = jnp.take(pattern_rows, key_pos // BLK, axis=1) == 1
    causal = key_pos[None, :] <= query_pos[:, None]
    return allowed & causal & query_live[:, None] & key_live[None, :]


def cluster_ranks(table, cluster_index):
    source_count, tok_count = table.shape
    in_cluster = table == cluster_index
    token_iota = jnp.arange(tok_count, dtype=jnp.int32)
    earlier_table = (token_iota[:, None] < token_iota[None, :]).astype(jnp.bfloat16)
    earlier = jnp.dot(
        in_cluster.astype(jnp.bfloat16), earlier_table, preferred_element_type=jnp.float32
    ).astype(jnp.int32)
    global_pos = (
        jnp.arange(source_count, dtype=jnp.int32)[:, None] * tok_count + token_iota[None, :]
    )
    return (in_cluster, earlier, global_pos)


def code_positions(slot_code, global_pos, capacity):
    matches = slot_code[:, :, None] == jnp.arange(capacity, dtype=jnp.int32)[None, None, :]
    positions = jnp.sum(jnp.where(matches, global_pos[:, :, None], 0), axis=1)
    occupied = jnp.any(matches, axis=1)
    return (positions, occupied)


def rank_positions(table, cluster_index, capacity):
    in_cluster, earlier, global_pos = cluster_ranks(table, cluster_index)
    rank_code = jnp.where(in_cluster, earlier, -1)
    positions, occupied = code_positions(rank_code, global_pos, capacity)
    return (positions.reshape(-1), occupied.reshape(-1))


def dispatch_rows(outgoing):
    return lax.all_to_all(outgoing, "seq", split_axis=1, concat_axis=1, tiled=True)


def combine_rows(outgoing):
    return lax.all_to_all(outgoing, "seq", split_axis=1, concat_axis=1, tiled=True)


def forward_heads(query_slots, key_slots, value_slots, grad_slots, visible, score_scale):
    query_count, features = query_slots.shape
    key_count = key_slots.shape[0]
    head_count = features // HEAD_DIM
    attended = jnp.zeros((query_count, features), jnp.bfloat16)
    query_grad = jnp.zeros((query_count, features), jnp.bfloat16)
    side_result = jnp.zeros((2, key_count, features), jnp.float32)

    def one_head(head_index, running):
        attended_acc, query_acc, side_acc = running
        column_start = head_index * HEAD_DIM
        query_rows = lax.dynamic_slice_in_dim(query_slots, column_start, HEAD_DIM, 1)
        key_rows = lax.dynamic_slice_in_dim(key_slots, column_start, HEAD_DIM, 1)
        value_rows = lax.dynamic_slice_in_dim(value_slots, column_start, HEAD_DIM, 1)
        grad_rows = lax.dynamic_slice_in_dim(grad_slots, column_start, HEAD_DIM, 1)
        scores = jnp.where(visible, contract_last(query_rows, key_rows) * score_scale, NEG_FILL)
        row_max = jnp.max(scores, axis=1, keepdims=True)
        weights = jnp.where(visible, jnp.exp(scores - row_max), 0.0)
        row_total = jnp.maximum(jnp.sum(weights, axis=1, keepdims=True), 1.0)
        probabilities = weights / row_total
        prob_half = probabilities.astype(jnp.bfloat16)
        attended_head = jnp.dot(prob_half, value_rows, preferred_element_type=jnp.float32).astype(
            jnp.bfloat16
        )
        prob_grad = contract_last(grad_rows, value_rows)
        row_delta = jnp.sum(probabilities * prob_grad, axis=1, keepdims=True)
        score_grad = (probabilities * (prob_grad - row_delta)).astype(jnp.bfloat16)
        query_head = (
            jnp.dot(score_grad, key_rows, preferred_element_type=jnp.float32) * score_scale
        ).astype(jnp.bfloat16)
        attended_acc = lax.dynamic_update_slice_in_dim(attended_acc, attended_head, column_start, 1)
        query_acc = lax.dynamic_update_slice_in_dim(query_acc, query_head, column_start, 1)
        key_part = contract_first(score_grad, query_rows)
        value_part = contract_first(prob_half, grad_rows)
        side_acc = lax.dynamic_update_slice_in_dim(
            side_acc, jnp.stack([key_part, value_part]), column_start, 2
        )
        return (attended_acc, query_acc, side_acc)

    return lax.fori_loop(0, head_count, one_head, (attended, query_grad, side_result))


def per_device(queries, key_vectors, values, cotangent, cluster, block_pattern):
    seq_count = lax.axis_size("seq")
    tok_count, features = queries.shape
    slot_count = 2 * tok_count // seq_count
    group_count = seq_count // GS
    score_scale = HEAD_DIM ** (-0.5)
    my_index = lax.axis_index("seq")
    group_index = my_index // GS
    key_float = key_vectors.astype(jnp.float32)
    square_sum = lax.psum(jnp.sum(key_float * key_float, axis=1), "head")
    key_rms = jnp.sqrt(square_sum / (HEADS * HEAD_DIM) + EPSILON)[:, None]
    normed_float = key_float / key_rms
    normed = normed_float.astype(jnp.bfloat16)
    own_ids = cluster[:, 0]
    everyone = lax.all_gather(own_ids, "seq", axis=0, tiled=True)
    table = everyone.reshape(seq_count, tok_count)
    token_iota = jnp.arange(tok_count, dtype=jnp.int32)
    onehot_own = (own_ids[:, None] == jnp.arange(group_count, dtype=jnp.int32)[None, :]).astype(
        jnp.bfloat16
    )
    before_table = (token_iota[:, None] > token_iota[None, :]).astype(jnp.bfloat16)
    before = jnp.dot(before_table, onehot_own, preferred_element_type=jnp.float32)
    own_rank = jnp.sum(before * onehot_own.astype(jnp.float32), axis=1).astype(jnp.int32)
    pattern = lax.dynamic_index_in_dim(block_pattern, group_index, 0, keepdims=False)
    stacked_inputs = jnp.stack([queries, normed, values, cotangent])
    quarter = features // GS
    capacity = GS * slot_count
    split_inputs = stacked_inputs.reshape(4, tok_count, GS, quarter)
    placed = (
        jnp.zeros((4, group_count, capacity, GS, quarter), jnp.bfloat16)
        .at[:, own_ids, own_rank]
        .set(split_inputs)
    )
    outgoing = placed.transpose(0, 1, 3, 2, 4).reshape(4, seq_count * capacity, quarter)
    arrived = dispatch_rows(outgoing)
    flat_positions, flat_present = rank_positions(table, group_index, capacity)
    visible = visible_mask(pattern, flat_positions, flat_present, flat_positions, flat_present)
    attended, query_grad, both_terms = forward_heads(
        arrived[0], arrived[1], arrived[2], arrived[3], visible, score_scale
    )
    normed_grad = (both_terms[0] * score_scale).astype(jnp.bfloat16)
    value_slots = both_terms[1].astype(jnp.bfloat16)
    outgoing_back = jnp.stack([attended, query_grad, normed_grad, value_slots])
    returned = combine_rows(outgoing_back)
    arranged = returned.reshape(4, group_count, GS, capacity, quarter).transpose(1, 3, 0, 2, 4)
    home_rows = arranged[own_ids, own_rank].transpose(1, 0, 2, 3).reshape(4, tok_count, features)
    grad_float = home_rows[2].astype(jnp.float32)
    inner = lax.psum(jnp.sum(normed_float * grad_float, axis=1), "head")
    key_grad = (
        (grad_float - normed_float * (inner / (HEADS * HEAD_DIM))[:, None]) / key_rms
    ).astype(jnp.bfloat16)
    return (home_rows[0], home_rows[1], key_grad, home_rows[3])


def column_of(rows, first_row, count):
    turned = jnp.transpose(rows)
    pieces = []
    for start in range(0, count, LANES):
        place = first_row + start // LANES
        pieces.append(turned[: min(LANES, count - start), place : place + 1])
    return jnp.concatenate(pieces, axis=0)


def ids_of(ref, first_row, count):
    rows = ref[first_row : first_row + ID_ROWS, :LANES].astype(jnp.float32)
    return column_of(rows, 0, count)


def store_as_rows(out_ref, first_row, column):
    count = column.shape[0]
    for start in range(0, count, LANES):
        size = min(LANES, count - start)
        diagonal = lax.broadcasted_iota(jnp.int32, (size, LANES), 0) == lax.broadcasted_iota(
            jnp.int32, (size, LANES), 1
        )
        spread = jnp.where(diagonal, column[start : start + size], 0.0)
        row = first_row + start // LANES
        out_ref[row : row + 1, :] = jnp.sum(spread, axis=0, keepdims=True)


def block_rows(index, size):
    return pl.ds(pl.multiple_of(index * size, 16), size)


def pack_kernel(half_count, query_ref, value_ref, grad_ref, out_ref, held, sorted_rows, in_sems, out_sems):
    tokens, features = query_ref.shape
    width = features // half_count
    arrivals = [
        pltpu.make_async_copy(source_ref, held.at[place], in_sems.at[place])
        for place, source_ref in enumerate((query_ref, value_ref, grad_ref))
    ]
    for arrival in arrivals:
        arrival.start()
    copies = []
    for place, arrival in enumerate(arrivals):
        arrival.wait()
        for owner in range(half_count):
            rows = pl.ds((owner * 3 + place) * tokens, tokens)
            sorted_rows[rows, :] = held[place, :, owner * width : (owner + 1) * width]
            copy = pltpu.make_async_copy(
                sorted_rows.at[rows, :], out_ref.at[rows, :], out_sems.at[place * half_count + owner]
            )
            copy.start()
            copies.append(copy)
    for copy in copies:
        copy.wait()


def pack_keys_kernel(
    half_count, me_ref, query_ref, value_ref, grad_ref, key_ref, rms_ref, ids_ref, *out_refs
):
    tokens, features = key_ref.shape
    width = features // half_count
    single = width // 2
    is_high = me_ref[0] >= half_count
    inside = me_ref[0] & (half_count - 1)
    key_refs, cross_refs = out_refs[:half_count], out_refs[half_count:]
    rms = column_of(rms_ref[...], 0, tokens)

    def normed_columns(first, size):
        return (key_ref[:, pl.ds(first, size)].astype(jnp.float32) / rms).astype(jnp.bfloat16)

    for distance in range(half_count):
        first = pl.multiple_of((inside ^ distance) * width, LANES)
        cross_ref = cross_refs[distance]
        key_refs[distance][:tokens, :] = normed_columns(first, width)
        key_refs[distance][tokens:, :LANES] = ids_ref[...]
        key_refs[distance][tokens:, LANES:] = jnp.zeros((ID_ROWS, width - LANES), jnp.bfloat16)
        cross_ref[2 * tokens :, :LANES] = ids_ref[...]
        if single > LANES:
            cross_ref[2 * tokens :, LANES:] = jnp.zeros((ID_ROWS, single - LANES), jnp.bfloat16)

        @pl.when(is_high)
        def send_down():
            second = pl.multiple_of(first + single, LANES)
            cross_ref[:tokens, :] = query_ref[:, pl.ds(second, single)]
            cross_ref[tokens : 2 * tokens, :] = grad_ref[:, pl.ds(second, single)]

        @pl.when(jnp.logical_not(is_high))
        def send_up():
            cross_ref[:tokens, :] = normed_columns(first, single)
            cross_ref[tokens : 2 * tokens, :] = value_ref[:, pl.ds(first, single)]


class Slots:
    def __init__(self, shape, me_ref, pattern_ref, packed_ref, key_refs, cross_refs):
        self.tokens, self.half_count, self.cluster_count, self.block_count = shape
        self.half_len = self.tokens * self.half_count
        self.half_blocks = self.half_len // BLK
        self.is_high = me_ref[0] >= self.half_count
        self.inside = me_ref[0] & (self.half_count - 1)
        self.pattern_ref, self.packed_ref = pattern_ref, packed_ref
        self.key_refs, self.cross_refs = key_refs, cross_refs
        lane = lax.broadcasted_iota(jnp.int32, (1, LANES), 1)
        lane_cluster = jnp.zeros((1, LANES), jnp.int32)
        for index in range(1, self.cluster_count + 1):
            lane_cluster = lane_cluster + (lane >= index * self.block_count).astype(jnp.int32)
        self.lane_block = lane - lane_cluster * self.block_count
        self.lane_cluster = lane_cluster.astype(jnp.float32)

    def own_ids(self, ids_all):
        for distance in range(self.half_count):
            ids_all[block_rows(self.inside ^ distance, self.tokens), :] = ids_of(
                self.key_refs[distance], self.tokens, self.tokens
            )

    def cross_ids(self, ids_all):
        for distance in range(self.half_count):
            ids_all[block_rows(self.inside ^ distance, self.tokens), :] = ids_of(
                self.cross_refs[distance], 2 * self.tokens, self.tokens
            )

    def query_features(self, ids_all, target, high):
        for block in range(self.half_blocks):
            rows = slice(block * BLK, (block + 1) * BLK)
            place = block + high * self.half_blocks
            allowed = self.pattern_ref[pl.ds(place, 1), :] == 1.0
            same = ids_all[rows, :] == self.lane_cluster
            target[rows, HEAD_DIM:] = jnp.where(same & allowed, 0.0, NEG_FILL).astype(jnp.bfloat16)

    def key_features(self, ids_all, target, high):
        for block in range(self.half_blocks):
            rows = slice(block * BLK, (block + 1) * BLK)
            place = block + high * self.half_blocks
            same = ids_all[rows, :] == self.lane_cluster
            target[rows, HEAD_DIM:] = jnp.where(same & (self.lane_block == place), 1.0, 0.0).astype(
                jnp.bfloat16
            )

    def own(self, column, query_all, key_all, value_all, grad_all):
        columns = slice(column, column + HEAD_DIM)
        stride = 3 * self.tokens
        for source in range(self.half_count):
            rows = slice(source * self.tokens, (source + 1) * self.tokens)
            for place, target in enumerate((query_all, value_all, grad_all)):
                first = source * stride + place * self.tokens
                target[rows, :HEAD_DIM] = self.packed_ref[first : first + self.tokens, columns]
        for distance in range(self.half_count):
            rows = block_rows(self.inside ^ distance, self.tokens)
            key_all[rows, :HEAD_DIM] = self.key_refs[distance][: self.tokens, columns]

    def cross(self, column, first_all, second_all):
        columns = slice(column, column + HEAD_DIM)
        for distance in range(self.half_count):
            rows = block_rows(self.inside ^ distance, self.tokens)
            cross_ref = self.cross_refs[distance]
            first_all[rows, :HEAD_DIM] = cross_ref[: self.tokens, columns]
            second_all[rows, :] = cross_ref[self.tokens : 2 * self.tokens, columns]


def tile_scores(query_tile, pieces):
    results = []
    for key_all, _, limit, first in pieces:
        scores = contract_last(query_tile, key_all[:limit, :])
        if first is not None:
            column_index = lax.broadcasted_iota(jnp.int32, scores.shape, 1)
            row_index = lax.broadcasted_iota(jnp.int32, scores.shape, 0) + first
            scores = jnp.where(column_index <= row_index, scores, NEG_FILL)
        results.append(scores)
    return results


def tile_stats(scores, prob_grads):
    row_max = functools.reduce(
        jnp.maximum, [jnp.max(part, axis=1, keepdims=True) for part in scores]
    )
    weights = [jnp.exp2((part - row_max) * EXPONENT_SCALE) for part in scores]
    row_total = sum(jnp.sum(part, axis=1, keepdims=True) for part in weights)
    row_delta = sum(
        jnp.sum(part * grad, axis=1, keepdims=True) for part, grad in zip(weights, prob_grads)
    )
    return weights, row_max, row_total, row_delta


def tile_backward(query_tile, grad_tile, pieces, sums, stats, is_first):
    scores = tile_scores(query_tile, pieces)
    prob_grads = [contract_last(grad_tile, piece[1][: piece[2], :]) for piece in pieces]
    if stats is None:
        weights, _, row_total, row_delta = tile_stats(scores, prob_grads)
        inverse = 1.0 / jnp.maximum(row_total, 1.0)
        row_delta = row_delta * inverse
    else:
        row_max, inverse, row_delta = stats
        weights = [jnp.exp2((part - row_max) * EXPONENT_SCALE) for part in scores]
    attended, query_grad = 0.0, 0.0
    for index, (key_all, value_all, limit, first) in enumerate(pieces):
        probabilities = weights[index] * inverse
        prob_half = probabilities.astype(jnp.bfloat16)
        score_grad = (probabilities * (prob_grads[index] - row_delta)).astype(jnp.bfloat16)
        attended += jnp.dot(prob_half, value_all[:limit, :], preferred_element_type=jnp.float32)
        query_grad += jnp.dot(
            score_grad, key_all[:limit, :HEAD_DIM], preferred_element_type=jnp.float32
        )
        key_part = contract_first(score_grad, query_tile[:, :HEAD_DIM])
        value_part = contract_first(prob_half, grad_tile)
        key_sum, value_sum = sums[index]
        fresh = 0 if is_first else (limit if first is None else first)
        if fresh:
            key_sum[:fresh, :] += key_part[:fresh]
            value_sum[:fresh, :] += value_part[:fresh]
        if fresh < limit:
            key_sum[fresh:limit, :] = key_part[fresh:]
            value_sum[fresh:limit, :] = value_part[fresh:]
    return attended.astype(jnp.bfloat16), (query_grad * SCORE_SCALE).astype(jnp.bfloat16)


def own_tiles(half_len):
    tile = QUERY_TILE if half_len % QUERY_TILE == 0 else BLK
    return [(first, slice(first, first + tile), first + tile) for first in range(0, half_len, tile)]


def note_stats(out_ref, stat_rows, head, first, found):
    for place, column in enumerate(found[1:]):
        store_as_rows(out_ref, (3 * head + place) * stat_rows + first // LANES, column)


def stats_kernel(shape, stat_rows, me_ref, pattern_ref, packed_ref, *refs):
    half_count = shape[1]
    cross_refs, key_refs = refs[:half_count], refs[half_count : 2 * half_count]
    out_ref, query_all, key_all, value_all, grad_all, ids, other_ids = refs[2 * half_count :]
    slots = Slots(shape, me_ref, pattern_ref, packed_ref, key_refs, cross_refs)
    single = packed_ref.shape[1] // 2
    out_ref[...] = jnp.zeros_like(out_ref)
    slots.own_ids(ids)
    slots.key_features(ids, key_all, slots.is_high.astype(jnp.int32))

    @pl.when(slots.is_high)
    def _():
        slots.query_features(ids, query_all, 1)

    @pl.when(jnp.logical_not(slots.is_high))
    def _():
        slots.cross_ids(other_ids)
        slots.query_features(other_ids, query_all, 1)

    for head in range(single // HEAD_DIM):
        column = head * HEAD_DIM
        slots.own(single + column, query_all, key_all, value_all, grad_all)

        def note(first, rows, limit, causal_from):
            pieces = [(key_all, value_all, limit, causal_from)]
            scores = tile_scores(query_all[rows, :], pieces)
            prob_grad = contract_last(grad_all[rows, :], value_all[:limit, :])
            for place, found in enumerate(tile_stats(scores, [prob_grad])[1:]):
                store_as_rows(out_ref, (3 * head + place) * stat_rows + first // LANES, found)

        @pl.when(slots.is_high)
        def _():
            for first, rows, limit in own_tiles(slots.half_len):
                note(first, rows, limit, first)

        @pl.when(jnp.logical_not(slots.is_high))
        def _():
            slots.cross(column, query_all, grad_all)
            for first, rows, _ in own_tiles(slots.half_len):
                note(first, rows, slots.half_len, None)


def store_own(slots, result_refs, column, attended, query_grad, value_sum, key_sum):
    tokens = slots.tokens
    columns = slice(column, column + HEAD_DIM)
    for distance, target in enumerate(result_refs):
        rows = block_rows(slots.inside ^ distance, tokens)
        target[:tokens, columns] = attended[rows, :]
        target[tokens : 2 * tokens, columns] = query_grad[rows, :]
        target[2 * tokens : 3 * tokens, columns] = value_sum[rows, :].astype(jnp.bfloat16)
        target[3 * tokens :, columns] = (key_sum[rows, :] * SCORE_SCALE).astype(jnp.bfloat16)


def first_kernel(shape, me_ref, pattern_ref, packed_ref, *refs):
    half_count = shape[1]
    cross_refs, key_refs = refs[:half_count], refs[half_count : 2 * half_count]
    refs = refs[2 * half_count + 1 :]
    result_refs, cross_out_refs = refs[:half_count], refs[half_count : 2 * half_count]
    second_ref, sums_ref = refs[2 * half_count : 2 * half_count + 2]
    (query_all, key_all, value_all, grad_all, other_key, other_value, ids, other_ids, attended,
     query_grad, key_sum, value_sum, other_key_sum, other_value_sum) = refs[2 * half_count + 2 :]
    slots = Slots(shape, me_ref, pattern_ref, packed_ref, key_refs, cross_refs)
    single = packed_ref.shape[1] // 2
    half_len = slots.half_len
    high = slots.is_high.astype(jnp.int32)
    slots.own_ids(ids)
    slots.key_features(ids, key_all, high)
    slots.query_features(ids, query_all, high)

    def run(others, other_sums, attended_out, query_grad_out, key_out, value_out):
        for first, rows, limit in own_tiles(half_len):
            attended_out[rows, :], query_grad_out[rows, :] = tile_backward(
                query_all[rows, :],
                grad_all[rows, :],
                others + [(key_all, value_all, limit, first)],
                other_sums + [(key_out, value_out)],
                None,
                first == 0,
            )

    @pl.when(slots.is_high)
    def _():
        slots.cross_ids(other_ids)
        slots.key_features(other_ids, other_key, 0)

    for head in range(single // HEAD_DIM):
        column = head * HEAD_DIM
        columns = slice(column, column + HEAD_DIM)
        slots.own(column, query_all, key_all, value_all, grad_all)

        @pl.when(slots.is_high)
        def _():
            slots.cross(column, other_key, other_value)
            run(
                [(other_key, other_value, half_len, None)],
                [(other_key_sum, other_value_sum)],
                attended, query_grad, key_sum, value_sum,
            )
            for distance in range(half_count):
                rows = block_rows(slots.inside ^ distance, slots.tokens)
                target = cross_out_refs[distance]
                target[: slots.tokens, columns] = (other_key_sum[rows, :] * SCORE_SCALE).astype(
                    jnp.bfloat16
                )
                target[slots.tokens :, columns] = other_value_sum[rows, :].astype(jnp.bfloat16)

        @pl.when(jnp.logical_not(slots.is_high))
        def _():
            run([], [], attended, query_grad, key_sum, value_sum)

        store_own(slots, result_refs, column, attended, query_grad, value_sum, key_sum)

        @pl.when(jnp.logical_not(slots.is_high))
        def _():
            slots.own(single + column, query_all, key_all, value_all, grad_all)
            run(
                [], [],
                second_ref.at[:half_len, columns],
                second_ref.at[half_len:, columns],
                sums_ref.at[:half_len, columns],
                sums_ref.at[half_len:, columns],
            )


def joint_rows(stat_rows, head, own_stats_ref, far_stats_ref):
    (own_max, own_total, own_delta), (far_max, far_total, far_delta) = [
        [
            ref[(3 * head + place) * stat_rows : (3 * head + place + 1) * stat_rows, :]
            for place in range(3)
        ]
        for ref in (own_stats_ref, far_stats_ref)
    ]
    row_max = jnp.maximum(own_max, far_max)
    own_part = jnp.exp2((own_max - row_max) * EXPONENT_SCALE)
    far_part = jnp.exp2((far_max - row_max) * EXPONENT_SCALE)
    inverse = 1.0 / jnp.maximum(own_total * own_part + far_total * far_part, 1.0)
    return row_max, inverse, (own_delta * own_part + far_delta * far_part) * inverse


def second_head_kernel(shape, stat_rows, me_ref, pattern_ref, packed_ref, *refs):
    half_count = shape[1]
    cross_refs, key_refs = refs[:half_count], refs[half_count : 2 * half_count]
    own_stats_ref, far_stats_ref, early_ref, sums_ref = refs[2 * half_count : 2 * half_count + 4]
    refs = refs[2 * half_count + 4 :]
    first_cross_refs, result_refs, cross_out_refs = [
        refs[place * half_count : (place + 1) * half_count] for place in range(3)
    ]
    (query_all, key_all, value_all, grad_all, other_query, other_grad, ids, other_ids, attended,
     query_grad, key_sum, value_sum, other_attended, other_query_grad) = refs[3 * half_count :]
    slots = Slots(shape, me_ref, pattern_ref, packed_ref, key_refs, cross_refs)
    single = packed_ref.shape[1] // 2
    half_len, tokens = slots.half_len, slots.tokens
    slots.own_ids(ids)
    slots.key_features(ids, key_all, slots.is_high.astype(jnp.int32))

    @pl.when(slots.is_high)
    def _():
        slots.query_features(ids, query_all, 1)
        for distance in range(half_count):
            cross_out_refs[distance][...] = first_cross_refs[distance][...]

    @pl.when(jnp.logical_not(slots.is_high))
    def _():
        slots.cross_ids(other_ids)
        slots.query_features(other_ids, other_query, 1)

    for head in range(single // HEAD_DIM):
        column = head * HEAD_DIM
        columns = slice(column, column + HEAD_DIM)
        slots.own(single + column, query_all, key_all, value_all, grad_all)
        joint_table = joint_rows(stat_rows, head, own_stats_ref, far_stats_ref)

        def joint_stats(first, size):
            return [column_of(rows, first // LANES, size) for rows in joint_table]

        @pl.when(slots.is_high)
        def _():
            for first, rows, limit in own_tiles(half_len):
                attended[rows, :], query_grad[rows, :] = tile_backward(
                    query_all[rows, :],
                    grad_all[rows, :],
                    [(key_all, value_all, limit, first)],
                    [(key_sum, value_sum)],
                    joint_stats(first, limit - first),
                    first == 0,
                )

        @pl.when(jnp.logical_not(slots.is_high))
        def _():
            slots.cross(column, other_query, other_grad)
            attended[...] = early_ref[:half_len, columns]
            query_grad[...] = early_ref[half_len:, columns]
            key_sum[...] = sums_ref[:half_len, columns]
            value_sum[...] = sums_ref[half_len:, columns]
            for first, rows, limit in own_tiles(half_len):
                other_attended[rows, :], other_query_grad[rows, :] = tile_backward(
                    other_query[rows, :],
                    other_grad[rows, :],
                    [(key_all, value_all, half_len, None)],
                    [(key_sum, value_sum)],
                    joint_stats(first, limit - first),
                    False,
                )
            for distance in range(half_count):
                rows = block_rows(slots.inside ^ distance, tokens)
                target = cross_out_refs[distance]
                target[:tokens, columns] = other_attended[rows, :]
                target[tokens:, columns] = other_query_grad[rows, :]

        store_own(slots, result_refs, column, attended, query_grad, value_sum, key_sum)


def normed_grad_of(half_count, me_ref, first_ref, second_ref, cross_ref):
    tokens = second_ref.shape[0] // 4
    is_low = me_ref[0] < half_count
    far = jnp.where(is_low, cross_ref[:tokens, :].astype(jnp.float32), 0.0)
    first_float = first_ref[3 * tokens :, :].astype(jnp.float32) + far
    second_float = second_ref[3 * tokens :, :].astype(jnp.float32)
    return jnp.concatenate([first_float, second_float], axis=1)


def inner_kernel(half_count, me_ref, key_ref, rms_ref, *refs):
    cross_refs, first_refs, second_refs = [
        refs[place * half_count : (place + 1) * half_count] for place in range(3)
    ]
    out_ref = refs[3 * half_count]
    tokens, features = key_ref.shape
    width = features // half_count
    inside = me_ref[0] & (half_count - 1)
    total = jnp.zeros((tokens, width), jnp.float32)
    for distance in range(half_count):
        owner = inside ^ distance
        start = pl.multiple_of(owner * width, LANES)
        key_float = key_ref[:, pl.ds(start, width)].astype(jnp.float32)
        total = total + key_float * normed_grad_of(
            half_count, me_ref, first_refs[distance], second_refs[distance], cross_refs[distance]
        )
    column = jnp.sum(total, axis=1, keepdims=True) / column_of(rms_ref[...], 0, tokens)
    out_ref[...] = jnp.zeros_like(out_ref)
    store_as_rows(out_ref, 0, column)


def final_kernel(half_count, feature_total, me_ref, key_ref, rms_ref, inner_ref, *refs):
    cross_refs, first_refs, second_refs = [
        refs[place * half_count : (place + 1) * half_count] for place in range(3)
    ]
    attended_ref, query_ref, key_out_ref, value_ref = refs[3 * half_count :]
    tokens, features = key_ref.shape
    width = features // half_count
    single = width // 2
    is_high = me_ref[0] >= half_count
    inside = me_ref[0] & (half_count - 1)
    rms = column_of(rms_ref[...], 0, tokens)
    inner = column_of(inner_ref[...], 0, tokens) / feature_total
    for distance in range(half_count):
        owner = inside ^ distance
        start = pl.multiple_of(owner * width, LANES)
        columns = pl.ds(start, width)
        normed_float = key_ref[:, columns].astype(jnp.float32) / rms
        grad_float = normed_grad_of(
            half_count, me_ref, first_refs[distance], second_refs[distance], cross_refs[distance]
        )
        key_out_ref[:, columns] = ((grad_float - normed_float * inner) / rms).astype(jnp.bfloat16)
        cross_ref = cross_refs[distance]
        second = pl.ds(pl.multiple_of(start + single, LANES), single)
        for place, target in enumerate((attended_ref, query_ref, value_ref)):
            rows = slice(place * tokens, (place + 1) * tokens)
            target[:, pl.ds(start, single)] = first_refs[distance][rows, :]
            target[:, second] = second_refs[distance][rows, :]

        def add(target, columns, first):
            far = cross_ref[first : first + tokens, :].astype(jnp.float32)
            target[:, columns] = (target[:, columns].astype(jnp.float32) + far).astype(jnp.bfloat16)

        @pl.when(is_high)
        def _():
            add(attended_ref, second, 0)
            add(query_ref, second, tokens)

        @pl.when(jnp.logical_not(is_high))
        def _():
            add(value_ref, pl.ds(start, single), tokens)


def lane_rows(vector, row_count):
    return jnp.pad(vector, (0, row_count * LANES - vector.shape[0])).reshape(row_count, LANES)


def half_array(rows, columns):
    return jax.ShapeDtypeStruct((rows, columns), jnp.bfloat16)


def call(kernel, out_shapes, scalars, arrays, scratch=(), in_hbm=0, out_hbm=False, flops=0):
    vmem, anywhere = pl.BlockSpec(memory_space=pltpu.VMEM), pl.BlockSpec(memory_space=pl.ANY)
    return pl.pallas_call(
        kernel,
        out_shape=out_shapes,
        in_specs=[pl.BlockSpec(memory_space=pltpu.SMEM)] * len(scalars)
        + [anywhere] * in_hbm
        + [vmem] * (len(arrays) - in_hbm),
        out_specs=jax.tree.map(lambda shape: anywhere if out_hbm else vmem, out_shapes),
        scratch_shapes=list(scratch),
        compiler_params=pltpu.CompilerParams(vmem_limit_bytes=PACK_VMEM_BYTES if in_hbm else VMEM_BYTES),
        cost_estimate=pl.CostEstimate(flops=flops, bytes_accessed=0, transcendentals=0) if flops else None,
    )(*scalars, *arrays)


def swap(block, distance):
    count = lax.axis_size("seq")
    return lax.ppermute(block, "seq", [(i, i ^ distance) for i in range(count)])


def swap_inside(blocks):
    return [blocks[0]] + [swap(block, d) for d, block in enumerate(blocks) if d]


def swap_across(blocks):
    return [swap(block, len(blocks) + d) for d, block in enumerate(blocks)]


def exchange_inside(rows, half_count):
    count = 2 * half_count
    groups = [list(range(half_count)), list(range(half_count, count))]
    parts = rows.reshape(half_count, -1, rows.shape[1])
    return lax.all_to_all(
        parts, "seq", split_axis=0, concat_axis=0, tiled=True, axis_index_groups=groups
    ).reshape(rows.shape)


def sum_over_head(block):
    count = lax.axis_size("head")
    if count & (count - 1):
        return lax.psum(block, "head")
    return block + sum(
        lax.ppermute(block, "head", [(i, i ^ d) for i in range(count)]) for d in range(1, count)
    )


def by_halves(queries, key_vectors, values, cotangent, cluster, block_pattern):
    count = lax.axis_size("seq")
    half_count = count // 2
    tokens, features = queries.shape
    width = features // half_count
    single = width // 2
    cluster_count, block_count, _ = block_pattern.shape
    half_len = half_count * tokens
    shape = (tokens, half_count, cluster_count, block_count)
    row_count = -(-tokens // (8 * LANES)) * 8
    stat_rows = -(-half_len // (8 * LANES)) * 8
    me = lax.axis_index("seq").astype(jnp.int32).reshape(1)
    packed_shape = half_array(half_count * 3 * tokens, width)
    packed = call(
        functools.partial(pack_kernel, half_count),
        packed_shape,
        [],
        [queries, values, cotangent],
        [
            pltpu.VMEM((3, tokens, features), jnp.bfloat16),
            pltpu.VMEM(packed_shape.shape, jnp.bfloat16),
            pltpu.SemaphoreType.DMA((3,)),
            pltpu.SemaphoreType.DMA((3 * half_count,)),
        ],
        in_hbm=3,
        out_hbm=True,
    )
    packed, key_vectors, cluster = lax.optimization_barrier((packed, key_vectors, cluster))
    packed = exchange_inside(packed, half_count)
    ids = lane_rows(cluster[:, 0], ID_ROWS).astype(jnp.bfloat16)
    key_float = key_vectors.astype(jnp.float32)
    square_sum = sum_over_head(lane_rows(jnp.sum(key_float * key_float, axis=1), row_count))
    feature_total = HEADS * HEAD_DIM
    key_rms = jnp.sqrt(square_sum / feature_total + EPSILON)
    sent = call(
        functools.partial(pack_keys_kernel, half_count),
        [half_array(tokens + ID_ROWS, width)] * half_count
        + [half_array(2 * tokens + ID_ROWS, single)] * half_count,
        [me],
        [queries, values, cotangent, key_vectors, key_rms, ids],
    )
    keys = swap_inside(sent[:half_count])
    cross_sent = list(sent[half_count:])
    for distance in range(half_count // 2, half_count):
        cross_sent[distance], keys[1] = lax.optimization_barrier((cross_sent[distance], keys[1]))
    cross = swap_across(cross_sent)
    pattern_rows = block_pattern.transpose(1, 0, 2).reshape(block_count, -1).astype(jnp.float32)
    pattern_rows = jnp.pad(pattern_rows, ((0, 0), (0, LANES - cluster_count * block_count)))
    wide = pltpu.VMEM((half_len, 2 * HEAD_DIM), jnp.bfloat16)
    slim = pltpu.VMEM((half_len, HEAD_DIM), jnp.bfloat16)
    sums = pltpu.VMEM((half_len, HEAD_DIM), jnp.float32)
    ids_column = pltpu.VMEM((half_len, 1), jnp.float32)
    block_flops = 12 * half_len * half_len * single
    inputs = [pattern_rows, packed] + cross + keys
    stats = call(
        functools.partial(stats_kernel, shape, stat_rows),
        jax.ShapeDtypeStruct((3 * stat_rows * (single // HEAD_DIM), LANES), jnp.float32),
        [me],
        inputs,
        [wide, wide, slim, slim, ids_column, ids_column],
        flops=block_flops // 3,
    )
    far_stats = swap(stats, half_count)
    firsts = call(
        functools.partial(first_kernel, shape),
        [half_array(4 * tokens, single)] * half_count
        + [half_array(2 * tokens, single)] * half_count
        + [
            half_array(2 * half_len, single),
            jax.ShapeDtypeStruct((2 * half_len, single), jnp.float32),
        ],
        [me],
        inputs + [stats],
        [wide, wide, slim, slim, wide, slim, ids_column, ids_column, slim, slim]
        + [sums, sums, sums, sums],
        flops=block_flops + block_flops // 2,
    )
    *firsts, far_stats = lax.optimization_barrier((*firsts, far_stats))
    rest = firsts[half_count:]
    firsts = swap_inside(firsts[:half_count])
    results = call(
        functools.partial(second_head_kernel, shape, stat_rows),
        [half_array(4 * tokens, single)] * half_count
        + [half_array(2 * tokens, single)] * half_count,
        [me],
        inputs + [stats, far_stats] + rest[half_count:] + rest[:half_count],
        [wide, wide, slim, slim, wide, slim, ids_column, ids_column, slim, slim]
        + [sums, sums, slim, slim],
        flops=block_flops,
    )
    far_sent = list(results[half_count:])
    far_sent, firsts = lax.optimization_barrier((far_sent, firsts))
    far_parts = swap_across(far_sent)
    seconds = swap_inside(results[:half_count])
    inner = call(
        functools.partial(inner_kernel, half_count),
        jax.ShapeDtypeStruct((row_count, LANES), jnp.float32),
        [me],
        [key_vectors, key_rms] + far_parts + firsts + seconds,
    )
    inner = sum_over_head(inner)
    return tuple(
        call(
            functools.partial(final_kernel, half_count, feature_total),
            [half_array(tokens, features)] * 4,
            [me],
            [key_vectors, key_rms, inner] + far_parts + firsts + seconds,
        )
    )


def per_device_any(queries, key_vectors, values, cotangent, cluster, block_pattern):
    count = lax.axis_size("seq")
    tokens, features = queries.shape
    cluster_count, block_count, _ = block_pattern.shape
    fits = (
        count % 2 == 0
        and count & (count - 1) == 0
        and features % (count * HEAD_DIM) == 0
        and tokens % ID_ROWS == 0
        and tokens * count % (2 * BLK) == 0
        and cluster_count * block_count <= LANES
    )
    chosen = by_halves if fits else per_device
    return chosen(queries, key_vectors, values, cotangent, cluster, block_pattern)


def solution(mesh):
    in_specs = (
        P("seq", "head"),
        P("seq", "head"),
        P("seq", "head"),
        P("seq", "head"),
        P("seq", None),
        P(),
    )
    out_specs = (P("seq", "head"), P("seq", "head"), P("seq", "head"), P("seq", "head"))
    return jax.shard_map(
        per_device_any, mesh=mesh, in_specs=in_specs, out_specs=out_specs, check_vma=False
    )
```

```python
import functools

import jax
import jax.numpy as jnp
from jax import lax
from jax.experimental import pallas as pl
from jax.experimental.pallas import tpu as pltpu
from jax.sharding import PartitionSpec as P

HEADS = 32
HEAD_DIM = 128
GS = 4
BLK = 128


NEG_FILL = -1e30
EPSILON = 1e-05
SCORE_SCALE = HEAD_DIM ** (-0.5)
EXPONENT_SCALE = SCORE_SCALE * 1.4426950408889634
LANES = 128
ID_ROWS = 16
QUERY_TILE = 256
VMEM_BYTES = 32 << 20
PACK_VMEM_BYTES = 60 << 20


def contract_last(left_side, right_side):
    return lax.dot_general(
        left_side, right_side, (((1,), (1,)), ((), ())), preferred_element_type=jnp.float32
    )


def contract_first(left_side, right_side):
    return lax.dot_general(
        left_side, right_side, (((0,), (0,)), ((), ())), preferred_element_type=jnp.float32
    )


def visible_mask(pattern, query_pos, query_live, key_pos, key_live):
    pattern_rows = pattern[query_pos // BLK]
    allowed = jnp.take(pattern_rows, key_pos // BLK, axis=1) == 1
    causal = key_pos[None, :] <= query_pos[:, None]
    return allowed & causal & query_live[:, None] & key_live[None, :]


def cluster_ranks(table, cluster_index):
    source_count, tok_count = table.shape
    in_cluster = table == cluster_index
    token_iota = jnp.arange(tok_count, dtype=jnp.int32)
    earlier_table = (token_iota[:, None] < token_iota[None, :]).astype(jnp.bfloat16)
    earlier = jnp.dot(
        in_cluster.astype(jnp.bfloat16), earlier_table, preferred_element_type=jnp.float32
    ).astype(jnp.int32)
    global_pos = (
        jnp.arange(source_count, dtype=jnp.int32)[:, None] * tok_count + token_iota[None, :]
    )
    return (in_cluster, earlier, global_pos)


def code_positions(slot_code, global_pos, capacity):
    matches = slot_code[:, :, None] == jnp.arange(capacity, dtype=jnp.int32)[None, None, :]
    positions = jnp.sum(jnp.where(matches, global_pos[:, :, None], 0), axis=1)
    occupied = jnp.any(matches, axis=1)
    return (positions, occupied)


def rank_positions(table, cluster_index, capacity):
    in_cluster, earlier, global_pos = cluster_ranks(table, cluster_index)
    rank_code = jnp.where(in_cluster, earlier, -1)
    positions, occupied = code_positions(rank_code, global_pos, capacity)
    return (positions.reshape(-1), occupied.reshape(-1))


def dispatch_rows(outgoing):
    return lax.all_to_all(outgoing, "seq", split_axis=1, concat_axis=1, tiled=True)


def combine_rows(outgoing):
    return lax.all_to_all(outgoing, "seq", split_axis=1, concat_axis=1, tiled=True)


def forward_heads(query_slots, key_slots, value_slots, grad_slots, visible, score_scale):
    query_count, features = query_slots.shape
    key_count = key_slots.shape[0]
    head_count = features // HEAD_DIM
    attended = jnp.zeros((query_count, features), jnp.bfloat16)
    query_grad = jnp.zeros((query_count, features), jnp.bfloat16)
    side_result = jnp.zeros((2, key_count, features), jnp.float32)

    def one_head(head_index, running):
        attended_acc, query_acc, side_acc = running
        column_start = head_index * HEAD_DIM
        query_rows = lax.dynamic_slice_in_dim(query_slots, column_start, HEAD_DIM, 1)
        key_rows = lax.dynamic_slice_in_dim(key_slots, column_start, HEAD_DIM, 1)
        value_rows = lax.dynamic_slice_in_dim(value_slots, column_start, HEAD_DIM, 1)
        grad_rows = lax.dynamic_slice_in_dim(grad_slots, column_start, HEAD_DIM, 1)
        scores = jnp.where(visible, contract_last(query_rows, key_rows) * score_scale, NEG_FILL)
        row_max = jnp.max(scores, axis=1, keepdims=True)
        weights = jnp.where(visible, jnp.exp(scores - row_max), 0.0)
        row_total = jnp.maximum(jnp.sum(weights, axis=1, keepdims=True), 1.0)
        probabilities = weights / row_total
        prob_half = probabilities.astype(jnp.bfloat16)
        attended_head = jnp.dot(prob_half, value_rows, preferred_element_type=jnp.float32).astype(
            jnp.bfloat16
        )
        prob_grad = contract_last(grad_rows, value_rows)
        row_delta = jnp.sum(probabilities * prob_grad, axis=1, keepdims=True)
        score_grad = (probabilities * (prob_grad - row_delta)).astype(jnp.bfloat16)
        query_head = (
            jnp.dot(score_grad, key_rows, preferred_element_type=jnp.float32) * score_scale
        ).astype(jnp.bfloat16)
        attended_acc = lax.dynamic_update_slice_in_dim(attended_acc, attended_head, column_start, 1)
        query_acc = lax.dynamic_update_slice_in_dim(query_acc, query_head, column_start, 1)
        key_part = contract_first(score_grad, query_rows)
        value_part = contract_first(prob_half, grad_rows)
        side_acc = lax.dynamic_update_slice_in_dim(
            side_acc, jnp.stack([key_part, value_part]), column_start, 2
        )
        return (attended_acc, query_acc, side_acc)

    return lax.fori_loop(0, head_count, one_head, (attended, query_grad, side_result))


def per_device(queries, key_vectors, values, cotangent, cluster, block_pattern):
    seq_count = lax.axis_size("seq")
    tok_count, features = queries.shape
    slot_count = 2 * tok_count // seq_count
    group_count = seq_count // GS
    score_scale = HEAD_DIM ** (-0.5)
    my_index = lax.axis_index("seq")
    group_index = my_index // GS
    key_float = key_vectors.astype(jnp.float32)
    square_sum = lax.psum(jnp.sum(key_float * key_float, axis=1), "head")
    key_rms = jnp.sqrt(square_sum / (HEADS * HEAD_DIM) + EPSILON)[:, None]
    normed_float = key_float / key_rms
    normed = normed_float.astype(jnp.bfloat16)
    own_ids = cluster[:, 0]
    everyone = lax.all_gather(own_ids, "seq", axis=0, tiled=True)
    table = everyone.reshape(seq_count, tok_count)
    token_iota = jnp.arange(tok_count, dtype=jnp.int32)
    onehot_own = (own_ids[:, None] == jnp.arange(group_count, dtype=jnp.int32)[None, :]).astype(
        jnp.bfloat16
    )
    before_table = (token_iota[:, None] > token_iota[None, :]).astype(jnp.bfloat16)
    before = jnp.dot(before_table, onehot_own, preferred_element_type=jnp.float32)
    own_rank = jnp.sum(before * onehot_own.astype(jnp.float32), axis=1).astype(jnp.int32)
    pattern = lax.dynamic_index_in_dim(block_pattern, group_index, 0, keepdims=False)
    stacked_inputs = jnp.stack([queries, normed, values, cotangent])
    quarter = features // GS
    capacity = GS * slot_count
    split_inputs = stacked_inputs.reshape(4, tok_count, GS, quarter)
    placed = (
        jnp.zeros((4, group_count, capacity, GS, quarter), jnp.bfloat16)
        .at[:, own_ids, own_rank]
        .set(split_inputs)
    )
    outgoing = placed.transpose(0, 1, 3, 2, 4).reshape(4, seq_count * capacity, quarter)
    arrived = dispatch_rows(outgoing)
    flat_positions, flat_present = rank_positions(table, group_index, capacity)
    visible = visible_mask(pattern, flat_positions, flat_present, flat_positions, flat_present)
    attended, query_grad, both_terms = forward_heads(
        arrived[0], arrived[1], arrived[2], arrived[3], visible, score_scale
    )
    normed_grad = (both_terms[0] * score_scale).astype(jnp.bfloat16)
    value_slots = both_terms[1].astype(jnp.bfloat16)
    outgoing_back = jnp.stack([attended, query_grad, normed_grad, value_slots])
    returned = combine_rows(outgoing_back)
    arranged = returned.reshape(4, group_count, GS, capacity, quarter).transpose(1, 3, 0, 2, 4)
    home_rows = arranged[own_ids, own_rank].transpose(1, 0, 2, 3).reshape(4, tok_count, features)
    grad_float = home_rows[2].astype(jnp.float32)
    inner = lax.psum(jnp.sum(normed_float * grad_float, axis=1), "head")
    key_grad = (
        (grad_float - normed_float * (inner / (HEADS * HEAD_DIM))[:, None]) / key_rms
    ).astype(jnp.bfloat16)
    return (home_rows[0], home_rows[1], key_grad, home_rows[3])


def column_of(rows, first_row, count):
    turned = jnp.transpose(rows)
    pieces = []
    for start in range(0, count, LANES):
        place = first_row + start // LANES
        pieces.append(turned[: min(LANES, count - start), place : place + 1])
    return jnp.concatenate(pieces, axis=0)


def ids_of(ref, first_row, count):
    rows = ref[first_row : first_row + ID_ROWS, :LANES].astype(jnp.float32)
    return column_of(rows, 0, count)


def store_as_rows(out_ref, first_row, column):
    count = column.shape[0]
    for start in range(0, count, LANES):
        size = min(LANES, count - start)
        diagonal = lax.broadcasted_iota(jnp.int32, (size, LANES), 0) == lax.broadcasted_iota(
            jnp.int32, (size, LANES), 1
        )
        spread = jnp.where(diagonal, column[start : start + size], 0.0)
        row = first_row + start // LANES
        out_ref[row : row + 1, :] = jnp.sum(spread, axis=0, keepdims=True)


def block_rows(index, size):
    return pl.ds(pl.multiple_of(index * size, 16), size)


def pack_kernel(half_count, query_ref, value_ref, grad_ref, out_ref, held, sorted_rows, in_sems, out_sems):
    tokens, features = query_ref.shape
    width = features // half_count
    arrivals = [
        pltpu.make_async_copy(source_ref, held.at[place], in_sems.at[place])
        for place, source_ref in enumerate((query_ref, value_ref, grad_ref))
    ]
    for arrival in arrivals:
        arrival.start()
    copies = []
    for place, arrival in enumerate(arrivals):
        arrival.wait()
        for owner in range(half_count):
            rows = pl.ds((owner * 3 + place) * tokens, tokens)
            sorted_rows[rows, :] = held[place, :, owner * width : (owner + 1) * width]
            copy = pltpu.make_async_copy(
                sorted_rows.at[rows, :], out_ref.at[rows, :], out_sems.at[place * half_count + owner]
            )
            copy.start()
            copies.append(copy)
    for copy in copies:
        copy.wait()


def pack_keys_kernel(
    half_count, me_ref, query_ref, value_ref, grad_ref, key_ref, rms_ref, ids_ref, *out_refs
):
    tokens, features = key_ref.shape
    width = features // half_count
    single = width // 2
    is_high = me_ref[0] >= half_count
    inside = me_ref[0] & (half_count - 1)
    key_refs, cross_refs = out_refs[:half_count], out_refs[half_count:]
    rms = column_of(rms_ref[...], 0, tokens)

    def normed_columns(first, size):
        return (key_ref[:, pl.ds(first, size)].astype(jnp.float32) / rms).astype(jnp.bfloat16)

    for distance in range(half_count):
        first = pl.multiple_of((inside ^ distance) * width, LANES)
        cross_ref = cross_refs[distance]
        key_refs[distance][:tokens, :] = normed_columns(first, width)
        key_refs[distance][tokens:, :LANES] = ids_ref[...]
        key_refs[distance][tokens:, LANES:] = jnp.zeros((ID_ROWS, width - LANES), jnp.bfloat16)
        cross_ref[2 * tokens :, :LANES] = ids_ref[...]
        if single > LANES:
            cross_ref[2 * tokens :, LANES:] = jnp.zeros((ID_ROWS, single - LANES), jnp.bfloat16)

        @pl.when(is_high)
        def send_down():
            second = pl.multiple_of(first + single, LANES)
            cross_ref[:tokens, :] = query_ref[:, pl.ds(second, single)]
            cross_ref[tokens : 2 * tokens, :] = grad_ref[:, pl.ds(second, single)]

        @pl.when(jnp.logical_not(is_high))
        def send_up():
            cross_ref[:tokens, :] = normed_columns(first, single)
            cross_ref[tokens : 2 * tokens, :] = value_ref[:, pl.ds(first, single)]


class Slots:
    def __init__(self, shape, me_ref, pattern_ref, packed_ref, key_refs, cross_refs):
        self.tokens, self.half_count, self.cluster_count, self.block_count = shape
        self.half_len = self.tokens * self.half_count
        self.half_blocks = self.half_len // BLK
        self.is_high = me_ref[0] >= self.half_count
        self.inside = me_ref[0] & (self.half_count - 1)
        self.pattern_ref, self.packed_ref = pattern_ref, packed_ref
        self.key_refs, self.cross_refs = key_refs, cross_refs
        lane = lax.broadcasted_iota(jnp.int32, (1, LANES), 1)
        lane_cluster = jnp.zeros((1, LANES), jnp.int32)
        for index in range(1, self.cluster_count + 1):
            lane_cluster = lane_cluster + (lane >= index * self.block_count).astype(jnp.int32)
        self.lane_block = lane - lane_cluster * self.block_count
        self.lane_cluster = lane_cluster.astype(jnp.float32)

    def own_ids(self, ids_all):
        for distance in range(self.half_count):
            ids_all[block_rows(self.inside ^ distance, self.tokens), :] = ids_of(
                self.key_refs[distance], self.tokens, self.tokens
            )

    def cross_ids(self, ids_all):
        for distance in range(self.half_count):
            ids_all[block_rows(self.inside ^ distance, self.tokens), :] = ids_of(
                self.cross_refs[distance], 2 * self.tokens, self.tokens
            )

    def query_features(self, ids_all, target, high):
        for block in range(self.half_blocks):
            rows = slice(block * BLK, (block + 1) * BLK)
            place = block + high * self.half_blocks
            allowed = self.pattern_ref[pl.ds(place, 1), :] == 1.0
            same = ids_all[rows, :] == self.lane_cluster
            target[rows, HEAD_DIM:] = jnp.where(same & allowed, 0.0, NEG_FILL).astype(jnp.bfloat16)

    def key_features(self, ids_all, target, high):
        for block in range(self.half_blocks):
            rows = slice(block * BLK, (block + 1) * BLK)
            place = block + high * self.half_blocks
            same = ids_all[rows, :] == self.lane_cluster
            target[rows, HEAD_DIM:] = jnp.where(same & (self.lane_block == place), 1.0, 0.0).astype(
                jnp.bfloat16
            )

    def own(self, column, query_all, key_all, value_all, grad_all):
        columns = slice(column, column + HEAD_DIM)
        stride = 3 * self.tokens
        for source in range(self.half_count):
            rows = slice(source * self.tokens, (source + 1) * self.tokens)
            for place, target in enumerate((query_all, value_all, grad_all)):
                first = source * stride + place * self.tokens
                target[rows, :HEAD_DIM] = self.packed_ref[first : first + self.tokens, columns]
        for distance in range(self.half_count):
            rows = block_rows(self.inside ^ distance, self.tokens)
            key_all[rows, :HEAD_DIM] = self.key_refs[distance][: self.tokens, columns]

    def cross(self, column, first_all, second_all):
        columns = slice(column, column + HEAD_DIM)
        for distance in range(self.half_count):
            rows = block_rows(self.inside ^ distance, self.tokens)
            cross_ref = self.cross_refs[distance]
            first_all[rows, :HEAD_DIM] = cross_ref[: self.tokens, columns]
            second_all[rows, :] = cross_ref[self.tokens : 2 * self.tokens, columns]


class Keys:
    def __init__(self, key, value, key_turned=None, value_turned=None):
        self.key, self.value = key, value
        self.key_turned, self.value_turned = key_turned, value_turned

    def turn(self):
        self.key_turned[...] = jnp.transpose(self.key[:, :HEAD_DIM])
        self.value_turned[...] = jnp.transpose(self.value[...])


def tile_scores(query_tile, keys, limit, first):
    scores = contract_last(keys.key[:limit, :], query_tile)
    if first is not None:
        key_index = lax.broadcasted_iota(jnp.int32, scores.shape, 0)
        query_index = lax.broadcasted_iota(jnp.int32, scores.shape, 1) + first
        scores = jnp.where(key_index <= query_index, scores, NEG_FILL)
    return scores


def tile_stats(scores, prob_grads):
    row_max = functools.reduce(
        jnp.maximum, [jnp.max(part, axis=0, keepdims=True) for part in scores]
    )
    weights = [jnp.exp2((part - row_max) * EXPONENT_SCALE) for part in scores]
    row_total = sum(jnp.sum(part, axis=0, keepdims=True) for part in weights)
    row_delta = sum(
        jnp.sum(part * grad, axis=0, keepdims=True) for part, grad in zip(weights, prob_grads)
    )
    return weights, row_max, row_total, row_delta


def tile_products(query_tile, grad_tile, pieces):
    scores = [tile_scores(query_tile, *piece) for piece in pieces]
    return scores, [contract_last(keys.value[:limit, :], grad_tile) for keys, limit, _ in pieces]


def all_tiles(query_all, grad_all, half_len, pieces_of, sums, stats_of, keep, add=False):
    tiles = own_tiles(half_len)
    ready = None
    for index, (first, rows, limit) in enumerate(tiles):
        now = ready or tile_products(query_all[rows, :], grad_all[rows, :], pieces_of(first, limit))
        ready = None
        if index + 1 < len(tiles):
            later, later_rows, later_limit = tiles[index + 1]
            ready = tile_products(
                query_all[later_rows, :], grad_all[later_rows, :], pieces_of(later, later_limit)
            )
        keep(
            rows,
            *tile_backward(
                query_all[rows, :],
                grad_all[rows, :],
                pieces_of(first, limit),
                sums,
                stats_of(first, limit - first) if stats_of else None,
                first == 0 and not add,
                *now,
            ),
        )


def tile_backward(query_tile, grad_tile, pieces, sums, stats, is_first, scores, prob_grads):
    if stats is None:
        weights, _, row_total, row_delta = tile_stats(scores, prob_grads)
        inverse = 1.0 / jnp.maximum(row_total, 1.0)
        row_delta = row_delta * inverse
    else:
        row_max, inverse, row_delta = stats
        weights = [jnp.exp2((part - row_max) * EXPONENT_SCALE) for part in scores]
    attended, query_grad = 0.0, 0.0
    for index, (keys, limit, first) in enumerate(pieces):
        probabilities = weights[index] * inverse
        prob_half = probabilities.astype(jnp.bfloat16)
        score_grad = (probabilities * (prob_grads[index] - row_delta)).astype(jnp.bfloat16)
        attended += jnp.dot(
            keys.value_turned[:, :limit], prob_half, preferred_element_type=jnp.float32
        )
        query_grad += jnp.dot(
            keys.key_turned[:, :limit], score_grad, preferred_element_type=jnp.float32
        )
        key_part = jnp.dot(
            score_grad, query_tile[:, :HEAD_DIM], preferred_element_type=jnp.float32
        )
        value_part = jnp.dot(prob_half, grad_tile, preferred_element_type=jnp.float32)
        key_sum, value_sum = sums[index]
        fresh = 0 if is_first else (limit if first is None else first)
        if fresh:
            key_sum[:fresh, :] += key_part[:fresh]
            value_sum[:fresh, :] += value_part[:fresh]
        if fresh < limit:
            key_sum[fresh:limit, :] = key_part[fresh:]
            value_sum[fresh:limit, :] = value_part[fresh:]
    return (
        jnp.transpose(attended).astype(jnp.bfloat16),
        jnp.transpose(query_grad * SCORE_SCALE).astype(jnp.bfloat16),
    )


def own_tiles(half_len):
    tile = QUERY_TILE if half_len % QUERY_TILE == 0 else BLK
    return [(first, slice(first, first + tile), first + tile) for first in range(0, half_len, tile)]


def note_stats(out_ref, stat_rows, head, first, found):
    for place, column in enumerate(found[1:]):
        store_as_rows(out_ref, (3 * head + place) * stat_rows + first // LANES, column)


def stats_kernel(shape, stat_rows, me_ref, pattern_ref, packed_ref, *refs):
    half_count = shape[1]
    cross_refs, key_refs = refs[:half_count], refs[half_count : 2 * half_count]
    out_ref, query_all, key_all, value_all, grad_all, ids, other_ids = refs[2 * half_count :]
    slots = Slots(shape, me_ref, pattern_ref, packed_ref, key_refs, cross_refs)
    single = packed_ref.shape[1] // 2
    out_ref[...] = jnp.zeros_like(out_ref)
    slots.own_ids(ids)
    slots.key_features(ids, key_all, slots.is_high.astype(jnp.int32))

    @pl.when(slots.is_high)
    def _():
        slots.query_features(ids, query_all, 1)

    @pl.when(jnp.logical_not(slots.is_high))
    def _():
        slots.cross_ids(other_ids)
        slots.query_features(other_ids, query_all, 1)

    for head in range(single // HEAD_DIM):
        column = head * HEAD_DIM
        slots.own(single + column, query_all, key_all, value_all, grad_all)

        def note(first, rows, limit, causal_from):
            scores = tile_scores(query_all[rows, :], Keys(key_all, value_all), limit, causal_from)
            prob_grad = contract_last(value_all[:limit, :], grad_all[rows, :])
            for place, found in enumerate(tile_stats([scores], [prob_grad])[1:]):
                row = (3 * head + place) * stat_rows + first // LANES
                for start in range(0, found.shape[1], LANES):
                    out_ref[row + start // LANES : row + start // LANES + 1, :] = found[
                        :, start : start + LANES
                    ]

        @pl.when(slots.is_high)
        def _():
            for first, rows, limit in own_tiles(slots.half_len):
                note(first, rows, limit, first)

        @pl.when(jnp.logical_not(slots.is_high))
        def _():
            slots.cross(column, query_all, grad_all)
            for first, rows, _ in own_tiles(slots.half_len):
                note(first, rows, slots.half_len, None)


def store_own(slots, result_refs, column, attended, query_grad, value_sum, key_sum):
    tokens = slots.tokens
    columns = slice(column, column + HEAD_DIM)
    for distance, target in enumerate(result_refs):
        rows = block_rows(slots.inside ^ distance, tokens)
        target[:tokens, columns] = attended[rows, :]
        target[tokens : 2 * tokens, columns] = query_grad[rows, :]
        target[2 * tokens : 3 * tokens, columns] = value_sum[rows, :].astype(jnp.bfloat16)
        target[3 * tokens :, columns] = (key_sum[rows, :] * SCORE_SCALE).astype(jnp.bfloat16)


def first_kernel(shape, me_ref, pattern_ref, packed_ref, *refs):
    half_count = shape[1]
    cross_refs, key_refs = refs[:half_count], refs[half_count : 2 * half_count]
    refs = refs[2 * half_count + 1 :]
    result_refs, cross_out_refs = refs[:half_count], refs[half_count : 2 * half_count]
    second_ref, sums_ref = refs[2 * half_count : 2 * half_count + 2]
    (query_all, key_all, value_all, grad_all, other_key, other_value, ids, other_ids, attended,
     query_grad, key_sum, value_sum, other_key_sum, other_value_sum, *turned) = refs[
        2 * half_count + 2 :
    ]
    own, other = Keys(key_all, value_all, *turned[:2]), Keys(other_key, other_value, *turned[2:])
    slots = Slots(shape, me_ref, pattern_ref, packed_ref, key_refs, cross_refs)
    single = packed_ref.shape[1] // 2
    half_len = slots.half_len
    high = slots.is_high.astype(jnp.int32)
    slots.own_ids(ids)
    slots.key_features(ids, key_all, high)
    slots.query_features(ids, query_all, high)

    def run(others, other_sums, attended_out, query_grad_out, key_out, value_out):
        def keep(rows, attended_tile, query_grad_tile):
            attended_out[rows, :], query_grad_out[rows, :] = attended_tile, query_grad_tile

        all_tiles(
            query_all,
            grad_all,
            half_len,
            lambda first, limit: others + [(own, limit, first)],
            other_sums + [(key_out, value_out)],
            None,
            keep,
        )

    @pl.when(slots.is_high)
    def _():
        slots.cross_ids(other_ids)
        slots.key_features(other_ids, other_key, 0)

    for head in range(single // HEAD_DIM):
        column = head * HEAD_DIM
        columns = slice(column, column + HEAD_DIM)
        slots.own(column, query_all, key_all, value_all, grad_all)
        own.turn()

        @pl.when(slots.is_high)
        def _():
            slots.cross(column, other_key, other_value)
            other.turn()
            run(
                [(other, half_len, None)],
                [(other_key_sum, other_value_sum)],
                attended, query_grad, key_sum, value_sum,
            )
            for distance in range(half_count):
                rows = block_rows(slots.inside ^ distance, slots.tokens)
                target = cross_out_refs[distance]
                target[: slots.tokens, columns] = (other_key_sum[rows, :] * SCORE_SCALE).astype(
                    jnp.bfloat16
                )
                target[slots.tokens :, columns] = other_value_sum[rows, :].astype(jnp.bfloat16)

        @pl.when(jnp.logical_not(slots.is_high))
        def _():
            run([], [], attended, query_grad, key_sum, value_sum)

        store_own(slots, result_refs, column, attended, query_grad, value_sum, key_sum)

        @pl.when(jnp.logical_not(slots.is_high))
        def _():
            slots.own(single + column, query_all, key_all, value_all, grad_all)
            own.turn()
            run(
                [], [],
                second_ref.at[:half_len, columns],
                second_ref.at[half_len:, columns],
                sums_ref.at[:half_len, columns],
                sums_ref.at[half_len:, columns],
            )


def joint_rows(stat_rows, head, own_stats_ref, far_stats_ref):
    (own_max, own_total, own_delta), (far_max, far_total, far_delta) = [
        [
            ref[(3 * head + place) * stat_rows : (3 * head + place + 1) * stat_rows, :]
            for place in range(3)
        ]
        for ref in (own_stats_ref, far_stats_ref)
    ]
    row_max = jnp.maximum(own_max, far_max)
    own_part = jnp.exp2((own_max - row_max) * EXPONENT_SCALE)
    far_part = jnp.exp2((far_max - row_max) * EXPONENT_SCALE)
    inverse = 1.0 / jnp.maximum(own_total * own_part + far_total * far_part, 1.0)
    return row_max, inverse, (own_delta * own_part + far_delta * far_part) * inverse


def second_head_kernel(shape, stat_rows, me_ref, pattern_ref, packed_ref, *refs):
    half_count = shape[1]
    cross_refs, key_refs = refs[:half_count], refs[half_count : 2 * half_count]
    own_stats_ref, far_stats_ref, early_ref, sums_ref = refs[2 * half_count : 2 * half_count + 4]
    refs = refs[2 * half_count + 4 :]
    first_cross_refs, result_refs, cross_out_refs = [
        refs[place * half_count : (place + 1) * half_count] for place in range(3)
    ]
    (query_all, key_all, value_all, grad_all, other_query, other_grad, ids, other_ids, attended,
     query_grad, key_sum, value_sum, other_attended, other_query_grad, *turned) = refs[
        3 * half_count :
    ]
    own = Keys(key_all, value_all, *turned)
    slots = Slots(shape, me_ref, pattern_ref, packed_ref, key_refs, cross_refs)
    single = packed_ref.shape[1] // 2
    half_len, tokens = slots.half_len, slots.tokens
    slots.own_ids(ids)
    slots.key_features(ids, key_all, slots.is_high.astype(jnp.int32))

    @pl.when(slots.is_high)
    def _():
        slots.query_features(ids, query_all, 1)
        for distance in range(half_count):
            cross_out_refs[distance][...] = first_cross_refs[distance][...]

    @pl.when(jnp.logical_not(slots.is_high))
    def _():
        slots.cross_ids(other_ids)
        slots.query_features(other_ids, other_query, 1)

    for head in range(single // HEAD_DIM):
        column = head * HEAD_DIM
        columns = slice(column, column + HEAD_DIM)
        slots.own(single + column, query_all, key_all, value_all, grad_all)
        own.turn()
        joint_table = joint_rows(stat_rows, head, own_stats_ref, far_stats_ref)

        def joint_stats(first, size):
            places = range(first // LANES, (first + size) // LANES)
            return [
                jnp.concatenate([rows[place : place + 1, :] for place in places], axis=1)
                for rows in joint_table
            ]

        @pl.when(slots.is_high)
        def _():
            def keep(rows, attended_tile, query_grad_tile):
                attended[rows, :], query_grad[rows, :] = attended_tile, query_grad_tile

            all_tiles(
                query_all,
                grad_all,
                half_len,
                lambda first, limit: [(own, limit, first)],
                [(key_sum, value_sum)],
                joint_stats,
                keep,
            )

        @pl.when(jnp.logical_not(slots.is_high))
        def _():
            slots.cross(column, other_query, other_grad)
            attended[...] = early_ref[:half_len, columns]
            query_grad[...] = early_ref[half_len:, columns]
            key_sum[...] = sums_ref[:half_len, columns]
            value_sum[...] = sums_ref[half_len:, columns]

            def keep(rows, attended_tile, query_grad_tile):
                other_attended[rows, :], other_query_grad[rows, :] = attended_tile, query_grad_tile

            all_tiles(
                other_query,
                other_grad,
                half_len,
                lambda first, limit: [(own, half_len, None)],
                [(key_sum, value_sum)],
                joint_stats,
                keep,
                add=True,
            )
            for distance in range(half_count):
                rows = block_rows(slots.inside ^ distance, tokens)
                target = cross_out_refs[distance]
                target[:tokens, columns] = other_attended[rows, :]
                target[tokens:, columns] = other_query_grad[rows, :]

        store_own(slots, result_refs, column, attended, query_grad, value_sum, key_sum)


def normed_grad_of(half_count, me_ref, first_ref, second_ref, cross_ref):
    tokens = second_ref.shape[0] // 4
    is_low = me_ref[0] < half_count
    far = jnp.where(is_low, cross_ref[:tokens, :].astype(jnp.float32), 0.0)
    first_float = first_ref[3 * tokens :, :].astype(jnp.float32) + far
    second_float = second_ref[3 * tokens :, :].astype(jnp.float32)
    return jnp.concatenate([first_float, second_float], axis=1)


def inner_kernel(half_count, me_ref, key_ref, rms_ref, *refs):
    cross_refs, first_refs, second_refs = [
        refs[place * half_count : (place + 1) * half_count] for place in range(3)
    ]
    out_ref = refs[3 * half_count]
    tokens, features = key_ref.shape
    width = features // half_count
    inside = me_ref[0] & (half_count - 1)
    total = jnp.zeros((tokens, width), jnp.float32)
    for distance in range(half_count):
        owner = inside ^ distance
        start = pl.multiple_of(owner * width, LANES)
        key_float = key_ref[:, pl.ds(start, width)].astype(jnp.float32)
        total = total + key_float * normed_grad_of(
            half_count, me_ref, first_refs[distance], second_refs[distance], cross_refs[distance]
        )
    column = jnp.sum(total, axis=1, keepdims=True) / column_of(rms_ref[...], 0, tokens)
    out_ref[...] = jnp.zeros_like(out_ref)
    store_as_rows(out_ref, 0, column)


def key_kernel(half_count, feature_total, me_ref, key_ref, rms_ref, inner_ref, *refs):
    cross_refs, first_refs, second_refs = [
        refs[place * half_count : (place + 1) * half_count] for place in range(3)
    ]
    key_out_ref = refs[3 * half_count]
    tokens, features = key_ref.shape
    width = features // half_count
    inside = me_ref[0] & (half_count - 1)
    rms = column_of(rms_ref[...], 0, tokens)
    inner = column_of(inner_ref[...], 0, tokens) / feature_total
    for distance in range(half_count):
        columns = pl.ds(pl.multiple_of((inside ^ distance) * width, LANES), width)
        normed_float = key_ref[:, columns].astype(jnp.float32) / rms
        grad_float = normed_grad_of(
            half_count, me_ref, first_refs[distance], second_refs[distance], cross_refs[distance]
        )
        key_out_ref[:, columns] = ((grad_float - normed_float * inner) / rms).astype(jnp.bfloat16)


def final_kernel(half_count, me_ref, *refs):
    cross_refs, first_refs, second_refs = [
        refs[place * half_count : (place + 1) * half_count] for place in range(3)
    ]
    attended_ref, query_ref, value_ref = refs[3 * half_count :]
    tokens, features = attended_ref.shape
    width = features // half_count
    single = width // 2
    is_high = me_ref[0] >= half_count
    inside = me_ref[0] & (half_count - 1)
    for distance in range(half_count):
        start = pl.multiple_of((inside ^ distance) * width, LANES)
        first = pl.ds(start, single)
        second = pl.ds(pl.multiple_of(start + single, LANES), single)
        cross_ref = cross_refs[distance]

        def block(refs, place):
            return refs[distance][place * tokens : (place + 1) * tokens, :]

        def joined(refs, place, far):
            whole = block(refs, place).astype(jnp.float32) + cross_ref[
                far * tokens : (far + 1) * tokens, :
            ].astype(jnp.float32)
            return whole.astype(jnp.bfloat16)

        attended_ref[:, first] = block(first_refs, 0)
        query_ref[:, first] = block(first_refs, 1)
        value_ref[:, second] = block(second_refs, 2)

        @pl.when(is_high)
        def _():
            attended_ref[:, second] = joined(second_refs, 0, 0)
            query_ref[:, second] = joined(second_refs, 1, 1)
            value_ref[:, first] = block(first_refs, 2)

        @pl.when(jnp.logical_not(is_high))
        def _():
            attended_ref[:, second] = block(second_refs, 0)
            query_ref[:, second] = block(second_refs, 1)
            value_ref[:, first] = joined(first_refs, 2, 1)


def lane_rows(vector, row_count):
    return jnp.pad(vector, (0, row_count * LANES - vector.shape[0])).reshape(row_count, LANES)


def half_array(rows, columns):
    return jax.ShapeDtypeStruct((rows, columns), jnp.bfloat16)


def call(kernel, out_shapes, scalars, arrays, scratch=(), in_hbm=0, out_hbm=False, flops=0):
    vmem, anywhere = pl.BlockSpec(memory_space=pltpu.VMEM), pl.BlockSpec(memory_space=pl.ANY)
    return pl.pallas_call(
        kernel,
        out_shape=out_shapes,
        in_specs=[pl.BlockSpec(memory_space=pltpu.SMEM)] * len(scalars)
        + [anywhere] * in_hbm
        + [vmem] * (len(arrays) - in_hbm),
        out_specs=jax.tree.map(lambda shape: anywhere if out_hbm else vmem, out_shapes),
        scratch_shapes=list(scratch),
        compiler_params=pltpu.CompilerParams(vmem_limit_bytes=PACK_VMEM_BYTES if in_hbm else VMEM_BYTES),
        cost_estimate=pl.CostEstimate(flops=flops, bytes_accessed=0, transcendentals=0) if flops else None,
    )(*scalars, *arrays)


def swap(block, distance):
    count = lax.axis_size("seq")
    return lax.ppermute(block, "seq", [(i, i ^ distance) for i in range(count)])


def swap_inside(blocks):
    return [blocks[0]] + [swap(block, d) for d, block in enumerate(blocks) if d]


def swap_across(blocks):
    return [swap(block, len(blocks) + d) for d, block in enumerate(blocks)]


def exchange_inside(rows, half_count):
    count = 2 * half_count
    groups = [list(range(half_count)), list(range(half_count, count))]
    parts = rows.reshape(half_count, -1, rows.shape[1])
    return lax.all_to_all(
        parts, "seq", split_axis=0, concat_axis=0, tiled=True, axis_index_groups=groups
    ).reshape(rows.shape)


def sum_over_head(block):
    count = lax.axis_size("head")
    if count & (count - 1):
        return lax.psum(block, "head")
    return block + sum(
        lax.ppermute(block, "head", [(i, i ^ d) for i in range(count)]) for d in range(1, count)
    )


def by_halves(queries, key_vectors, values, cotangent, cluster, block_pattern):
    count = lax.axis_size("seq")
    half_count = count // 2
    tokens, features = queries.shape
    width = features // half_count
    single = width // 2
    cluster_count, block_count, _ = block_pattern.shape
    half_len = half_count * tokens
    shape = (tokens, half_count, cluster_count, block_count)
    row_count = -(-tokens // (8 * LANES)) * 8
    stat_rows = -(-half_len // (8 * LANES)) * 8
    me = lax.axis_index("seq").astype(jnp.int32).reshape(1)
    packed_shape = half_array(half_count * 3 * tokens, width)
    packed = call(
        functools.partial(pack_kernel, half_count),
        packed_shape,
        [],
        [queries, values, cotangent],
        [
            pltpu.VMEM((3, tokens, features), jnp.bfloat16),
            pltpu.VMEM(packed_shape.shape, jnp.bfloat16),
            pltpu.SemaphoreType.DMA((3,)),
            pltpu.SemaphoreType.DMA((3 * half_count,)),
        ],
        in_hbm=3,
        out_hbm=True,
    )
    packed, key_vectors, cluster = lax.optimization_barrier((packed, key_vectors, cluster))
    packed = exchange_inside(packed, half_count)
    ids = lane_rows(cluster[:, 0], ID_ROWS).astype(jnp.bfloat16)
    key_float = key_vectors.astype(jnp.float32)
    square_sum = sum_over_head(lane_rows(jnp.sum(key_float * key_float, axis=1), row_count))
    feature_total = HEADS * HEAD_DIM
    key_rms = jnp.sqrt(square_sum / feature_total + EPSILON)
    sent = call(
        functools.partial(pack_keys_kernel, half_count),
        [half_array(tokens + ID_ROWS, width)] * half_count
        + [half_array(2 * tokens + ID_ROWS, single)] * half_count,
        [me],
        [queries, values, cotangent, key_vectors, key_rms, ids],
    )
    keys = swap_inside(sent[:half_count])
    cross_sent = list(sent[half_count:])
    for distance in range(half_count // 2):
        cross_sent[distance], keys[1] = lax.optimization_barrier((cross_sent[distance], keys[1]))
    cross = swap_across(cross_sent)
    pattern_rows = block_pattern.transpose(1, 0, 2).reshape(block_count, -1).astype(jnp.float32)
    pattern_rows = jnp.pad(pattern_rows, ((0, 0), (0, LANES - cluster_count * block_count)))
    wide = pltpu.VMEM((half_len, 2 * HEAD_DIM), jnp.bfloat16)
    slim = pltpu.VMEM((half_len, HEAD_DIM), jnp.bfloat16)
    sums = pltpu.VMEM((half_len, HEAD_DIM), jnp.float32)
    turned = pltpu.VMEM((HEAD_DIM, half_len), jnp.bfloat16)
    ids_column = pltpu.VMEM((half_len, 1), jnp.float32)
    block_flops = 12 * half_len * half_len * single
    inputs = [pattern_rows, packed] + cross + keys
    stats = call(
        functools.partial(stats_kernel, shape, stat_rows),
        jax.ShapeDtypeStruct((3 * stat_rows * (single // HEAD_DIM), LANES), jnp.float32),
        [me],
        inputs,
        [wide, wide, slim, slim, ids_column, ids_column],
        flops=block_flops // 3,
    )
    far_stats = swap(stats, half_count)
    firsts = call(
        functools.partial(first_kernel, shape),
        [half_array(4 * tokens, single)] * half_count
        + [half_array(2 * tokens, single)] * half_count
        + [
            half_array(2 * half_len, single),
            jax.ShapeDtypeStruct((2 * half_len, single), jnp.float32),
        ],
        [me],
        inputs + [stats],
        [wide, wide, slim, slim, wide, slim, ids_column, ids_column, slim, slim]
        + [sums, sums, sums, sums] + [turned] * 4,
        flops=block_flops + block_flops // 2,
    )
    *firsts, far_stats = lax.optimization_barrier((*firsts, far_stats))
    rest = firsts[half_count:]
    firsts = swap_inside(firsts[:half_count])
    results = call(
        functools.partial(second_head_kernel, shape, stat_rows),
        [half_array(4 * tokens, single)] * half_count
        + [half_array(2 * tokens, single)] * half_count,
        [me],
        inputs + [stats, far_stats] + rest[half_count:] + rest[:half_count],
        [wide, wide, slim, slim, wide, slim, ids_column, ids_column, slim, slim]
        + [sums, sums, slim, slim] + [turned] * 2,
        flops=block_flops,
    )
    far_sent, seconds = list(results[half_count:]), list(results[:half_count])
    near = half_count // 2
    far_sent[:near], firsts = lax.optimization_barrier((far_sent[:near], firsts))
    far_parts = swap_across(far_sent)
    seconds, far_parts[-1] = lax.optimization_barrier((seconds, far_parts[-1]))
    seconds = swap_inside(seconds)
    inner = call(
        functools.partial(inner_kernel, half_count),
        jax.ShapeDtypeStruct((row_count, LANES), jnp.float32),
        [me],
        [key_vectors, key_rms] + far_parts + firsts + seconds,
    )
    inner = sum_over_head(inner)
    attended, query_grad, value_grad = call(
        functools.partial(final_kernel, half_count),
        [half_array(tokens, features)] * 3,
        [me],
        far_parts + firsts + seconds,
    )
    key_grad = call(
        functools.partial(key_kernel, half_count, feature_total),
        half_array(tokens, features),
        [me],
        [key_vectors, key_rms, inner] + far_parts + firsts + seconds,
    )
    return attended, query_grad, key_grad, value_grad


def per_device_any(queries, key_vectors, values, cotangent, cluster, block_pattern):
    count = lax.axis_size("seq")
    tokens, features = queries.shape
    cluster_count, block_count, _ = block_pattern.shape
    fits = (
        count % 2 == 0
        and count & (count - 1) == 0
        and features % (count * HEAD_DIM) == 0
        and tokens % ID_ROWS == 0
        and tokens * count % (2 * BLK) == 0
        and cluster_count * block_count <= LANES
    )
    chosen = by_halves if fits else per_device
    return chosen(queries, key_vectors, values, cotangent, cluster, block_pattern)


def solution(mesh):
    in_specs = (
        P("seq", "head"),
        P("seq", "head"),
        P("seq", "head"),
        P("seq", "head"),
        P("seq", None),
        P(),
    )
    out_specs = (P("seq", "head"), P("seq", "head"), P("seq", "head"), P("seq", "head"))
    return jax.shard_map(
        per_device_any, mesh=mesh, in_specs=in_specs, out_specs=out_specs, check_vma=False
    )
```

```python
import functools

import jax
import jax.numpy as jnp
from jax import lax
from jax.experimental import pallas as pl
from jax.experimental.pallas import tpu as pltpu
from jax.sharding import PartitionSpec as P

HEADS = 32
HEAD_DIM = 128
GS = 4
BLK = 128


NEG_FILL = -1e30
EPSILON = 1e-05
SCORE_SCALE = HEAD_DIM ** (-0.5)
EXPONENT_SCALE = SCORE_SCALE * 1.4426950408889634
LANES = 128
ID_ROWS = 16
QUERY_TILE = 256
VMEM_BYTES = 32 << 20
PACK_VMEM_BYTES = 60 << 20


def contract_last(left_side, right_side):
    return lax.dot_general(
        left_side, right_side, (((1,), (1,)), ((), ())), preferred_element_type=jnp.float32
    )


def contract_first(left_side, right_side):
    return lax.dot_general(
        left_side, right_side, (((0,), (0,)), ((), ())), preferred_element_type=jnp.float32
    )


def visible_mask(pattern, query_pos, query_live, key_pos, key_live):
    pattern_rows = pattern[query_pos // BLK]
    allowed = jnp.take(pattern_rows, key_pos // BLK, axis=1) == 1
    causal = key_pos[None, :] <= query_pos[:, None]
    return allowed & causal & query_live[:, None] & key_live[None, :]


def cluster_ranks(table, cluster_index):
    source_count, tok_count = table.shape
    in_cluster = table == cluster_index
    token_iota = jnp.arange(tok_count, dtype=jnp.int32)
    earlier_table = (token_iota[:, None] < token_iota[None, :]).astype(jnp.bfloat16)
    earlier = jnp.dot(
        in_cluster.astype(jnp.bfloat16), earlier_table, preferred_element_type=jnp.float32
    ).astype(jnp.int32)
    global_pos = (
        jnp.arange(source_count, dtype=jnp.int32)[:, None] * tok_count + token_iota[None, :]
    )
    return (in_cluster, earlier, global_pos)


def code_positions(slot_code, global_pos, capacity):
    matches = slot_code[:, :, None] == jnp.arange(capacity, dtype=jnp.int32)[None, None, :]
    positions = jnp.sum(jnp.where(matches, global_pos[:, :, None], 0), axis=1)
    occupied = jnp.any(matches, axis=1)
    return (positions, occupied)


def rank_positions(table, cluster_index, capacity):
    in_cluster, earlier, global_pos = cluster_ranks(table, cluster_index)
    rank_code = jnp.where(in_cluster, earlier, -1)
    positions, occupied = code_positions(rank_code, global_pos, capacity)
    return (positions.reshape(-1), occupied.reshape(-1))


def dispatch_rows(outgoing):
    return lax.all_to_all(outgoing, "seq", split_axis=1, concat_axis=1, tiled=True)


def combine_rows(outgoing):
    return lax.all_to_all(outgoing, "seq", split_axis=1, concat_axis=1, tiled=True)


def forward_heads(query_slots, key_slots, value_slots, grad_slots, visible, score_scale):
    query_count, features = query_slots.shape
    key_count = key_slots.shape[0]
    head_count = features // HEAD_DIM
    attended = jnp.zeros((query_count, features), jnp.bfloat16)
    query_grad = jnp.zeros((query_count, features), jnp.bfloat16)
    side_result = jnp.zeros((2, key_count, features), jnp.float32)

    def one_head(head_index, running):
        attended_acc, query_acc, side_acc = running
        column_start = head_index * HEAD_DIM
        query_rows = lax.dynamic_slice_in_dim(query_slots, column_start, HEAD_DIM, 1)
        key_rows = lax.dynamic_slice_in_dim(key_slots, column_start, HEAD_DIM, 1)
        value_rows = lax.dynamic_slice_in_dim(value_slots, column_start, HEAD_DIM, 1)
        grad_rows = lax.dynamic_slice_in_dim(grad_slots, column_start, HEAD_DIM, 1)
        scores = jnp.where(visible, contract_last(query_rows, key_rows) * score_scale, NEG_FILL)
        row_max = jnp.max(scores, axis=1, keepdims=True)
        weights = jnp.where(visible, jnp.exp(scores - row_max), 0.0)
        row_total = jnp.maximum(jnp.sum(weights, axis=1, keepdims=True), 1.0)
        probabilities = weights / row_total
        prob_half = probabilities.astype(jnp.bfloat16)
        attended_head = jnp.dot(prob_half, value_rows, preferred_element_type=jnp.float32).astype(
            jnp.bfloat16
        )
        prob_grad = contract_last(grad_rows, value_rows)
        row_delta = jnp.sum(probabilities * prob_grad, axis=1, keepdims=True)
        score_grad = (probabilities * (prob_grad - row_delta)).astype(jnp.bfloat16)
        query_head = (
            jnp.dot(score_grad, key_rows, preferred_element_type=jnp.float32) * score_scale
        ).astype(jnp.bfloat16)
        attended_acc = lax.dynamic_update_slice_in_dim(attended_acc, attended_head, column_start, 1)
        query_acc = lax.dynamic_update_slice_in_dim(query_acc, query_head, column_start, 1)
        key_part = contract_first(score_grad, query_rows)
        value_part = contract_first(prob_half, grad_rows)
        side_acc = lax.dynamic_update_slice_in_dim(
            side_acc, jnp.stack([key_part, value_part]), column_start, 2
        )
        return (attended_acc, query_acc, side_acc)

    return lax.fori_loop(0, head_count, one_head, (attended, query_grad, side_result))


def per_device(queries, key_vectors, values, cotangent, cluster, block_pattern):
    seq_count = lax.axis_size("seq")
    tok_count, features = queries.shape
    slot_count = 2 * tok_count // seq_count
    group_count = seq_count // GS
    score_scale = HEAD_DIM ** (-0.5)
    my_index = lax.axis_index("seq")
    group_index = my_index // GS
    key_float = key_vectors.astype(jnp.float32)
    square_sum = lax.psum(jnp.sum(key_float * key_float, axis=1), "head")
    key_rms = jnp.sqrt(square_sum / (HEADS * HEAD_DIM) + EPSILON)[:, None]
    normed_float = key_float / key_rms
    normed = normed_float.astype(jnp.bfloat16)
    own_ids = cluster[:, 0]
    everyone = lax.all_gather(own_ids, "seq", axis=0, tiled=True)
    table = everyone.reshape(seq_count, tok_count)
    token_iota = jnp.arange(tok_count, dtype=jnp.int32)
    onehot_own = (own_ids[:, None] == jnp.arange(group_count, dtype=jnp.int32)[None, :]).astype(
        jnp.bfloat16
    )
    before_table = (token_iota[:, None] > token_iota[None, :]).astype(jnp.bfloat16)
    before = jnp.dot(before_table, onehot_own, preferred_element_type=jnp.float32)
    own_rank = jnp.sum(before * onehot_own.astype(jnp.float32), axis=1).astype(jnp.int32)
    pattern = lax.dynamic_index_in_dim(block_pattern, group_index, 0, keepdims=False)
    stacked_inputs = jnp.stack([queries, normed, values, cotangent])
    quarter = features // GS
    capacity = GS * slot_count
    split_inputs = stacked_inputs.reshape(4, tok_count, GS, quarter)
    placed = (
        jnp.zeros((4, group_count, capacity, GS, quarter), jnp.bfloat16)
        .at[:, own_ids, own_rank]
        .set(split_inputs)
    )
    outgoing = placed.transpose(0, 1, 3, 2, 4).reshape(4, seq_count * capacity, quarter)
    arrived = dispatch_rows(outgoing)
    flat_positions, flat_present = rank_positions(table, group_index, capacity)
    visible = visible_mask(pattern, flat_positions, flat_present, flat_positions, flat_present)
    attended, query_grad, both_terms = forward_heads(
        arrived[0], arrived[1], arrived[2], arrived[3], visible, score_scale
    )
    normed_grad = (both_terms[0] * score_scale).astype(jnp.bfloat16)
    value_slots = both_terms[1].astype(jnp.bfloat16)
    outgoing_back = jnp.stack([attended, query_grad, normed_grad, value_slots])
    returned = combine_rows(outgoing_back)
    arranged = returned.reshape(4, group_count, GS, capacity, quarter).transpose(1, 3, 0, 2, 4)
    home_rows = arranged[own_ids, own_rank].transpose(1, 0, 2, 3).reshape(4, tok_count, features)
    grad_float = home_rows[2].astype(jnp.float32)
    inner = lax.psum(jnp.sum(normed_float * grad_float, axis=1), "head")
    key_grad = (
        (grad_float - normed_float * (inner / (HEADS * HEAD_DIM))[:, None]) / key_rms
    ).astype(jnp.bfloat16)
    return (home_rows[0], home_rows[1], key_grad, home_rows[3])


def column_of(rows, first_row, count):
    turned = jnp.transpose(rows)
    pieces = []
    for start in range(0, count, LANES):
        place = first_row + start // LANES
        pieces.append(turned[: min(LANES, count - start), place : place + 1])
    return jnp.concatenate(pieces, axis=0)


def ids_of(ref, first_row, count):
    rows = ref[first_row : first_row + ID_ROWS, :LANES].astype(jnp.float32)
    return column_of(rows, 0, count)


def store_as_rows(out_ref, first_row, column):
    count = column.shape[0]
    for start in range(0, count, LANES):
        size = min(LANES, count - start)
        diagonal = lax.broadcasted_iota(jnp.int32, (size, LANES), 0) == lax.broadcasted_iota(
            jnp.int32, (size, LANES), 1
        )
        spread = jnp.where(diagonal, column[start : start + size], 0.0)
        row = first_row + start // LANES
        out_ref[row : row + 1, :] = jnp.sum(spread, axis=0, keepdims=True)


def block_rows(index, size):
    return pl.ds(pl.multiple_of(index * size, 16), size)


def pack_kernel(half_count, query_ref, value_ref, grad_ref, out_ref, held, sorted_rows, in_sems, out_sems):
    tokens, features = query_ref.shape
    width = features // half_count
    arrivals = [
        pltpu.make_async_copy(source_ref, held.at[place], in_sems.at[place])
        for place, source_ref in enumerate((query_ref, value_ref, grad_ref))
    ]
    for arrival in arrivals:
        arrival.start()
    copies = []
    for place, arrival in enumerate(arrivals):
        arrival.wait()
        for owner in range(half_count):
            rows = pl.ds((owner * 3 + place) * tokens, tokens)
            sorted_rows[rows, :] = held[place, :, owner * width : (owner + 1) * width]
            copy = pltpu.make_async_copy(
                sorted_rows.at[rows, :], out_ref.at[rows, :], out_sems.at[place * half_count + owner]
            )
            copy.start()
            copies.append(copy)
    for copy in copies:
        copy.wait()


def pack_keys_kernel(
    half_count, me_ref, query_ref, value_ref, grad_ref, key_ref, rms_ref, ids_ref, *out_refs
):
    tokens, features = key_ref.shape
    width = features // half_count
    single = width // 2
    is_high = me_ref[0] >= half_count
    inside = me_ref[0] & (half_count - 1)
    key_refs, cross_refs = out_refs[:half_count], out_refs[half_count:]
    rms = column_of(rms_ref[...], 0, tokens)

    def normed_columns(first, size):
        return (key_ref[:, pl.ds(first, size)].astype(jnp.float32) / rms).astype(jnp.bfloat16)

    for distance in range(half_count):
        first = pl.multiple_of((inside ^ distance) * width, LANES)
        cross_ref = cross_refs[distance]
        key_refs[distance][:tokens, :] = normed_columns(first, width)
        key_refs[distance][tokens:, :LANES] = ids_ref[...]
        key_refs[distance][tokens:, LANES:] = jnp.zeros((ID_ROWS, width - LANES), jnp.bfloat16)
        cross_ref[2 * tokens :, :LANES] = ids_ref[...]
        if single > LANES:
            cross_ref[2 * tokens :, LANES:] = jnp.zeros((ID_ROWS, single - LANES), jnp.bfloat16)

        @pl.when(is_high)
        def send_down():
            second = pl.multiple_of(first + single, LANES)
            cross_ref[:tokens, :] = query_ref[:, pl.ds(second, single)]
            cross_ref[tokens : 2 * tokens, :] = grad_ref[:, pl.ds(second, single)]

        @pl.when(jnp.logical_not(is_high))
        def send_up():
            cross_ref[:tokens, :] = normed_columns(first, single)
            cross_ref[tokens : 2 * tokens, :] = value_ref[:, pl.ds(first, single)]


class Slots:
    def __init__(self, shape, me_ref, pattern_ref, packed_ref, key_refs, cross_refs):
        self.tokens, self.half_count, self.cluster_count, self.block_count = shape
        self.half_len = self.tokens * self.half_count
        self.half_blocks = self.half_len // BLK
        self.is_high = me_ref[0] >= self.half_count
        self.inside = me_ref[0] & (self.half_count - 1)
        self.pattern_ref, self.packed_ref = pattern_ref, packed_ref
        self.key_refs, self.cross_refs = key_refs, cross_refs
        lane = lax.broadcasted_iota(jnp.int32, (1, LANES), 1)
        lane_cluster = jnp.zeros((1, LANES), jnp.int32)
        for index in range(1, self.cluster_count + 1):
            lane_cluster = lane_cluster + (lane >= index * self.block_count).astype(jnp.int32)
        self.lane_block = lane - lane_cluster * self.block_count
        self.lane_cluster = lane_cluster.astype(jnp.float32)

    def own_ids(self, ids_all):
        for distance in range(self.half_count):
            ids_all[block_rows(self.inside ^ distance, self.tokens), :] = ids_of(
                self.key_refs[distance], self.tokens, self.tokens
            )

    def cross_ids(self, ids_all):
        for distance in range(self.half_count):
            ids_all[block_rows(self.inside ^ distance, self.tokens), :] = ids_of(
                self.cross_refs[distance], 2 * self.tokens, self.tokens
            )

    def query_features(self, ids_all, target, high):
        for block in range(self.half_blocks):
            rows = slice(block * BLK, (block + 1) * BLK)
            place = block + high * self.half_blocks
            allowed = self.pattern_ref[pl.ds(place, 1), :] == 1.0
            same = ids_all[rows, :] == self.lane_cluster
            target[rows, HEAD_DIM:] = jnp.where(same & allowed, 0.0, NEG_FILL).astype(jnp.bfloat16)

    def key_features(self, ids_all, target, high):
        for block in range(self.half_blocks):
            rows = slice(block * BLK, (block + 1) * BLK)
            place = block + high * self.half_blocks
            same = ids_all[rows, :] == self.lane_cluster
            target[rows, HEAD_DIM:] = jnp.where(same & (self.lane_block == place), 1.0, 0.0).astype(
                jnp.bfloat16
            )

    def own(self, column, query_all, key_all, value_all, grad_all):
        columns = slice(column, column + HEAD_DIM)
        stride = 3 * self.tokens
        for source in range(self.half_count):
            rows = slice(source * self.tokens, (source + 1) * self.tokens)
            for place, target in enumerate((query_all, value_all, grad_all)):
                first = source * stride + place * self.tokens
                target[rows, :HEAD_DIM] = self.packed_ref[first : first + self.tokens, columns]
        for distance in range(self.half_count):
            rows = block_rows(self.inside ^ distance, self.tokens)
            key_all[rows, :HEAD_DIM] = self.key_refs[distance][: self.tokens, columns]

    def cross(self, column, first_all, second_all):
        columns = slice(column, column + HEAD_DIM)
        for distance in range(self.half_count):
            rows = block_rows(self.inside ^ distance, self.tokens)
            cross_ref = self.cross_refs[distance]
            first_all[rows, :HEAD_DIM] = cross_ref[: self.tokens, columns]
            second_all[rows, :] = cross_ref[self.tokens : 2 * self.tokens, columns]


class Keys:
    def __init__(self, key, value, key_turned=None, value_turned=None):
        self.key, self.value = key, value
        self.key_turned, self.value_turned = key_turned, value_turned

    def turn(self):
        self.key_turned[...] = jnp.transpose(self.key[:, :HEAD_DIM])
        self.value_turned[...] = jnp.transpose(self.value[...])


def tile_scores(query_tile, keys, limit, first):
    scores = contract_last(keys.key[:limit, :], query_tile)
    if first is not None:
        key_index = lax.broadcasted_iota(jnp.int32, scores.shape, 0)
        query_index = lax.broadcasted_iota(jnp.int32, scores.shape, 1) + first
        scores = jnp.where(key_index <= query_index, scores, NEG_FILL)
    return scores


def tile_stats(scores, prob_grads):
    row_max = functools.reduce(
        jnp.maximum, [jnp.max(part, axis=0, keepdims=True) for part in scores]
    )
    weights = [jnp.exp2((part - row_max) * EXPONENT_SCALE) for part in scores]
    row_total = sum(jnp.sum(part, axis=0, keepdims=True) for part in weights)
    row_delta = sum(
        jnp.sum(part * grad, axis=0, keepdims=True) for part, grad in zip(weights, prob_grads)
    )
    return weights, row_max, row_total, row_delta


def tile_products(query_tile, grad_tile, pieces):
    scores = [tile_scores(query_tile, *piece) for piece in pieces]
    return scores, [contract_last(keys.value[:limit, :], grad_tile) for keys, limit, _ in pieces]


def all_tiles(query_all, grad_all, half_len, pieces_of, sums, stats_of, keep, add=False):
    tiles = own_tiles(half_len)
    ready = None
    for index, (first, rows, limit) in enumerate(tiles):
        now = ready or tile_products(query_all[rows, :], grad_all[rows, :], pieces_of(first, limit))
        ready = None
        if index + 1 < len(tiles):
            later, later_rows, later_limit = tiles[index + 1]
            ready = tile_products(
                query_all[later_rows, :], grad_all[later_rows, :], pieces_of(later, later_limit)
            )
        keep(
            rows,
            *tile_backward(
                query_all[rows, :],
                grad_all[rows, :],
                pieces_of(first, limit),
                sums,
                stats_of(first, limit - first) if stats_of else None,
                first == 0 and not add,
                *now,
            ),
        )


def tile_backward(query_tile, grad_tile, pieces, sums, stats, is_first, scores, prob_grads):
    if stats is None:
        weights, _, row_total, row_delta = tile_stats(scores, prob_grads)
        inverse = 1.0 / jnp.maximum(row_total, 1.0)
        row_delta = row_delta * inverse
    else:
        row_max, inverse, row_delta = stats
        weights = [jnp.exp2((part - row_max) * EXPONENT_SCALE) for part in scores]
    attended, query_grad = 0.0, 0.0
    for index, (keys, limit, first) in enumerate(pieces):
        probabilities = weights[index] * inverse
        prob_half = probabilities.astype(jnp.bfloat16)
        score_grad = (probabilities * (prob_grads[index] - row_delta)).astype(jnp.bfloat16)
        attended += jnp.dot(
            keys.value_turned[:, :limit], prob_half, preferred_element_type=jnp.float32
        )
        query_grad += jnp.dot(
            keys.key_turned[:, :limit], score_grad, preferred_element_type=jnp.float32
        )
        key_part = jnp.dot(
            score_grad, query_tile[:, :HEAD_DIM], preferred_element_type=jnp.float32
        )
        value_part = jnp.dot(prob_half, grad_tile, preferred_element_type=jnp.float32)
        key_sum, value_sum = sums[index]
        fresh = 0 if is_first else (limit if first is None else first)
        if fresh:
            key_sum[:fresh, :] += key_part[:fresh]
            value_sum[:fresh, :] += value_part[:fresh]
        if fresh < limit:
            key_sum[fresh:limit, :] = key_part[fresh:]
            value_sum[fresh:limit, :] = value_part[fresh:]
    return (
        jnp.transpose(attended).astype(jnp.bfloat16),
        jnp.transpose(query_grad * SCORE_SCALE).astype(jnp.bfloat16),
    )


def own_tiles(half_len):
    tile = QUERY_TILE if half_len % QUERY_TILE == 0 else BLK
    return [(first, slice(first, first + tile), first + tile) for first in range(0, half_len, tile)]


def note_stats(out_ref, stat_rows, head, first, found):
    for place, column in enumerate(found[1:]):
        store_as_rows(out_ref, (3 * head + place) * stat_rows + first // LANES, column)


def stats_kernel(shape, stat_rows, me_ref, pattern_ref, packed_ref, *refs):
    half_count = shape[1]
    cross_refs, key_refs = refs[:half_count], refs[half_count : 2 * half_count]
    out_ref, query_all, key_all, value_all, grad_all, ids, other_ids = refs[2 * half_count :]
    slots = Slots(shape, me_ref, pattern_ref, packed_ref, key_refs, cross_refs)
    single = packed_ref.shape[1] // 2
    out_ref[...] = jnp.zeros_like(out_ref)
    slots.own_ids(ids)
    slots.key_features(ids, key_all, slots.is_high.astype(jnp.int32))

    @pl.when(slots.is_high)
    def _():
        slots.query_features(ids, query_all, 1)

    @pl.when(jnp.logical_not(slots.is_high))
    def _():
        slots.cross_ids(other_ids)
        slots.query_features(other_ids, query_all, 1)

    for head in range(single // HEAD_DIM):
        column = head * HEAD_DIM
        slots.own(single + column, query_all, key_all, value_all, grad_all)

        def note(first, rows, limit, causal_from):
            scores = tile_scores(query_all[rows, :], Keys(key_all, value_all), limit, causal_from)
            prob_grad = contract_last(value_all[:limit, :], grad_all[rows, :])
            for place, found in enumerate(tile_stats([scores], [prob_grad])[1:]):
                row = (3 * head + place) * stat_rows + first // LANES
                for start in range(0, found.shape[1], LANES):
                    out_ref[row + start // LANES : row + start // LANES + 1, :] = found[
                        :, start : start + LANES
                    ]

        @pl.when(slots.is_high)
        def _():
            for first, rows, limit in own_tiles(slots.half_len):
                note(first, rows, limit, first)

        @pl.when(jnp.logical_not(slots.is_high))
        def _():
            slots.cross(column, query_all, grad_all)
            for first, rows, _ in own_tiles(slots.half_len):
                note(first, rows, slots.half_len, None)


def store_own(slots, result_refs, column, attended, query_grad, value_sum, key_sum):
    tokens = slots.tokens
    columns = slice(column, column + HEAD_DIM)
    for distance, target in enumerate(result_refs):
        rows = block_rows(slots.inside ^ distance, tokens)
        target[:tokens, columns] = attended[rows, :]
        target[tokens : 2 * tokens, columns] = query_grad[rows, :]
        target[2 * tokens : 3 * tokens, columns] = value_sum[rows, :].astype(jnp.bfloat16)
        target[3 * tokens :, columns] = (key_sum[rows, :] * SCORE_SCALE).astype(jnp.bfloat16)


def first_kernel(shape, me_ref, pattern_ref, packed_ref, *refs):
    half_count = shape[1]
    cross_refs, key_refs = refs[:half_count], refs[half_count : 2 * half_count]
    refs = refs[2 * half_count + 1 :]
    result_refs, cross_out_refs = refs[:half_count], refs[half_count : 2 * half_count]
    second_ref, sums_ref = refs[2 * half_count : 2 * half_count + 2]
    (query_all, key_all, value_all, grad_all, other_key, other_value, ids, other_ids, attended,
     query_grad, key_sum, value_sum, other_key_sum, other_value_sum, *turned) = refs[
        2 * half_count + 2 :
    ]
    own, other = Keys(key_all, value_all, *turned[:2]), Keys(other_key, other_value, *turned[2:])
    slots = Slots(shape, me_ref, pattern_ref, packed_ref, key_refs, cross_refs)
    single = packed_ref.shape[1] // 2
    half_len = slots.half_len
    high = slots.is_high.astype(jnp.int32)
    slots.own_ids(ids)
    slots.key_features(ids, key_all, high)
    slots.query_features(ids, query_all, high)

    def run(others, other_sums, attended_out, query_grad_out, key_out, value_out):
        def keep(rows, attended_tile, query_grad_tile):
            attended_out[rows, :], query_grad_out[rows, :] = attended_tile, query_grad_tile

        all_tiles(
            query_all,
            grad_all,
            half_len,
            lambda first, limit: others + [(own, limit, first)],
            other_sums + [(key_out, value_out)],
            None,
            keep,
        )

    @pl.when(slots.is_high)
    def _():
        slots.cross_ids(other_ids)
        slots.key_features(other_ids, other_key, 0)

    for head in range(single // HEAD_DIM):
        column = head * HEAD_DIM
        columns = slice(column, column + HEAD_DIM)
        slots.own(column, query_all, key_all, value_all, grad_all)
        own.turn()

        @pl.when(slots.is_high)
        def _():
            slots.cross(column, other_key, other_value)
            other.turn()
            run(
                [(other, half_len, None)],
                [(other_key_sum, other_value_sum)],
                attended, query_grad, key_sum, value_sum,
            )
            for distance in range(half_count):
                rows = block_rows(slots.inside ^ distance, slots.tokens)
                target = cross_out_refs[distance]
                target[: slots.tokens, columns] = (other_key_sum[rows, :] * SCORE_SCALE).astype(
                    jnp.bfloat16
                )
                target[slots.tokens :, columns] = other_value_sum[rows, :].astype(jnp.bfloat16)

        @pl.when(jnp.logical_not(slots.is_high))
        def _():
            run([], [], attended, query_grad, key_sum, value_sum)

        store_own(slots, result_refs, column, attended, query_grad, value_sum, key_sum)

        @pl.when(jnp.logical_not(slots.is_high))
        def _():
            slots.own(single + column, query_all, key_all, value_all, grad_all)
            own.turn()
            run(
                [], [],
                second_ref.at[:half_len, columns],
                second_ref.at[half_len:, columns],
                sums_ref.at[:half_len, columns],
                sums_ref.at[half_len:, columns],
            )


def joint_rows(stat_rows, head, own_stats_ref, far_stats_ref):
    (own_max, own_total, own_delta), (far_max, far_total, far_delta) = [
        [
            ref[(3 * head + place) * stat_rows : (3 * head + place + 1) * stat_rows, :]
            for place in range(3)
        ]
        for ref in (own_stats_ref, far_stats_ref)
    ]
    row_max = jnp.maximum(own_max, far_max)
    own_part = jnp.exp2((own_max - row_max) * EXPONENT_SCALE)
    far_part = jnp.exp2((far_max - row_max) * EXPONENT_SCALE)
    inverse = 1.0 / jnp.maximum(own_total * own_part + far_total * far_part, 1.0)
    return row_max, inverse, (own_delta * own_part + far_delta * far_part) * inverse


def second_head_kernel(shape, stat_rows, me_ref, pattern_ref, packed_ref, *refs):
    half_count = shape[1]
    cross_refs, key_refs = refs[:half_count], refs[half_count : 2 * half_count]
    own_stats_ref, far_stats_ref, early_ref, sums_ref = refs[2 * half_count : 2 * half_count + 4]
    refs = refs[2 * half_count + 4 :]
    first_cross_refs, result_refs, cross_out_refs = [
        refs[place * half_count : (place + 1) * half_count] for place in range(3)
    ]
    (query_all, key_all, value_all, grad_all, other_query, other_grad, ids, other_ids, attended,
     query_grad, key_sum, value_sum, other_attended, other_query_grad, *turned) = refs[
        3 * half_count :
    ]
    own = Keys(key_all, value_all, *turned)
    slots = Slots(shape, me_ref, pattern_ref, packed_ref, key_refs, cross_refs)
    single = packed_ref.shape[1] // 2
    half_len, tokens = slots.half_len, slots.tokens
    slots.own_ids(ids)
    slots.key_features(ids, key_all, slots.is_high.astype(jnp.int32))

    @pl.when(slots.is_high)
    def _():
        slots.query_features(ids, query_all, 1)
        for distance in range(half_count):
            cross_out_refs[distance][...] = first_cross_refs[distance][...]

    @pl.when(jnp.logical_not(slots.is_high))
    def _():
        slots.cross_ids(other_ids)
        slots.query_features(other_ids, other_query, 1)

    for head in range(single // HEAD_DIM):
        column = head * HEAD_DIM
        columns = slice(column, column + HEAD_DIM)
        slots.own(single + column, query_all, key_all, value_all, grad_all)
        own.turn()
        joint_table = joint_rows(stat_rows, head, own_stats_ref, far_stats_ref)

        def joint_stats(first, size):
            places = range(first // LANES, (first + size) // LANES)
            return [
                jnp.concatenate([rows[place : place + 1, :] for place in places], axis=1)
                for rows in joint_table
            ]

        @pl.when(slots.is_high)
        def _():
            def keep(rows, attended_tile, query_grad_tile):
                attended[rows, :], query_grad[rows, :] = attended_tile, query_grad_tile

            all_tiles(
                query_all,
                grad_all,
                half_len,
                lambda first, limit: [(own, limit, first)],
                [(key_sum, value_sum)],
                joint_stats,
                keep,
            )

        @pl.when(jnp.logical_not(slots.is_high))
        def _():
            slots.cross(column, other_query, other_grad)
            attended[...] = early_ref[:half_len, columns]
            query_grad[...] = early_ref[half_len:, columns]
            key_sum[...] = sums_ref[:half_len, columns]
            value_sum[...] = sums_ref[half_len:, columns]

            def keep(rows, attended_tile, query_grad_tile):
                other_attended[rows, :], other_query_grad[rows, :] = attended_tile, query_grad_tile

            all_tiles(
                other_query,
                other_grad,
                half_len,
                lambda first, limit: [(own, half_len, None)],
                [(key_sum, value_sum)],
                joint_stats,
                keep,
                add=True,
            )
            for distance in range(half_count):
                rows = block_rows(slots.inside ^ distance, tokens)
                target = cross_out_refs[distance]
                target[:tokens, columns] = other_attended[rows, :]
                target[tokens:, columns] = other_query_grad[rows, :]

        store_own(slots, result_refs, column, attended, query_grad, value_sum, key_sum)


def normed_grad_of(half_count, me_ref, first_ref, second_ref, cross_ref):
    tokens = second_ref.shape[0] // 4
    is_low = me_ref[0] < half_count
    far = jnp.where(is_low, cross_ref[:tokens, :].astype(jnp.float32), 0.0)
    first_float = first_ref[3 * tokens :, :].astype(jnp.float32) + far
    second_float = second_ref[3 * tokens :, :].astype(jnp.float32)
    return jnp.concatenate([first_float, second_float], axis=1)


def inner_kernel(half_count, me_ref, key_ref, rms_ref, *refs):
    cross_refs, first_refs, second_refs = [
        refs[place * half_count : (place + 1) * half_count] for place in range(3)
    ]
    out_ref = refs[3 * half_count]
    tokens, features = key_ref.shape
    width = features // half_count
    inside = me_ref[0] & (half_count - 1)
    total = jnp.zeros((tokens, width), jnp.float32)
    for distance in range(half_count):
        owner = inside ^ distance
        start = pl.multiple_of(owner * width, LANES)
        key_float = key_ref[:, pl.ds(start, width)].astype(jnp.float32)
        total = total + key_float * normed_grad_of(
            half_count, me_ref, first_refs[distance], second_refs[distance], cross_refs[distance]
        )
    column = jnp.sum(total, axis=1, keepdims=True) / column_of(rms_ref[...], 0, tokens)
    out_ref[...] = jnp.zeros_like(out_ref)
    store_as_rows(out_ref, 0, column)


def key_kernel(half_count, feature_total, me_ref, key_ref, rms_ref, inner_ref, *refs):
    cross_refs, first_refs, second_refs = [
        refs[place * half_count : (place + 1) * half_count] for place in range(3)
    ]
    key_out_ref = refs[3 * half_count]
    tokens, features = key_ref.shape
    width = features // half_count
    inside = me_ref[0] & (half_count - 1)
    rms = column_of(rms_ref[...], 0, tokens)
    inner = column_of(inner_ref[...], 0, tokens) / feature_total
    for distance in range(half_count):
        columns = pl.ds(pl.multiple_of((inside ^ distance) * width, LANES), width)
        normed_float = key_ref[:, columns].astype(jnp.float32) / rms
        grad_float = normed_grad_of(
            half_count, me_ref, first_refs[distance], second_refs[distance], cross_refs[distance]
        )
        key_out_ref[:, columns] = ((grad_float - normed_float * inner) / rms).astype(jnp.bfloat16)


def final_kernel(half_count, me_ref, *refs):
    cross_refs, first_refs, second_refs = [
        refs[place * half_count : (place + 1) * half_count] for place in range(3)
    ]
    attended_ref, query_ref, value_ref = refs[3 * half_count :]
    tokens, features = attended_ref.shape
    width = features // half_count
    single = width // 2
    is_high = me_ref[0] >= half_count
    inside = me_ref[0] & (half_count - 1)
    for distance in range(half_count):
        start = pl.multiple_of((inside ^ distance) * width, LANES)
        first = pl.ds(start, single)
        second = pl.ds(pl.multiple_of(start + single, LANES), single)
        cross_ref = cross_refs[distance]

        def block(refs, place):
            return refs[distance][place * tokens : (place + 1) * tokens, :]

        def joined(refs, place, far):
            whole = block(refs, place).astype(jnp.float32) + cross_ref[
                far * tokens : (far + 1) * tokens, :
            ].astype(jnp.float32)
            return whole.astype(jnp.bfloat16)

        attended_ref[:, first] = block(first_refs, 0)
        query_ref[:, first] = block(first_refs, 1)
        value_ref[:, second] = block(second_refs, 2)

        @pl.when(is_high)
        def _():
            attended_ref[:, second] = joined(second_refs, 0, 0)
            query_ref[:, second] = joined(second_refs, 1, 1)
            value_ref[:, first] = block(first_refs, 2)

        @pl.when(jnp.logical_not(is_high))
        def _():
            attended_ref[:, second] = block(second_refs, 0)
            query_ref[:, second] = block(second_refs, 1)
            value_ref[:, first] = joined(first_refs, 2, 1)


def lane_rows(vector, row_count):
    return jnp.pad(vector, (0, row_count * LANES - vector.shape[0])).reshape(row_count, LANES)


def half_array(rows, columns):
    return jax.ShapeDtypeStruct((rows, columns), jnp.bfloat16)


def call(kernel, out_shapes, scalars, arrays, scratch=(), in_hbm=0, out_hbm=False, flops=0):
    vmem, anywhere = pl.BlockSpec(memory_space=pltpu.VMEM), pl.BlockSpec(memory_space=pl.ANY)
    return pl.pallas_call(
        kernel,
        out_shape=out_shapes,
        in_specs=[pl.BlockSpec(memory_space=pltpu.SMEM)] * len(scalars)
        + [anywhere] * in_hbm
        + [vmem] * (len(arrays) - in_hbm),
        out_specs=jax.tree.map(lambda shape: anywhere if out_hbm else vmem, out_shapes),
        scratch_shapes=list(scratch),
        compiler_params=pltpu.CompilerParams(vmem_limit_bytes=PACK_VMEM_BYTES if in_hbm else VMEM_BYTES),
        cost_estimate=pl.CostEstimate(flops=flops, bytes_accessed=0, transcendentals=0) if flops else None,
    )(*scalars, *arrays)


def swap(block, distance):
    count = lax.axis_size("seq")
    return lax.ppermute(block, "seq", [(i, i ^ distance) for i in range(count)])


def swap_inside(blocks):
    return [blocks[0]] + [swap(block, d) for d, block in enumerate(blocks) if d]


def swap_across(blocks):
    return [swap(block, len(blocks) + d) for d, block in enumerate(blocks)]


def exchange_inside(rows, half_count):
    count = 2 * half_count
    groups = [list(range(half_count)), list(range(half_count, count))]
    parts = rows.reshape(half_count, -1, rows.shape[1])
    return lax.all_to_all(
        parts, "seq", split_axis=0, concat_axis=0, tiled=True, axis_index_groups=groups
    ).reshape(rows.shape)


def sum_over_head(block):
    count = lax.axis_size("head")
    if count & (count - 1):
        return lax.psum(block, "head")
    return block + sum(
        lax.ppermute(block, "head", [(i, i ^ d) for i in range(count)]) for d in range(1, count)
    )


def by_halves(queries, key_vectors, values, cotangent, cluster, block_pattern):
    count = lax.axis_size("seq")
    half_count = count // 2
    tokens, features = queries.shape
    width = features // half_count
    single = width // 2
    cluster_count, block_count, _ = block_pattern.shape
    half_len = half_count * tokens
    shape = (tokens, half_count, cluster_count, block_count)
    row_count = -(-tokens // (8 * LANES)) * 8
    stat_rows = -(-half_len // (8 * LANES)) * 8
    me = lax.axis_index("seq").astype(jnp.int32).reshape(1)
    packed_shape = half_array(half_count * 3 * tokens, width)
    packed = call(
        functools.partial(pack_kernel, half_count),
        packed_shape,
        [],
        [queries, values, cotangent],
        [
            pltpu.VMEM((3, tokens, features), jnp.bfloat16),
            pltpu.VMEM(packed_shape.shape, jnp.bfloat16),
            pltpu.SemaphoreType.DMA((3,)),
            pltpu.SemaphoreType.DMA((3 * half_count,)),
        ],
        in_hbm=3,
        out_hbm=True,
    )
    packed, key_vectors, cluster = lax.optimization_barrier((packed, key_vectors, cluster))
    packed = exchange_inside(packed, half_count)
    ids = lane_rows(cluster[:, 0], ID_ROWS).astype(jnp.bfloat16)
    key_float = key_vectors.astype(jnp.float32)
    square_sum = sum_over_head(lane_rows(jnp.sum(key_float * key_float, axis=1), row_count))
    feature_total = HEADS * HEAD_DIM
    key_rms = jnp.sqrt(square_sum / feature_total + EPSILON)
    sent = call(
        functools.partial(pack_keys_kernel, half_count),
        [half_array(tokens + ID_ROWS, width)] * half_count
        + [half_array(2 * tokens + ID_ROWS, single)] * half_count,
        [me],
        [queries, values, cotangent, key_vectors, key_rms, ids],
    )
    keys = swap_inside(sent[:half_count])
    cross = swap_across(sent[half_count:])
    pattern_rows = block_pattern.transpose(1, 0, 2).reshape(block_count, -1).astype(jnp.float32)
    pattern_rows = jnp.pad(pattern_rows, ((0, 0), (0, LANES - cluster_count * block_count)))
    wide = pltpu.VMEM((half_len, 2 * HEAD_DIM), jnp.bfloat16)
    slim = pltpu.VMEM((half_len, HEAD_DIM), jnp.bfloat16)
    sums = pltpu.VMEM((half_len, HEAD_DIM), jnp.float32)
    turned = pltpu.VMEM((HEAD_DIM, half_len), jnp.bfloat16)
    ids_column = pltpu.VMEM((half_len, 1), jnp.float32)
    block_flops = 12 * half_len * half_len * single
    inputs = [pattern_rows, packed] + cross + keys
    stats = call(
        functools.partial(stats_kernel, shape, stat_rows),
        jax.ShapeDtypeStruct((3 * stat_rows * (single // HEAD_DIM), LANES), jnp.float32),
        [me],
        inputs,
        [wide, wide, slim, slim, ids_column, ids_column],
        flops=block_flops // 3,
    )
    far_stats = swap(stats, half_count)
    firsts = call(
        functools.partial(first_kernel, shape),
        [half_array(4 * tokens, single)] * half_count
        + [half_array(2 * tokens, single)] * half_count
        + [
            half_array(2 * half_len, single),
            jax.ShapeDtypeStruct((2 * half_len, single), jnp.float32),
        ],
        [me],
        inputs + [stats],
        [wide, wide, slim, slim, wide, slim, ids_column, ids_column, slim, slim]
        + [sums, sums, sums, sums] + [turned] * 4,
        flops=block_flops + block_flops // 2,
    )
    *firsts, far_stats = lax.optimization_barrier((*firsts, far_stats))
    rest = firsts[half_count:]
    firsts = swap_inside(firsts[:half_count])
    results = call(
        functools.partial(second_head_kernel, shape, stat_rows),
        [half_array(4 * tokens, single)] * half_count
        + [half_array(2 * tokens, single)] * half_count,
        [me],
        inputs + [stats, far_stats] + rest[half_count:] + rest[:half_count],
        [wide, wide, slim, slim, wide, slim, ids_column, ids_column, slim, slim]
        + [sums, sums, slim, slim] + [turned] * 2,
        flops=block_flops,
    )
    far_sent, seconds = list(results[half_count:]), list(results[:half_count])
    near = half_count // 2
    far_parts = swap_across(far_sent)
    seconds, firsts, far_parts[-1] = lax.optimization_barrier((seconds, firsts, far_parts[-1]))
    seconds = swap_inside(seconds)
    inner = call(
        functools.partial(inner_kernel, half_count),
        jax.ShapeDtypeStruct((row_count, LANES), jnp.float32),
        [me],
        [key_vectors, key_rms] + far_parts + firsts + seconds,
    )
    inner = sum_over_head(inner)
    attended, query_grad, value_grad = call(
        functools.partial(final_kernel, half_count),
        [half_array(tokens, features)] * 3,
        [me],
        far_parts + firsts + seconds,
    )
    key_grad = call(
        functools.partial(key_kernel, half_count, feature_total),
        half_array(tokens, features),
        [me],
        [key_vectors, key_rms, inner] + far_parts + firsts + seconds,
    )
    return attended, query_grad, key_grad, value_grad


def per_device_any(queries, key_vectors, values, cotangent, cluster, block_pattern):
    count = lax.axis_size("seq")
    tokens, features = queries.shape
    cluster_count, block_count, _ = block_pattern.shape
    fits = (
        count % 2 == 0
        and count & (count - 1) == 0
        and features % (count * HEAD_DIM) == 0
        and tokens % ID_ROWS == 0
        and tokens * count % (2 * BLK) == 0
        and cluster_count * block_count <= LANES
    )
    chosen = by_halves if fits else per_device
    return chosen(queries, key_vectors, values, cotangent, cluster, block_pattern)


def solution(mesh):
    in_specs = (
        P("seq", "head"),
        P("seq", "head"),
        P("seq", "head"),
        P("seq", "head"),
        P("seq", None),
        P(),
    )
    out_specs = (P("seq", "head"), P("seq", "head"), P("seq", "head"), P("seq", "head"))
    return jax.shard_map(
        per_device_any, mesh=mesh, in_specs=in_specs, out_specs=out_specs, check_vma=False
    )
```

```python
import functools

import jax
import jax.numpy as jnp
from jax import lax
from jax.experimental import pallas as pl
from jax.experimental.pallas import tpu as pltpu
from jax.sharding import PartitionSpec as P

HEADS = 32
HEAD_DIM = 128
GS = 4
BLK = 128


NEG_FILL = -1e30
EPSILON = 1e-05
SCORE_SCALE = HEAD_DIM ** (-0.5)
EXPONENT_SCALE = SCORE_SCALE * 1.4426950408889634
LANES = 128
ID_ROWS = 16
QUERY_TILE = 256
STATS_TILE = 384
VMEM_BYTES = 32 << 20
PACK_VMEM_BYTES = 60 << 20


def contract_last(left_side, right_side):
    return lax.dot_general(
        left_side, right_side, (((1,), (1,)), ((), ())), preferred_element_type=jnp.float32
    )


def contract_first(left_side, right_side):
    return lax.dot_general(
        left_side, right_side, (((0,), (0,)), ((), ())), preferred_element_type=jnp.float32
    )


def visible_mask(pattern, query_pos, query_live, key_pos, key_live):
    pattern_rows = pattern[query_pos // BLK]
    allowed = jnp.take(pattern_rows, key_pos // BLK, axis=1) == 1
    causal = key_pos[None, :] <= query_pos[:, None]
    return allowed & causal & query_live[:, None] & key_live[None, :]


def cluster_ranks(table, cluster_index):
    source_count, tok_count = table.shape
    in_cluster = table == cluster_index
    token_iota = jnp.arange(tok_count, dtype=jnp.int32)
    earlier_table = (token_iota[:, None] < token_iota[None, :]).astype(jnp.bfloat16)
    earlier = jnp.dot(
        in_cluster.astype(jnp.bfloat16), earlier_table, preferred_element_type=jnp.float32
    ).astype(jnp.int32)
    global_pos = (
        jnp.arange(source_count, dtype=jnp.int32)[:, None] * tok_count + token_iota[None, :]
    )
    return (in_cluster, earlier, global_pos)


def code_positions(slot_code, global_pos, capacity):
    matches = slot_code[:, :, None] == jnp.arange(capacity, dtype=jnp.int32)[None, None, :]
    positions = jnp.sum(jnp.where(matches, global_pos[:, :, None], 0), axis=1)
    occupied = jnp.any(matches, axis=1)
    return (positions, occupied)


def rank_positions(table, cluster_index, capacity):
    in_cluster, earlier, global_pos = cluster_ranks(table, cluster_index)
    rank_code = jnp.where(in_cluster, earlier, -1)
    positions, occupied = code_positions(rank_code, global_pos, capacity)
    return (positions.reshape(-1), occupied.reshape(-1))


def dispatch_rows(outgoing):
    return lax.all_to_all(outgoing, "seq", split_axis=1, concat_axis=1, tiled=True)


def combine_rows(outgoing):
    return lax.all_to_all(outgoing, "seq", split_axis=1, concat_axis=1, tiled=True)


def forward_heads(query_slots, key_slots, value_slots, grad_slots, visible, score_scale):
    query_count, features = query_slots.shape
    key_count = key_slots.shape[0]
    head_count = features // HEAD_DIM
    attended = jnp.zeros((query_count, features), jnp.bfloat16)
    query_grad = jnp.zeros((query_count, features), jnp.bfloat16)
    side_result = jnp.zeros((2, key_count, features), jnp.float32)

    def one_head(head_index, running):
        attended_acc, query_acc, side_acc = running
        column_start = head_index * HEAD_DIM
        query_rows = lax.dynamic_slice_in_dim(query_slots, column_start, HEAD_DIM, 1)
        key_rows = lax.dynamic_slice_in_dim(key_slots, column_start, HEAD_DIM, 1)
        value_rows = lax.dynamic_slice_in_dim(value_slots, column_start, HEAD_DIM, 1)
        grad_rows = lax.dynamic_slice_in_dim(grad_slots, column_start, HEAD_DIM, 1)
        scores = jnp.where(visible, contract_last(query_rows, key_rows) * score_scale, NEG_FILL)
        row_max = jnp.max(scores, axis=1, keepdims=True)
        weights = jnp.where(visible, jnp.exp(scores - row_max), 0.0)
        row_total = jnp.maximum(jnp.sum(weights, axis=1, keepdims=True), 1.0)
        probabilities = weights / row_total
        prob_half = probabilities.astype(jnp.bfloat16)
        attended_head = jnp.dot(prob_half, value_rows, preferred_element_type=jnp.float32).astype(
            jnp.bfloat16
        )
        prob_grad = contract_last(grad_rows, value_rows)
        row_delta = jnp.sum(probabilities * prob_grad, axis=1, keepdims=True)
        score_grad = (probabilities * (prob_grad - row_delta)).astype(jnp.bfloat16)
        query_head = (
            jnp.dot(score_grad, key_rows, preferred_element_type=jnp.float32) * score_scale
        ).astype(jnp.bfloat16)
        attended_acc = lax.dynamic_update_slice_in_dim(attended_acc, attended_head, column_start, 1)
        query_acc = lax.dynamic_update_slice_in_dim(query_acc, query_head, column_start, 1)
        key_part = contract_first(score_grad, query_rows)
        value_part = contract_first(prob_half, grad_rows)
        side_acc = lax.dynamic_update_slice_in_dim(
            side_acc, jnp.stack([key_part, value_part]), column_start, 2
        )
        return (attended_acc, query_acc, side_acc)

    return lax.fori_loop(0, head_count, one_head, (attended, query_grad, side_result))


def per_device(queries, key_vectors, values, cotangent, cluster, block_pattern):
    seq_count = lax.axis_size("seq")
    tok_count, features = queries.shape
    slot_count = 2 * tok_count // seq_count
    group_count = seq_count // GS
    score_scale = HEAD_DIM ** (-0.5)
    my_index = lax.axis_index("seq")
    group_index = my_index // GS
    key_float = key_vectors.astype(jnp.float32)
    square_sum = lax.psum(jnp.sum(key_float * key_float, axis=1), "head")
    key_rms = jnp.sqrt(square_sum / (HEADS * HEAD_DIM) + EPSILON)[:, None]
    normed_float = key_float / key_rms
    normed = normed_float.astype(jnp.bfloat16)
    own_ids = cluster[:, 0]
    everyone = lax.all_gather(own_ids, "seq", axis=0, tiled=True)
    table = everyone.reshape(seq_count, tok_count)
    token_iota = jnp.arange(tok_count, dtype=jnp.int32)
    onehot_own = (own_ids[:, None] == jnp.arange(group_count, dtype=jnp.int32)[None, :]).astype(
        jnp.bfloat16
    )
    before_table = (token_iota[:, None] > token_iota[None, :]).astype(jnp.bfloat16)
    before = jnp.dot(before_table, onehot_own, preferred_element_type=jnp.float32)
    own_rank = jnp.sum(before * onehot_own.astype(jnp.float32), axis=1).astype(jnp.int32)
    pattern = lax.dynamic_index_in_dim(block_pattern, group_index, 0, keepdims=False)
    stacked_inputs = jnp.stack([queries, normed, values, cotangent])
    quarter = features // GS
    capacity = GS * slot_count
    split_inputs = stacked_inputs.reshape(4, tok_count, GS, quarter)
    placed = (
        jnp.zeros((4, group_count, capacity, GS, quarter), jnp.bfloat16)
        .at[:, own_ids, own_rank]
        .set(split_inputs)
    )
    outgoing = placed.transpose(0, 1, 3, 2, 4).reshape(4, seq_count * capacity, quarter)
    arrived = dispatch_rows(outgoing)
    flat_positions, flat_present = rank_positions(table, group_index, capacity)
    visible = visible_mask(pattern, flat_positions, flat_present, flat_positions, flat_present)
    attended, query_grad, both_terms = forward_heads(
        arrived[0], arrived[1], arrived[2], arrived[3], visible, score_scale
    )
    normed_grad = (both_terms[0] * score_scale).astype(jnp.bfloat16)
    value_slots = both_terms[1].astype(jnp.bfloat16)
    outgoing_back = jnp.stack([attended, query_grad, normed_grad, value_slots])
    returned = combine_rows(outgoing_back)
    arranged = returned.reshape(4, group_count, GS, capacity, quarter).transpose(1, 3, 0, 2, 4)
    home_rows = arranged[own_ids, own_rank].transpose(1, 0, 2, 3).reshape(4, tok_count, features)
    grad_float = home_rows[2].astype(jnp.float32)
    inner = lax.psum(jnp.sum(normed_float * grad_float, axis=1), "head")
    key_grad = (
        (grad_float - normed_float * (inner / (HEADS * HEAD_DIM))[:, None]) / key_rms
    ).astype(jnp.bfloat16)
    return (home_rows[0], home_rows[1], key_grad, home_rows[3])


def column_of(rows, first_row, count):
    turned = jnp.transpose(rows)
    pieces = []
    for start in range(0, count, LANES):
        place = first_row + start // LANES
        pieces.append(turned[: min(LANES, count - start), place : place + 1])
    return jnp.concatenate(pieces, axis=0)


def ids_of(ref, first_row, count):
    rows = ref[first_row : first_row + ID_ROWS, :LANES].astype(jnp.float32)
    return column_of(rows, 0, count)


def store_as_rows(out_ref, first_row, column):
    count = column.shape[0]
    for start in range(0, count, LANES):
        size = min(LANES, count - start)
        diagonal = lax.broadcasted_iota(jnp.int32, (size, LANES), 0) == lax.broadcasted_iota(
            jnp.int32, (size, LANES), 1
        )
        spread = jnp.where(diagonal, column[start : start + size], 0.0)
        row = first_row + start // LANES
        out_ref[row : row + 1, :] = jnp.sum(spread, axis=0, keepdims=True)


def block_rows(index, size):
    return pl.ds(pl.multiple_of(index * size, 16), size)


def pack_kernel(half_count, query_ref, value_ref, grad_ref, out_ref, held, sorted_rows, in_sems, out_sems):
    tokens, features = query_ref.shape
    width = features // half_count
    arrivals = [
        pltpu.make_async_copy(source_ref, held.at[place], in_sems.at[place])
        for place, source_ref in enumerate((query_ref, value_ref, grad_ref))
    ]
    for arrival in arrivals:
        arrival.start()
    copies = []
    for place, arrival in enumerate(arrivals):
        arrival.wait()
        for owner in range(half_count):
            rows = pl.ds((owner * 3 + place) * tokens, tokens)
            sorted_rows[rows, :] = held[place, :, owner * width : (owner + 1) * width]
            copy = pltpu.make_async_copy(
                sorted_rows.at[rows, :], out_ref.at[rows, :], out_sems.at[place * half_count + owner]
            )
            copy.start()
            copies.append(copy)
    for copy in copies:
        copy.wait()


def pack_keys_kernel(
    half_count, me_ref, query_ref, value_ref, grad_ref, key_ref, rms_ref, ids_ref, *out_refs
):
    tokens, features = key_ref.shape
    width = features // half_count
    single = width // 2
    is_high = me_ref[0] >= half_count
    inside = me_ref[0] & (half_count - 1)
    key_refs, cross_refs = out_refs[:half_count], out_refs[half_count:]
    rms = column_of(rms_ref[...], 0, tokens)

    def normed_columns(first, size):
        return (key_ref[:, pl.ds(first, size)].astype(jnp.float32) / rms).astype(jnp.bfloat16)

    for distance in range(half_count):
        first = pl.multiple_of((inside ^ distance) * width, LANES)
        cross_ref = cross_refs[distance]
        key_refs[distance][:tokens, :] = normed_columns(first, width)
        key_refs[distance][tokens:, :LANES] = ids_ref[...]
        key_refs[distance][tokens:, LANES:] = jnp.zeros((ID_ROWS, width - LANES), jnp.bfloat16)
        cross_ref[2 * tokens :, :LANES] = ids_ref[...]
        if single > LANES:
            cross_ref[2 * tokens :, LANES:] = jnp.zeros((ID_ROWS, single - LANES), jnp.bfloat16)

        @pl.when(is_high)
        def send_down():
            second = pl.multiple_of(first + single, LANES)
            cross_ref[:tokens, :] = query_ref[:, pl.ds(second, single)]
            cross_ref[tokens : 2 * tokens, :] = grad_ref[:, pl.ds(second, single)]

        @pl.when(jnp.logical_not(is_high))
        def send_up():
            cross_ref[:tokens, :] = normed_columns(first, single)
            cross_ref[tokens : 2 * tokens, :] = value_ref[:, pl.ds(first, single)]


class Slots:
    def __init__(self, shape, me_ref, pattern_ref, packed_ref, key_refs, cross_refs):
        self.tokens, self.half_count, self.cluster_count, self.block_count = shape
        self.half_len = self.tokens * self.half_count
        self.half_blocks = self.half_len // BLK
        self.is_high = me_ref[0] >= self.half_count
        self.inside = me_ref[0] & (self.half_count - 1)
        self.pattern_ref, self.packed_ref = pattern_ref, packed_ref
        self.key_refs, self.cross_refs = key_refs, cross_refs
        lane = lax.broadcasted_iota(jnp.int32, (1, LANES), 1)
        lane_cluster = jnp.zeros((1, LANES), jnp.int32)
        for index in range(1, self.cluster_count + 1):
            lane_cluster = lane_cluster + (lane >= index * self.block_count).astype(jnp.int32)
        self.lane_block = lane - lane_cluster * self.block_count
        self.lane_cluster = lane_cluster.astype(jnp.float32)

    def own_ids(self, ids_all):
        for distance in range(self.half_count):
            ids_all[block_rows(self.inside ^ distance, self.tokens), :] = ids_of(
                self.key_refs[distance], self.tokens, self.tokens
            )

    def cross_ids(self, ids_all):
        for distance in range(self.half_count):
            ids_all[block_rows(self.inside ^ distance, self.tokens), :] = ids_of(
                self.cross_refs[distance], 2 * self.tokens, self.tokens
            )

    def query_features(self, ids_all, target, high):
        for block in range(self.half_blocks):
            rows = slice(block * BLK, (block + 1) * BLK)
            place = block + high * self.half_blocks
            allowed = self.pattern_ref[pl.ds(place, 1), :] == 1.0
            same = ids_all[rows, :] == self.lane_cluster
            target[rows, HEAD_DIM:] = jnp.where(same & allowed, 0.0, NEG_FILL).astype(jnp.bfloat16)

    def key_features(self, ids_all, target, high):
        for block in range(self.half_blocks):
            rows = slice(block * BLK, (block + 1) * BLK)
            place = block + high * self.half_blocks
            same = ids_all[rows, :] == self.lane_cluster
            target[rows, HEAD_DIM:] = jnp.where(same & (self.lane_block == place), 1.0, 0.0).astype(
                jnp.bfloat16
            )

    def own(self, column, query_all, key_all, value_all, grad_all):
        columns = slice(column, column + HEAD_DIM)
        stride = 3 * self.tokens
        for source in range(self.half_count):
            rows = slice(source * self.tokens, (source + 1) * self.tokens)
            for place, target in enumerate((query_all, value_all, grad_all)):
                first = source * stride + place * self.tokens
                target[rows, :HEAD_DIM] = self.packed_ref[first : first + self.tokens, columns]
        for distance in range(self.half_count):
            rows = block_rows(self.inside ^ distance, self.tokens)
            key_all[rows, :HEAD_DIM] = self.key_refs[distance][: self.tokens, columns]

    def cross(self, column, first_all, second_all):
        columns = slice(column, column + HEAD_DIM)
        for distance in range(self.half_count):
            rows = block_rows(self.inside ^ distance, self.tokens)
            cross_ref = self.cross_refs[distance]
            first_all[rows, :HEAD_DIM] = cross_ref[: self.tokens, columns]
            second_all[rows, :] = cross_ref[self.tokens : 2 * self.tokens, columns]


class Keys:
    def __init__(self, key, value, key_turned=None, value_turned=None):
        self.key, self.value = key, value
        self.key_turned, self.value_turned = key_turned, value_turned

    def turn(self):
        self.key_turned[...] = jnp.transpose(self.key[:, :HEAD_DIM])
        self.value_turned[...] = jnp.transpose(self.value[...])


def tile_scores(query_tile, keys, limit, first):
    scores = contract_last(keys.key[:limit, :], query_tile)
    if first is not None:
        key_index = lax.broadcasted_iota(jnp.int32, scores.shape, 0)
        query_index = lax.broadcasted_iota(jnp.int32, scores.shape, 1) + first
        scores = jnp.where(key_index <= query_index, scores, NEG_FILL)
    return scores


def tile_stats(scores, prob_grads):
    row_max = functools.reduce(
        jnp.maximum, [jnp.max(part, axis=0, keepdims=True) for part in scores]
    )
    weights = [jnp.exp2((part - row_max) * EXPONENT_SCALE) for part in scores]
    row_total = sum(jnp.sum(part, axis=0, keepdims=True) for part in weights)
    row_delta = sum(
        jnp.sum(part * grad, axis=0, keepdims=True) for part, grad in zip(weights, prob_grads)
    )
    return weights, row_max, row_total, row_delta


def tile_products(query_tile, grad_tile, pieces):
    scores = [tile_scores(query_tile, *piece) for piece in pieces]
    return scores, [contract_last(keys.value[:limit, :], grad_tile) for keys, limit, _ in pieces]


def all_tiles(query_all, grad_all, half_len, pieces_of, sums, stats_of, keep, add=False):
    tiles = own_tiles(half_len)
    ready = None
    for index, (first, rows, limit) in enumerate(tiles):
        now = ready or tile_products(query_all[rows, :], grad_all[rows, :], pieces_of(first, limit))
        ready = None
        if index + 1 < len(tiles):
            later, later_rows, later_limit = tiles[index + 1]
            ready = tile_products(
                query_all[later_rows, :], grad_all[later_rows, :], pieces_of(later, later_limit)
            )
        keep(
            rows,
            *tile_backward(
                query_all[rows, :],
                grad_all[rows, :],
                pieces_of(first, limit),
                sums,
                stats_of(first, limit - first) if stats_of else None,
                first == 0 and not add,
                *now,
            ),
        )


def tile_backward(query_tile, grad_tile, pieces, sums, stats, is_first, scores, prob_grads):
    if stats is None:
        weights, _, row_total, row_delta = tile_stats(scores, prob_grads)
        inverse = 1.0 / jnp.maximum(row_total, 1.0)
        row_delta = row_delta * inverse
    else:
        row_max, inverse, row_delta = stats
        weights = [jnp.exp2((part - row_max) * EXPONENT_SCALE) for part in scores]
    attended, query_grad = 0.0, 0.0
    for index, (keys, limit, first) in enumerate(pieces):
        probabilities = weights[index] * inverse
        prob_half = probabilities.astype(jnp.bfloat16)
        score_grad = (probabilities * (prob_grads[index] - row_delta)).astype(jnp.bfloat16)
        attended += jnp.dot(
            keys.value_turned[:, :limit], prob_half, preferred_element_type=jnp.float32
        )
        query_grad += jnp.dot(
            keys.key_turned[:, :limit], score_grad, preferred_element_type=jnp.float32
        )
        key_part = jnp.dot(
            score_grad, query_tile[:, :HEAD_DIM], preferred_element_type=jnp.float32
        )
        value_part = jnp.dot(prob_half, grad_tile, preferred_element_type=jnp.float32)
        key_sum, value_sum = sums[index]
        fresh = 0 if is_first else (limit if first is None else first)
        if fresh:
            key_sum[:fresh, :] += key_part[:fresh]
            value_sum[:fresh, :] += value_part[:fresh]
        if fresh < limit:
            key_sum[fresh:limit, :] = key_part[fresh:]
            value_sum[fresh:limit, :] = value_part[fresh:]
    return (
        jnp.transpose(attended).astype(jnp.bfloat16),
        jnp.transpose(query_grad * SCORE_SCALE).astype(jnp.bfloat16),
    )


def own_tiles(half_len, tile=QUERY_TILE):
    tile = tile if half_len % tile == 0 else BLK
    return [(first, slice(first, first + tile), first + tile) for first in range(0, half_len, tile)]


def note_stats(out_ref, stat_rows, head, first, found):
    for place, column in enumerate(found[1:]):
        store_as_rows(out_ref, (3 * head + place) * stat_rows + first // LANES, column)


def stats_kernel(shape, stat_rows, me_ref, pattern_ref, packed_ref, *refs):
    half_count = shape[1]
    cross_refs, key_refs = refs[:half_count], refs[half_count : 2 * half_count]
    out_ref, query_all, key_all, value_all, grad_all, ids, other_ids = refs[2 * half_count :]
    slots = Slots(shape, me_ref, pattern_ref, packed_ref, key_refs, cross_refs)
    single = packed_ref.shape[1] // 2
    out_ref[...] = jnp.zeros_like(out_ref)
    slots.own_ids(ids)
    slots.key_features(ids, key_all, slots.is_high.astype(jnp.int32))

    @pl.when(slots.is_high)
    def _():
        slots.query_features(ids, query_all, 1)

    @pl.when(jnp.logical_not(slots.is_high))
    def _():
        slots.cross_ids(other_ids)
        slots.query_features(other_ids, query_all, 1)

    for head in range(single // HEAD_DIM):
        column = head * HEAD_DIM
        slots.own(single + column, query_all, key_all, value_all, grad_all)

        def note(first, rows, limit, causal_from):
            scores = tile_scores(query_all[rows, :], Keys(key_all, value_all), limit, causal_from)
            prob_grad = contract_last(value_all[:limit, :], grad_all[rows, :])
            for place, found in enumerate(tile_stats([scores], [prob_grad])[1:]):
                row = (3 * head + place) * stat_rows + first // LANES
                for start in range(0, found.shape[1], LANES):
                    out_ref[row + start // LANES : row + start // LANES + 1, :] = found[
                        :, start : start + LANES
                    ]

        @pl.when(slots.is_high)
        def _():
            for first, rows, limit in own_tiles(slots.half_len, STATS_TILE):
                note(first, rows, limit, first)

        @pl.when(jnp.logical_not(slots.is_high))
        def _():
            slots.cross(column, query_all, grad_all)
            for first, rows, _ in own_tiles(slots.half_len, STATS_TILE):
                note(first, rows, slots.half_len, None)


def store_own(slots, result_refs, column, attended, query_grad, value_sum, key_sum):
    tokens = slots.tokens
    columns = slice(column, column + HEAD_DIM)
    for distance, target in enumerate(result_refs):
        rows = block_rows(slots.inside ^ distance, tokens)
        target[:tokens, columns] = attended[rows, :]
        target[tokens : 2 * tokens, columns] = query_grad[rows, :]
        target[2 * tokens : 3 * tokens, columns] = value_sum[rows, :].astype(jnp.bfloat16)
        target[3 * tokens :, columns] = (key_sum[rows, :] * SCORE_SCALE).astype(jnp.bfloat16)


def first_kernel(shape, me_ref, pattern_ref, packed_ref, *refs):
    half_count = shape[1]
    cross_refs, key_refs = refs[:half_count], refs[half_count : 2 * half_count]
    refs = refs[2 * half_count + 1 :]
    result_refs, cross_out_refs = refs[:half_count], refs[half_count : 2 * half_count]
    second_ref, sums_ref = refs[2 * half_count : 2 * half_count + 2]
    (query_all, key_all, value_all, grad_all, other_key, other_value, ids, other_ids, attended,
     query_grad, key_sum, value_sum, other_key_sum, other_value_sum, *turned) = refs[
        2 * half_count + 2 :
    ]
    own, other = Keys(key_all, value_all, *turned[:2]), Keys(other_key, other_value, *turned[2:])
    slots = Slots(shape, me_ref, pattern_ref, packed_ref, key_refs, cross_refs)
    single = packed_ref.shape[1] // 2
    half_len = slots.half_len
    high = slots.is_high.astype(jnp.int32)
    slots.own_ids(ids)
    slots.key_features(ids, key_all, high)
    slots.query_features(ids, query_all, high)

    def run(others, other_sums, attended_out, query_grad_out, key_out, value_out):
        def keep(rows, attended_tile, query_grad_tile):
            attended_out[rows, :], query_grad_out[rows, :] = attended_tile, query_grad_tile

        all_tiles(
            query_all,
            grad_all,
            half_len,
            lambda first, limit: others + [(own, limit, first)],
            other_sums + [(key_out, value_out)],
            None,
            keep,
        )

    @pl.when(slots.is_high)
    def _():
        slots.cross_ids(other_ids)
        slots.key_features(other_ids, other_key, 0)

    for head in range(single // HEAD_DIM):
        column = head * HEAD_DIM
        columns = slice(column, column + HEAD_DIM)
        slots.own(column, query_all, key_all, value_all, grad_all)
        own.turn()

        @pl.when(slots.is_high)
        def _():
            slots.cross(column, other_key, other_value)
            other.turn()
            run(
                [(other, half_len, None)],
                [(other_key_sum, other_value_sum)],
                attended, query_grad, key_sum, value_sum,
            )
            for distance in range(half_count):
                rows = block_rows(slots.inside ^ distance, slots.tokens)
                target = cross_out_refs[distance]
                target[: slots.tokens, columns] = (other_key_sum[rows, :] * SCORE_SCALE).astype(
                    jnp.bfloat16
                )
                target[slots.tokens :, columns] = other_value_sum[rows, :].astype(jnp.bfloat16)

        @pl.when(jnp.logical_not(slots.is_high))
        def _():
            run([], [], attended, query_grad, key_sum, value_sum)

        store_own(slots, result_refs, column, attended, query_grad, value_sum, key_sum)

        @pl.when(jnp.logical_not(slots.is_high))
        def _():
            slots.own(single + column, query_all, key_all, value_all, grad_all)
            own.turn()
            run(
                [], [],
                second_ref.at[:half_len, columns],
                second_ref.at[half_len:, columns],
                sums_ref.at[:half_len, columns],
                sums_ref.at[half_len:, columns],
            )


def joint_rows(stat_rows, head, own_stats_ref, far_stats_ref):
    (own_max, own_total, own_delta), (far_max, far_total, far_delta) = [
        [
            ref[(3 * head + place) * stat_rows : (3 * head + place + 1) * stat_rows, :]
            for place in range(3)
        ]
        for ref in (own_stats_ref, far_stats_ref)
    ]
    row_max = jnp.maximum(own_max, far_max)
    own_part = jnp.exp2((own_max - row_max) * EXPONENT_SCALE)
    far_part = jnp.exp2((far_max - row_max) * EXPONENT_SCALE)
    inverse = 1.0 / jnp.maximum(own_total * own_part + far_total * far_part, 1.0)
    return row_max, inverse, (own_delta * own_part + far_delta * far_part) * inverse


def second_head_kernel(shape, stat_rows, me_ref, pattern_ref, packed_ref, *refs):
    half_count = shape[1]
    cross_refs, key_refs = refs[:half_count], refs[half_count : 2 * half_count]
    own_stats_ref, far_stats_ref, early_ref, sums_ref = refs[2 * half_count : 2 * half_count + 4]
    refs = refs[2 * half_count + 4 :]
    first_cross_refs, result_refs, cross_out_refs = [
        refs[place * half_count : (place + 1) * half_count] for place in range(3)
    ]
    (query_all, key_all, value_all, grad_all, other_query, other_grad, ids, other_ids, attended,
     query_grad, key_sum, value_sum, other_attended, other_query_grad, *turned) = refs[
        3 * half_count :
    ]
    own = Keys(key_all, value_all, *turned)
    slots = Slots(shape, me_ref, pattern_ref, packed_ref, key_refs, cross_refs)
    single = packed_ref.shape[1] // 2
    half_len, tokens = slots.half_len, slots.tokens
    slots.own_ids(ids)
    slots.key_features(ids, key_all, slots.is_high.astype(jnp.int32))

    @pl.when(slots.is_high)
    def _():
        slots.query_features(ids, query_all, 1)
        for distance in range(half_count):
            cross_out_refs[distance][...] = first_cross_refs[distance][...]

    @pl.when(jnp.logical_not(slots.is_high))
    def _():
        slots.cross_ids(other_ids)
        slots.query_features(other_ids, other_query, 1)

    for head in range(single // HEAD_DIM):
        column = head * HEAD_DIM
        columns = slice(column, column + HEAD_DIM)
        slots.own(single + column, query_all, key_all, value_all, grad_all)
        own.turn()
        joint_table = joint_rows(stat_rows, head, own_stats_ref, far_stats_ref)

        def joint_stats(first, size):
            places = range(first // LANES, (first + size) // LANES)
            return [
                jnp.concatenate([rows[place : place + 1, :] for place in places], axis=1)
                for rows in joint_table
            ]

        @pl.when(slots.is_high)
        def _():
            def keep(rows, attended_tile, query_grad_tile):
                attended[rows, :], query_grad[rows, :] = attended_tile, query_grad_tile

            all_tiles(
                query_all,
                grad_all,
                half_len,
                lambda first, limit: [(own, limit, first)],
                [(key_sum, value_sum)],
                joint_stats,
                keep,
            )

        @pl.when(jnp.logical_not(slots.is_high))
        def _():
            slots.cross(column, other_query, other_grad)
            attended[...] = early_ref[:half_len, columns]
            query_grad[...] = early_ref[half_len:, columns]
            key_sum[...] = sums_ref[:half_len, columns]
            value_sum[...] = sums_ref[half_len:, columns]

            def keep(rows, attended_tile, query_grad_tile):
                other_attended[rows, :], other_query_grad[rows, :] = attended_tile, query_grad_tile

            all_tiles(
                other_query,
                other_grad,
                half_len,
                lambda first, limit: [(own, half_len, None)],
                [(key_sum, value_sum)],
                joint_stats,
                keep,
                add=True,
            )
            for distance in range(half_count):
                rows = block_rows(slots.inside ^ distance, tokens)
                target = cross_out_refs[distance]
                target[:tokens, columns] = other_attended[rows, :]
                target[tokens:, columns] = other_query_grad[rows, :]

        store_own(slots, result_refs, column, attended, query_grad, value_sum, key_sum)


def normed_grad_of(half_count, me_ref, first_ref, second_ref, cross_ref):
    tokens = second_ref.shape[0] // 4
    is_low = me_ref[0] < half_count
    far = jnp.where(is_low, cross_ref[:tokens, :].astype(jnp.float32), 0.0)
    first_float = first_ref[3 * tokens :, :].astype(jnp.float32) + far
    second_float = second_ref[3 * tokens :, :].astype(jnp.float32)
    return jnp.concatenate([first_float, second_float], axis=1)


def inner_kernel(half_count, me_ref, key_ref, rms_ref, *refs):
    cross_refs, first_refs, second_refs = [
        refs[place * half_count : (place + 1) * half_count] for place in range(3)
    ]
    out_ref = refs[3 * half_count]
    tokens, features = key_ref.shape
    width = features // half_count
    inside = me_ref[0] & (half_count - 1)
    total = jnp.zeros((tokens, width), jnp.float32)
    for distance in range(half_count):
        owner = inside ^ distance
        start = pl.multiple_of(owner * width, LANES)
        key_float = key_ref[:, pl.ds(start, width)].astype(jnp.float32)
        total = total + key_float * normed_grad_of(
            half_count, me_ref, first_refs[distance], second_refs[distance], cross_refs[distance]
        )
    column = jnp.sum(total, axis=1, keepdims=True) / column_of(rms_ref[...], 0, tokens)
    out_ref[...] = jnp.zeros_like(out_ref)
    store_as_rows(out_ref, 0, column)


def key_kernel(half_count, feature_total, me_ref, key_ref, rms_ref, inner_ref, *refs):
    cross_refs, first_refs, second_refs = [
        refs[place * half_count : (place + 1) * half_count] for place in range(3)
    ]
    key_out_ref = refs[3 * half_count]
    tokens, features = key_ref.shape
    width = features // half_count
    inside = me_ref[0] & (half_count - 1)
    rms = column_of(rms_ref[...], 0, tokens)
    inner = column_of(inner_ref[...], 0, tokens) / feature_total
    for distance in range(half_count):
        columns = pl.ds(pl.multiple_of((inside ^ distance) * width, LANES), width)
        normed_float = key_ref[:, columns].astype(jnp.float32) / rms
        grad_float = normed_grad_of(
            half_count, me_ref, first_refs[distance], second_refs[distance], cross_refs[distance]
        )
        key_out_ref[:, columns] = ((grad_float - normed_float * inner) / rms).astype(jnp.bfloat16)


def final_kernel(half_count, me_ref, *refs):
    cross_refs, first_refs, second_refs = [
        refs[place * half_count : (place + 1) * half_count] for place in range(3)
    ]
    attended_ref, query_ref, value_ref = refs[3 * half_count :]
    tokens, features = attended_ref.shape
    width = features // half_count
    single = width // 2
    is_high = me_ref[0] >= half_count
    inside = me_ref[0] & (half_count - 1)
    for distance in range(half_count):
        start = pl.multiple_of((inside ^ distance) * width, LANES)
        first = pl.ds(start, single)
        second = pl.ds(pl.multiple_of(start + single, LANES), single)
        cross_ref = cross_refs[distance]

        def block(refs, place):
            return refs[distance][place * tokens : (place + 1) * tokens, :]

        def joined(refs, place, far):
            whole = block(refs, place).astype(jnp.float32) + cross_ref[
                far * tokens : (far + 1) * tokens, :
            ].astype(jnp.float32)
            return whole.astype(jnp.bfloat16)

        attended_ref[:, first] = block(first_refs, 0)
        query_ref[:, first] = block(first_refs, 1)
        value_ref[:, second] = block(second_refs, 2)

        @pl.when(is_high)
        def _():
            attended_ref[:, second] = joined(second_refs, 0, 0)
            query_ref[:, second] = joined(second_refs, 1, 1)
            value_ref[:, first] = block(first_refs, 2)

        @pl.when(jnp.logical_not(is_high))
        def _():
            attended_ref[:, second] = block(second_refs, 0)
            query_ref[:, second] = block(second_refs, 1)
            value_ref[:, first] = joined(first_refs, 2, 1)


def lane_rows(vector, row_count):
    return jnp.pad(vector, (0, row_count * LANES - vector.shape[0])).reshape(row_count, LANES)


def half_array(rows, columns):
    return jax.ShapeDtypeStruct((rows, columns), jnp.bfloat16)


def call(kernel, out_shapes, scalars, arrays, scratch=(), in_hbm=0, out_hbm=False, flops=0):
    vmem, anywhere = pl.BlockSpec(memory_space=pltpu.VMEM), pl.BlockSpec(memory_space=pl.ANY)
    return pl.pallas_call(
        kernel,
        out_shape=out_shapes,
        in_specs=[pl.BlockSpec(memory_space=pltpu.SMEM)] * len(scalars)
        + [anywhere] * in_hbm
        + [vmem] * (len(arrays) - in_hbm),
        out_specs=jax.tree.map(lambda shape: anywhere if out_hbm else vmem, out_shapes),
        scratch_shapes=list(scratch),
        compiler_params=pltpu.CompilerParams(vmem_limit_bytes=PACK_VMEM_BYTES if in_hbm else VMEM_BYTES),
        cost_estimate=pl.CostEstimate(flops=flops, bytes_accessed=0, transcendentals=0) if flops else None,
    )(*scalars, *arrays)


def swap(block, distance):
    count = lax.axis_size("seq")
    return lax.ppermute(block, "seq", [(i, i ^ distance) for i in range(count)])


def swap_inside(blocks):
    return [blocks[0]] + [swap(block, d) for d, block in enumerate(blocks) if d]


def swap_across(blocks):
    return [swap(block, len(blocks) + d) for d, block in enumerate(blocks)]


def exchange_inside(rows, half_count):
    count = 2 * half_count
    groups = [list(range(half_count)), list(range(half_count, count))]
    parts = rows.reshape(half_count, -1, rows.shape[1])
    return lax.all_to_all(
        parts, "seq", split_axis=0, concat_axis=0, tiled=True, axis_index_groups=groups
    ).reshape(rows.shape)


def sum_over_head(block):
    count = lax.axis_size("head")
    if count & (count - 1):
        return lax.psum(block, "head")
    return block + sum(
        lax.ppermute(block, "head", [(i, i ^ d) for i in range(count)]) for d in range(1, count)
    )


def by_halves(queries, key_vectors, values, cotangent, cluster, block_pattern):
    count = lax.axis_size("seq")
    half_count = count // 2
    tokens, features = queries.shape
    width = features // half_count
    single = width // 2
    cluster_count, block_count, _ = block_pattern.shape
    half_len = half_count * tokens
    shape = (tokens, half_count, cluster_count, block_count)
    row_count = -(-tokens // (8 * LANES)) * 8
    stat_rows = -(-half_len // (8 * LANES)) * 8
    me = lax.axis_index("seq").astype(jnp.int32).reshape(1)
    packed_shape = half_array(half_count * 3 * tokens, width)
    packed = call(
        functools.partial(pack_kernel, half_count),
        packed_shape,
        [],
        [queries, values, cotangent],
        [
            pltpu.VMEM((3, tokens, features), jnp.bfloat16),
            pltpu.VMEM(packed_shape.shape, jnp.bfloat16),
            pltpu.SemaphoreType.DMA((3,)),
            pltpu.SemaphoreType.DMA((3 * half_count,)),
        ],
        in_hbm=3,
        out_hbm=True,
    )
    packed, key_vectors, cluster = lax.optimization_barrier((packed, key_vectors, cluster))
    packed = exchange_inside(packed, half_count)
    ids = lane_rows(cluster[:, 0], ID_ROWS).astype(jnp.bfloat16)
    key_float = key_vectors.astype(jnp.float32)
    square_sum = sum_over_head(lane_rows(jnp.sum(key_float * key_float, axis=1), row_count))
    feature_total = HEADS * HEAD_DIM
    key_rms = jnp.sqrt(square_sum / feature_total + EPSILON)
    sent = call(
        functools.partial(pack_keys_kernel, half_count),
        [half_array(tokens + ID_ROWS, width)] * half_count
        + [half_array(2 * tokens + ID_ROWS, single)] * half_count,
        [me],
        [queries, values, cotangent, key_vectors, key_rms, ids],
    )
    cross = swap_across(sent[half_count:])
    key_sent = list(sent[:half_count])
    key_sent[1], cross[0] = lax.optimization_barrier((key_sent[1], cross[0]))
    keys = swap_inside(key_sent)
    pattern_rows = block_pattern.transpose(1, 0, 2).reshape(block_count, -1).astype(jnp.float32)
    pattern_rows = jnp.pad(pattern_rows, ((0, 0), (0, LANES - cluster_count * block_count)))
    wide = pltpu.VMEM((half_len, 2 * HEAD_DIM), jnp.bfloat16)
    slim = pltpu.VMEM((half_len, HEAD_DIM), jnp.bfloat16)
    sums = pltpu.VMEM((half_len, HEAD_DIM), jnp.float32)
    turned = pltpu.VMEM((HEAD_DIM, half_len), jnp.bfloat16)
    ids_column = pltpu.VMEM((half_len, 1), jnp.float32)
    block_flops = 12 * half_len * half_len * single
    inputs = [pattern_rows, packed] + cross + keys
    stats = call(
        functools.partial(stats_kernel, shape, stat_rows),
        jax.ShapeDtypeStruct((3 * stat_rows * (single // HEAD_DIM), LANES), jnp.float32),
        [me],
        inputs,
        [wide, wide, slim, slim, ids_column, ids_column],
        flops=block_flops // 3,
    )
    far_stats = swap(stats, half_count)
    firsts = call(
        functools.partial(first_kernel, shape),
        [half_array(4 * tokens, single)] * half_count
        + [half_array(2 * tokens, single)] * half_count
        + [
            half_array(2 * half_len, single),
            jax.ShapeDtypeStruct((2 * half_len, single), jnp.float32),
        ],
        [me],
        inputs + [stats],
        [wide, wide, slim, slim, wide, slim, ids_column, ids_column, slim, slim]
        + [sums, sums, sums, sums] + [turned] * 4,
        flops=block_flops + block_flops // 2,
    )
    *firsts, far_stats = lax.optimization_barrier((*firsts, far_stats))
    rest = firsts[half_count:]
    firsts = swap_inside(firsts[:half_count])
    results = call(
        functools.partial(second_head_kernel, shape, stat_rows),
        [half_array(4 * tokens, single)] * half_count
        + [half_array(2 * tokens, single)] * half_count,
        [me],
        inputs + [stats, far_stats] + rest[half_count:] + rest[:half_count],
        [wide, wide, slim, slim, wide, slim, ids_column, ids_column, slim, slim]
        + [sums, sums, slim, slim] + [turned] * 2,
        flops=block_flops,
    )
    far_sent, seconds = list(results[half_count:]), list(results[:half_count])
    near = half_count // 2
    far_parts = swap_across(far_sent)
    seconds, firsts, far_parts[-1] = lax.optimization_barrier((seconds, firsts, far_parts[-1]))
    seconds = swap_inside(seconds)
    inner = call(
        functools.partial(inner_kernel, half_count),
        jax.ShapeDtypeStruct((row_count, LANES), jnp.float32),
        [me],
        [key_vectors, key_rms] + far_parts + firsts + seconds,
    )
    inner = sum_over_head(inner)
    attended, query_grad, value_grad = call(
        functools.partial(final_kernel, half_count),
        [half_array(tokens, features)] * 3,
        [me],
        far_parts + firsts + seconds,
    )
    key_grad = call(
        functools.partial(key_kernel, half_count, feature_total),
        half_array(tokens, features),
        [me],
        [key_vectors, key_rms, inner] + far_parts + firsts + seconds,
    )
    return attended, query_grad, key_grad, value_grad


def per_device_any(queries, key_vectors, values, cotangent, cluster, block_pattern):
    count = lax.axis_size("seq")
    tokens, features = queries.shape
    cluster_count, block_count, _ = block_pattern.shape
    fits = (
        count % 2 == 0
        and count & (count - 1) == 0
        and features % (count * HEAD_DIM) == 0
        and tokens % ID_ROWS == 0
        and tokens * count % (2 * BLK) == 0
        and cluster_count * block_count <= LANES
    )
    chosen = by_halves if fits else per_device
    return chosen(queries, key_vectors, values, cotangent, cluster, block_pattern)


def solution(mesh):
    in_specs = (
        P("seq", "head"),
        P("seq", "head"),
        P("seq", "head"),
        P("seq", "head"),
        P("seq", None),
        P(),
    )
    out_specs = (P("seq", "head"), P("seq", "head"), P("seq", "head"), P("seq", "head"))
    return jax.shard_map(
        per_device_any, mesh=mesh, in_specs=in_specs, out_specs=out_specs, check_vma=False
    )
```

```python
import functools

import jax
import jax.numpy as jnp
from jax import lax
from jax.experimental import pallas as pl
from jax.experimental.pallas import tpu as pltpu
from jax.sharding import PartitionSpec as P

HEADS = 32
HEAD_DIM = 128
GS = 4
BLK = 128


NEG_FILL = -1e30
EPSILON = 1e-05
SCORE_SCALE = HEAD_DIM ** (-0.5)
EXPONENT_SCALE = SCORE_SCALE * 1.4426950408889634
LANES = 128
ID_ROWS = 16
QUERY_TILE = 256
STATS_TILE = 384
VMEM_BYTES = 32 << 20
PACK_VMEM_BYTES = 60 << 20


def contract_last(left_side, right_side):
    return lax.dot_general(
        left_side, right_side, (((1,), (1,)), ((), ())), preferred_element_type=jnp.float32
    )


def contract_first(left_side, right_side):
    return lax.dot_general(
        left_side, right_side, (((0,), (0,)), ((), ())), preferred_element_type=jnp.float32
    )


def visible_mask(pattern, query_pos, query_live, key_pos, key_live):
    pattern_rows = pattern[query_pos // BLK]
    allowed = jnp.take(pattern_rows, key_pos // BLK, axis=1) == 1
    causal = key_pos[None, :] <= query_pos[:, None]
    return allowed & causal & query_live[:, None] & key_live[None, :]


def cluster_ranks(table, cluster_index):
    source_count, tok_count = table.shape
    in_cluster = table == cluster_index
    token_iota = jnp.arange(tok_count, dtype=jnp.int32)
    earlier_table = (token_iota[:, None] < token_iota[None, :]).astype(jnp.bfloat16)
    earlier = jnp.dot(
        in_cluster.astype(jnp.bfloat16), earlier_table, preferred_element_type=jnp.float32
    ).astype(jnp.int32)
    global_pos = (
        jnp.arange(source_count, dtype=jnp.int32)[:, None] * tok_count + token_iota[None, :]
    )
    return (in_cluster, earlier, global_pos)


def code_positions(slot_code, global_pos, capacity):
    matches = slot_code[:, :, None] == jnp.arange(capacity, dtype=jnp.int32)[None, None, :]
    positions = jnp.sum(jnp.where(matches, global_pos[:, :, None], 0), axis=1)
    occupied = jnp.any(matches, axis=1)
    return (positions, occupied)


def rank_positions(table, cluster_index, capacity):
    in_cluster, earlier, global_pos = cluster_ranks(table, cluster_index)
    rank_code = jnp.where(in_cluster, earlier, -1)
    positions, occupied = code_positions(rank_code, global_pos, capacity)
    return (positions.reshape(-1), occupied.reshape(-1))


def dispatch_rows(outgoing):
    return lax.all_to_all(outgoing, "seq", split_axis=1, concat_axis=1, tiled=True)


def combine_rows(outgoing):
    return lax.all_to_all(outgoing, "seq", split_axis=1, concat_axis=1, tiled=True)


def forward_heads(query_slots, key_slots, value_slots, grad_slots, visible, score_scale):
    query_count, features = query_slots.shape
    key_count = key_slots.shape[0]
    head_count = features // HEAD_DIM
    attended = jnp.zeros((query_count, features), jnp.bfloat16)
    query_grad = jnp.zeros((query_count, features), jnp.bfloat16)
    side_result = jnp.zeros((2, key_count, features), jnp.float32)

    def one_head(head_index, running):
        attended_acc, query_acc, side_acc = running
        column_start = head_index * HEAD_DIM
        query_rows = lax.dynamic_slice_in_dim(query_slots, column_start, HEAD_DIM, 1)
        key_rows = lax.dynamic_slice_in_dim(key_slots, column_start, HEAD_DIM, 1)
        value_rows = lax.dynamic_slice_in_dim(value_slots, column_start, HEAD_DIM, 1)
        grad_rows = lax.dynamic_slice_in_dim(grad_slots, column_start, HEAD_DIM, 1)
        scores = jnp.where(visible, contract_last(query_rows, key_rows) * score_scale, NEG_FILL)
        row_max = jnp.max(scores, axis=1, keepdims=True)
        weights = jnp.where(visible, jnp.exp(scores - row_max), 0.0)
        row_total = jnp.maximum(jnp.sum(weights, axis=1, keepdims=True), 1.0)
        probabilities = weights / row_total
        prob_half = probabilities.astype(jnp.bfloat16)
        attended_head = jnp.dot(prob_half, value_rows, preferred_element_type=jnp.float32).astype(
            jnp.bfloat16
        )
        prob_grad = contract_last(grad_rows, value_rows)
        row_delta = jnp.sum(probabilities * prob_grad, axis=1, keepdims=True)
        score_grad = (probabilities * (prob_grad - row_delta)).astype(jnp.bfloat16)
        query_head = (
            jnp.dot(score_grad, key_rows, preferred_element_type=jnp.float32) * score_scale
        ).astype(jnp.bfloat16)
        attended_acc = lax.dynamic_update_slice_in_dim(attended_acc, attended_head, column_start, 1)
        query_acc = lax.dynamic_update_slice_in_dim(query_acc, query_head, column_start, 1)
        key_part = contract_first(score_grad, query_rows)
        value_part = contract_first(prob_half, grad_rows)
        side_acc = lax.dynamic_update_slice_in_dim(
            side_acc, jnp.stack([key_part, value_part]), column_start, 2
        )
        return (attended_acc, query_acc, side_acc)

    return lax.fori_loop(0, head_count, one_head, (attended, query_grad, side_result))


def per_device(queries, key_vectors, values, cotangent, cluster, block_pattern):
    seq_count = lax.axis_size("seq")
    tok_count, features = queries.shape
    slot_count = 2 * tok_count // seq_count
    group_count = seq_count // GS
    score_scale = HEAD_DIM ** (-0.5)
    my_index = lax.axis_index("seq")
    group_index = my_index // GS
    key_float = key_vectors.astype(jnp.float32)
    square_sum = lax.psum(jnp.sum(key_float * key_float, axis=1), "head")
    key_rms = jnp.sqrt(square_sum / (HEADS * HEAD_DIM) + EPSILON)[:, None]
    normed_float = key_float / key_rms
    normed = normed_float.astype(jnp.bfloat16)
    own_ids = cluster[:, 0]
    everyone = lax.all_gather(own_ids, "seq", axis=0, tiled=True)
    table = everyone.reshape(seq_count, tok_count)
    token_iota = jnp.arange(tok_count, dtype=jnp.int32)
    onehot_own = (own_ids[:, None] == jnp.arange(group_count, dtype=jnp.int32)[None, :]).astype(
        jnp.bfloat16
    )
    before_table = (token_iota[:, None] > token_iota[None, :]).astype(jnp.bfloat16)
    before = jnp.dot(before_table, onehot_own, preferred_element_type=jnp.float32)
    own_rank = jnp.sum(before * onehot_own.astype(jnp.float32), axis=1).astype(jnp.int32)
    pattern = lax.dynamic_index_in_dim(block_pattern, group_index, 0, keepdims=False)
    stacked_inputs = jnp.stack([queries, normed, values, cotangent])
    quarter = features // GS
    capacity = GS * slot_count
    split_inputs = stacked_inputs.reshape(4, tok_count, GS, quarter)
    placed = (
        jnp.zeros((4, group_count, capacity, GS, quarter), jnp.bfloat16)
        .at[:, own_ids, own_rank]
        .set(split_inputs)
    )
    outgoing = placed.transpose(0, 1, 3, 2, 4).reshape(4, seq_count * capacity, quarter)
    arrived = dispatch_rows(outgoing)
    flat_positions, flat_present = rank_positions(table, group_index, capacity)
    visible = visible_mask(pattern, flat_positions, flat_present, flat_positions, flat_present)
    attended, query_grad, both_terms = forward_heads(
        arrived[0], arrived[1], arrived[2], arrived[3], visible, score_scale
    )
    normed_grad = (both_terms[0] * score_scale).astype(jnp.bfloat16)
    value_slots = both_terms[1].astype(jnp.bfloat16)
    outgoing_back = jnp.stack([attended, query_grad, normed_grad, value_slots])
    returned = combine_rows(outgoing_back)
    arranged = returned.reshape(4, group_count, GS, capacity, quarter).transpose(1, 3, 0, 2, 4)
    home_rows = arranged[own_ids, own_rank].transpose(1, 0, 2, 3).reshape(4, tok_count, features)
    grad_float = home_rows[2].astype(jnp.float32)
    inner = lax.psum(jnp.sum(normed_float * grad_float, axis=1), "head")
    key_grad = (
        (grad_float - normed_float * (inner / (HEADS * HEAD_DIM))[:, None]) / key_rms
    ).astype(jnp.bfloat16)
    return (home_rows[0], home_rows[1], key_grad, home_rows[3])


def column_of(rows, first_row, count):
    turned = jnp.transpose(rows)
    pieces = []
    for start in range(0, count, LANES):
        place = first_row + start // LANES
        pieces.append(turned[: min(LANES, count - start), place : place + 1])
    return jnp.concatenate(pieces, axis=0)


def ids_of(ref, first_row, count):
    rows = ref[first_row : first_row + ID_ROWS, :LANES].astype(jnp.float32)
    return column_of(rows, 0, count)


def store_as_rows(out_ref, first_row, column):
    count = column.shape[0]
    for start in range(0, count, LANES):
        size = min(LANES, count - start)
        diagonal = lax.broadcasted_iota(jnp.int32, (size, LANES), 0) == lax.broadcasted_iota(
            jnp.int32, (size, LANES), 1
        )
        spread = jnp.where(diagonal, column[start : start + size], 0.0)
        row = first_row + start // LANES
        out_ref[row : row + 1, :] = jnp.sum(spread, axis=0, keepdims=True)


def block_rows(index, size):
    return pl.ds(pl.multiple_of(index * size, 16), size)


def pack_kernel(half_count, query_ref, value_ref, grad_ref, out_ref, held, sorted_rows, in_sems, out_sems):
    tokens, features = query_ref.shape
    width = features // half_count
    arrivals = [
        pltpu.make_async_copy(source_ref, held.at[place], in_sems.at[place])
        for place, source_ref in enumerate((query_ref, value_ref, grad_ref))
    ]
    for arrival in arrivals:
        arrival.start()
    copies = []
    for place, arrival in enumerate(arrivals):
        arrival.wait()
        for owner in range(half_count):
            rows = pl.ds((owner * 3 + place) * tokens, tokens)
            sorted_rows[rows, :] = held[place, :, owner * width : (owner + 1) * width]
            copy = pltpu.make_async_copy(
                sorted_rows.at[rows, :], out_ref.at[rows, :], out_sems.at[place * half_count + owner]
            )
            copy.start()
            copies.append(copy)
    for copy in copies:
        copy.wait()


def pack_keys_kernel(
    half_count, me_ref, query_ref, value_ref, grad_ref, key_ref, rms_ref, ids_ref, *out_refs
):
    tokens, features = key_ref.shape
    width = features // half_count
    single = width // 2
    is_high = me_ref[0] >= half_count
    inside = me_ref[0] & (half_count - 1)
    key_refs, cross_refs = out_refs[:half_count], out_refs[half_count:]
    rms = column_of(rms_ref[...], 0, tokens)

    def normed_columns(first, size):
        return (key_ref[:, pl.ds(first, size)].astype(jnp.float32) / rms).astype(jnp.bfloat16)

    for distance in range(half_count):
        first = pl.multiple_of((inside ^ distance) * width, LANES)
        cross_ref = cross_refs[distance]
        key_refs[distance][:tokens, :] = normed_columns(first, width)
        key_refs[distance][tokens:, :LANES] = ids_ref[...]
        key_refs[distance][tokens:, LANES:] = jnp.zeros((ID_ROWS, width - LANES), jnp.bfloat16)
        cross_ref[2 * tokens :, :LANES] = ids_ref[...]
        if single > LANES:
            cross_ref[2 * tokens :, LANES:] = jnp.zeros((ID_ROWS, single - LANES), jnp.bfloat16)

        @pl.when(is_high)
        def send_down():
            second = pl.multiple_of(first + single, LANES)
            cross_ref[:tokens, :] = query_ref[:, pl.ds(second, single)]
            cross_ref[tokens : 2 * tokens, :] = grad_ref[:, pl.ds(second, single)]

        @pl.when(jnp.logical_not(is_high))
        def send_up():
            cross_ref[:tokens, :] = normed_columns(first, single)
            cross_ref[tokens : 2 * tokens, :] = value_ref[:, pl.ds(first, single)]


class Slots:
    def __init__(self, shape, me_ref, pattern_ref, packed_ref, key_refs, cross_refs):
        self.tokens, self.half_count, self.cluster_count, self.block_count = shape
        self.half_len = self.tokens * self.half_count
        self.half_blocks = self.half_len // BLK
        self.is_high = me_ref[0] >= self.half_count
        self.inside = me_ref[0] & (self.half_count - 1)
        self.pattern_ref, self.packed_ref = pattern_ref, packed_ref
        self.key_refs, self.cross_refs = key_refs, cross_refs
        lane = lax.broadcasted_iota(jnp.int32, (1, LANES), 1)
        lane_cluster = jnp.zeros((1, LANES), jnp.int32)
        for index in range(1, self.cluster_count + 1):
            lane_cluster = lane_cluster + (lane >= index * self.block_count).astype(jnp.int32)
        self.lane_block = lane - lane_cluster * self.block_count
        self.lane_cluster = lane_cluster.astype(jnp.float32)

    def own_ids(self, ids_all):
        for distance in range(self.half_count):
            ids_all[block_rows(self.inside ^ distance, self.tokens), :] = ids_of(
                self.key_refs[distance], self.tokens, self.tokens
            )

    def cross_ids(self, ids_all):
        for distance in range(self.half_count):
            ids_all[block_rows(self.inside ^ distance, self.tokens), :] = ids_of(
                self.cross_refs[distance], 2 * self.tokens, self.tokens
            )

    def query_features(self, ids_all, target, high):
        for block in range(self.half_blocks):
            rows = slice(block * BLK, (block + 1) * BLK)
            place = block + high * self.half_blocks
            allowed = self.pattern_ref[pl.ds(place, 1), :] == 1.0
            same = ids_all[rows, :] == self.lane_cluster
            target[rows, HEAD_DIM:] = jnp.where(same & allowed, 0.0, NEG_FILL).astype(jnp.bfloat16)

    def key_features(self, ids_all, target, high):
        for block in range(self.half_blocks):
            rows = slice(block * BLK, (block + 1) * BLK)
            place = block + high * self.half_blocks
            same = ids_all[rows, :] == self.lane_cluster
            target[rows, HEAD_DIM:] = jnp.where(same & (self.lane_block == place), 1.0, 0.0).astype(
                jnp.bfloat16
            )

    def own(self, column, query_all, key_all, value_all, grad_all):
        columns = slice(column, column + HEAD_DIM)
        stride = 3 * self.tokens
        for source in range(self.half_count):
            rows = slice(source * self.tokens, (source + 1) * self.tokens)
            for place, target in enumerate((query_all, value_all, grad_all)):
                first = source * stride + place * self.tokens
                target[rows, :HEAD_DIM] = self.packed_ref[first : first + self.tokens, columns]
        for distance in range(self.half_count):
            rows = block_rows(self.inside ^ distance, self.tokens)
            key_all[rows, :HEAD_DIM] = self.key_refs[distance][: self.tokens, columns]

    def cross(self, column, first_all, second_all):
        columns = slice(column, column + HEAD_DIM)
        for distance in range(self.half_count):
            rows = block_rows(self.inside ^ distance, self.tokens)
            cross_ref = self.cross_refs[distance]
            first_all[rows, :HEAD_DIM] = cross_ref[: self.tokens, columns]
            second_all[rows, :] = cross_ref[self.tokens : 2 * self.tokens, columns]


class Keys:
    def __init__(self, key, value, key_turned=None, value_turned=None):
        self.key, self.value = key, value
        self.key_turned, self.value_turned = key_turned, value_turned

    def turn(self):
        self.key_turned[...] = jnp.transpose(self.key[:, :HEAD_DIM])
        self.value_turned[...] = jnp.transpose(self.value[...])


def tile_scores(query_tile, keys, limit, first):
    scores = contract_last(keys.key[:limit, :], query_tile)
    if first is not None:
        key_index = lax.broadcasted_iota(jnp.int32, scores.shape, 0)
        query_index = lax.broadcasted_iota(jnp.int32, scores.shape, 1) + first
        scores = jnp.where(key_index <= query_index, scores, NEG_FILL)
    return scores


def tile_stats(scores, prob_grads):
    row_max = functools.reduce(
        jnp.maximum, [jnp.max(part, axis=0, keepdims=True) for part in scores]
    )
    weights = [jnp.exp2((part - row_max) * EXPONENT_SCALE) for part in scores]
    row_total = sum(jnp.sum(part, axis=0, keepdims=True) for part in weights)
    row_delta = sum(
        jnp.sum(part * grad, axis=0, keepdims=True) for part, grad in zip(weights, prob_grads)
    )
    return weights, row_max, row_total, row_delta


def tile_products(query_tile, grad_tile, pieces):
    scores = [tile_scores(query_tile, *piece) for piece in pieces]
    return scores, [contract_last(keys.value[:limit, :], grad_tile) for keys, limit, _ in pieces]


def all_tiles(query_all, grad_all, half_len, pieces_of, sums, stats_of, keep, add=False):
    tiles = own_tiles(half_len)
    ready = None
    for index, (first, rows, limit) in enumerate(tiles):
        now = ready or tile_products(query_all[rows, :], grad_all[rows, :], pieces_of(first, limit))
        ready = None
        if index + 1 < len(tiles):
            later, later_rows, later_limit = tiles[index + 1]
            ready = tile_products(
                query_all[later_rows, :], grad_all[later_rows, :], pieces_of(later, later_limit)
            )
        keep(
            rows,
            *tile_backward(
                query_all[rows, :],
                grad_all[rows, :],
                pieces_of(first, limit),
                sums,
                stats_of(first, limit - first) if stats_of else None,
                first == 0 and not add,
                *now,
            ),
        )


def tile_backward(query_tile, grad_tile, pieces, sums, stats, is_first, scores, prob_grads):
    if stats is None:
        weights, _, row_total, row_delta = tile_stats(scores, prob_grads)
        inverse = 1.0 / jnp.maximum(row_total, 1.0)
        row_delta = row_delta * inverse
    else:
        row_max, inverse, row_delta = stats
        weights = [jnp.exp2((part - row_max) * EXPONENT_SCALE) for part in scores]
    attended, query_grad = 0.0, 0.0
    for index, (keys, limit, first) in enumerate(pieces):
        probabilities = weights[index] * inverse
        prob_half = probabilities.astype(jnp.bfloat16)
        score_grad = (probabilities * (prob_grads[index] - row_delta)).astype(jnp.bfloat16)
        attended += jnp.dot(
            keys.value_turned[:, :limit], prob_half, preferred_element_type=jnp.float32
        )
        query_grad += jnp.dot(
            keys.key_turned[:, :limit], score_grad, preferred_element_type=jnp.float32
        )
        key_part = jnp.dot(
            score_grad, query_tile[:, :HEAD_DIM], preferred_element_type=jnp.float32
        )
        value_part = jnp.dot(prob_half, grad_tile, preferred_element_type=jnp.float32)
        key_sum, value_sum = sums[index]
        fresh = 0 if is_first else (limit if first is None else first)
        if fresh:
            key_sum[:fresh, :] += key_part[:fresh]
            value_sum[:fresh, :] += value_part[:fresh]
        if fresh < limit:
            key_sum[fresh:limit, :] = key_part[fresh:]
            value_sum[fresh:limit, :] = value_part[fresh:]
    return (
        jnp.transpose(attended).astype(jnp.bfloat16),
        jnp.transpose(query_grad * SCORE_SCALE).astype(jnp.bfloat16),
    )


def own_tiles(half_len, tile=QUERY_TILE):
    tile = tile if half_len % tile == 0 else BLK
    return [(first, slice(first, first + tile), first + tile) for first in range(0, half_len, tile)]


def note_stats(out_ref, stat_rows, head, first, found):
    for place, column in enumerate(found[1:]):
        store_as_rows(out_ref, (3 * head + place) * stat_rows + first // LANES, column)


def stats_kernel(shape, stat_rows, me_ref, pattern_ref, packed_ref, *refs):
    half_count = shape[1]
    cross_refs, key_refs = refs[:half_count], refs[half_count : 2 * half_count][::-1]
    out_ref, query_all, key_all, value_all, grad_all, ids, other_ids = refs[2 * half_count :]
    slots = Slots(shape, me_ref, pattern_ref, packed_ref, key_refs, cross_refs)
    single = packed_ref.shape[1] // 2
    out_ref[...] = jnp.zeros_like(out_ref)
    slots.own_ids(ids)
    slots.key_features(ids, key_all, slots.is_high.astype(jnp.int32))

    @pl.when(slots.is_high)
    def _():
        slots.query_features(ids, query_all, 1)

    @pl.when(jnp.logical_not(slots.is_high))
    def _():
        slots.cross_ids(other_ids)
        slots.query_features(other_ids, query_all, 1)

    for head in range(single // HEAD_DIM):
        column = head * HEAD_DIM
        slots.own(single + column, query_all, key_all, value_all, grad_all)

        def note(first, rows, limit, causal_from):
            scores = tile_scores(query_all[rows, :], Keys(key_all, value_all), limit, causal_from)
            prob_grad = contract_last(value_all[:limit, :], grad_all[rows, :])
            for place, found in enumerate(tile_stats([scores], [prob_grad])[1:]):
                row = (3 * head + place) * stat_rows + first // LANES
                for start in range(0, found.shape[1], LANES):
                    out_ref[row + start // LANES : row + start // LANES + 1, :] = found[
                        :, start : start + LANES
                    ]

        @pl.when(slots.is_high)
        def _():
            for first, rows, limit in own_tiles(slots.half_len, STATS_TILE):
                note(first, rows, limit, first)

        @pl.when(jnp.logical_not(slots.is_high))
        def _():
            slots.cross(column, query_all, grad_all)
            for first, rows, _ in own_tiles(slots.half_len, STATS_TILE):
                note(first, rows, slots.half_len, None)


def store_own(slots, result_refs, column, attended, query_grad, value_sum, key_sum):
    tokens = slots.tokens
    columns = slice(column, column + HEAD_DIM)
    for distance, target in enumerate(result_refs):
        rows = block_rows(slots.inside ^ distance, tokens)
        target[:tokens, columns] = attended[rows, :]
        target[tokens : 2 * tokens, columns] = query_grad[rows, :]
        target[2 * tokens : 3 * tokens, columns] = value_sum[rows, :].astype(jnp.bfloat16)
        target[3 * tokens :, columns] = (key_sum[rows, :] * SCORE_SCALE).astype(jnp.bfloat16)


def first_kernel(shape, me_ref, pattern_ref, packed_ref, *refs):
    half_count = shape[1]
    cross_refs, key_refs = refs[:half_count], refs[half_count : 2 * half_count][::-1]
    refs = refs[2 * half_count + 1 :]
    result_refs, cross_out_refs = refs[:half_count], refs[half_count : 2 * half_count]
    second_ref, sums_ref = refs[2 * half_count : 2 * half_count + 2]
    (query_all, key_all, value_all, grad_all, other_key, other_value, ids, other_ids, attended,
     query_grad, key_sum, value_sum, other_key_sum, other_value_sum, *turned) = refs[
        2 * half_count + 2 :
    ]
    own, other = Keys(key_all, value_all, *turned[:2]), Keys(other_key, other_value, *turned[2:])
    slots = Slots(shape, me_ref, pattern_ref, packed_ref, key_refs, cross_refs)
    single = packed_ref.shape[1] // 2
    half_len = slots.half_len
    high = slots.is_high.astype(jnp.int32)
    slots.own_ids(ids)
    slots.key_features(ids, key_all, high)
    slots.query_features(ids, query_all, high)

    def run(others, other_sums, attended_out, query_grad_out, key_out, value_out):
        def keep(rows, attended_tile, query_grad_tile):
            attended_out[rows, :], query_grad_out[rows, :] = attended_tile, query_grad_tile

        all_tiles(
            query_all,
            grad_all,
            half_len,
            lambda first, limit: others + [(own, limit, first)],
            other_sums + [(key_out, value_out)],
            None,
            keep,
        )

    @pl.when(slots.is_high)
    def _():
        slots.cross_ids(other_ids)
        slots.key_features(other_ids, other_key, 0)

    for head in range(single // HEAD_DIM):
        column = head * HEAD_DIM
        columns = slice(column, column + HEAD_DIM)
        slots.own(column, query_all, key_all, value_all, grad_all)
        own.turn()

        @pl.when(slots.is_high)
        def _():
            slots.cross(column, other_key, other_value)
            other.turn()
            run(
                [(other, half_len, None)],
                [(other_key_sum, other_value_sum)],
                attended, query_grad, key_sum, value_sum,
            )
            for distance in range(half_count):
                rows = block_rows(slots.inside ^ distance, slots.tokens)
                target = cross_out_refs[distance]
                target[: slots.tokens, columns] = (other_key_sum[rows, :] * SCORE_SCALE).astype(
                    jnp.bfloat16
                )
                target[slots.tokens :, columns] = other_value_sum[rows, :].astype(jnp.bfloat16)

        @pl.when(jnp.logical_not(slots.is_high))
        def _():
            run([], [], attended, query_grad, key_sum, value_sum)

        store_own(slots, result_refs, column, attended, query_grad, value_sum, key_sum)

        @pl.when(jnp.logical_not(slots.is_high))
        def _():
            slots.own(single + column, query_all, key_all, value_all, grad_all)
            own.turn()
            run(
                [], [],
                second_ref.at[:half_len, columns],
                second_ref.at[half_len:, columns],
                sums_ref.at[:half_len, columns],
                sums_ref.at[half_len:, columns],
            )


def joint_rows(stat_rows, head, own_stats_ref, far_stats_ref):
    (own_max, own_total, own_delta), (far_max, far_total, far_delta) = [
        [
            ref[(3 * head + place) * stat_rows : (3 * head + place + 1) * stat_rows, :]
            for place in range(3)
        ]
        for ref in (own_stats_ref, far_stats_ref)
    ]
    row_max = jnp.maximum(own_max, far_max)
    own_part = jnp.exp2((own_max - row_max) * EXPONENT_SCALE)
    far_part = jnp.exp2((far_max - row_max) * EXPONENT_SCALE)
    inverse = 1.0 / jnp.maximum(own_total * own_part + far_total * far_part, 1.0)
    return row_max, inverse, (own_delta * own_part + far_delta * far_part) * inverse


def second_head_kernel(shape, stat_rows, me_ref, pattern_ref, packed_ref, *refs):
    half_count = shape[1]
    cross_refs, key_refs = refs[:half_count], refs[half_count : 2 * half_count][::-1]
    own_stats_ref, far_stats_ref, early_ref, sums_ref = refs[2 * half_count : 2 * half_count + 4]
    refs = refs[2 * half_count + 4 :]
    first_cross_refs, result_refs, cross_out_refs = [
        refs[place * half_count : (place + 1) * half_count] for place in range(3)
    ]
    (query_all, key_all, value_all, grad_all, other_query, other_grad, ids, other_ids, attended,
     query_grad, key_sum, value_sum, other_attended, other_query_grad, *turned) = refs[
        3 * half_count :
    ]
    own = Keys(key_all, value_all, *turned)
    slots = Slots(shape, me_ref, pattern_ref, packed_ref, key_refs, cross_refs)
    single = packed_ref.shape[1] // 2
    half_len, tokens = slots.half_len, slots.tokens
    slots.own_ids(ids)
    slots.key_features(ids, key_all, slots.is_high.astype(jnp.int32))

    @pl.when(slots.is_high)
    def _():
        slots.query_features(ids, query_all, 1)
        for distance in range(half_count):
            cross_out_refs[distance][...] = first_cross_refs[distance][...]

    @pl.when(jnp.logical_not(slots.is_high))
    def _():
        slots.cross_ids(other_ids)
        slots.query_features(other_ids, other_query, 1)

    for head in range(single // HEAD_DIM):
        column = head * HEAD_DIM
        columns = slice(column, column + HEAD_DIM)
        slots.own(single + column, query_all, key_all, value_all, grad_all)
        own.turn()
        joint_table = joint_rows(stat_rows, head, own_stats_ref, far_stats_ref)

        def joint_stats(first, size):
            places = range(first // LANES, (first + size) // LANES)
            return [
                jnp.concatenate([rows[place : place + 1, :] for place in places], axis=1)
                for rows in joint_table
            ]

        @pl.when(slots.is_high)
        def _():
            def keep(rows, attended_tile, query_grad_tile):
                attended[rows, :], query_grad[rows, :] = attended_tile, query_grad_tile

            all_tiles(
                query_all,
                grad_all,
                half_len,
                lambda first, limit: [(own, limit, first)],
                [(key_sum, value_sum)],
                joint_stats,
                keep,
            )

        @pl.when(jnp.logical_not(slots.is_high))
        def _():
            slots.cross(column, other_query, other_grad)
            attended[...] = early_ref[:half_len, columns]
            query_grad[...] = early_ref[half_len:, columns]
            key_sum[...] = sums_ref[:half_len, columns]
            value_sum[...] = sums_ref[half_len:, columns]

            def keep(rows, attended_tile, query_grad_tile):
                other_attended[rows, :], other_query_grad[rows, :] = attended_tile, query_grad_tile

            all_tiles(
                other_query,
                other_grad,
                half_len,
                lambda first, limit: [(own, half_len, None)],
                [(key_sum, value_sum)],
                joint_stats,
                keep,
                add=True,
            )
            for distance in range(half_count):
                rows = block_rows(slots.inside ^ distance, tokens)
                target = cross_out_refs[distance]
                target[:tokens, columns] = other_attended[rows, :]
                target[tokens:, columns] = other_query_grad[rows, :]

        store_own(slots, result_refs, column, attended, query_grad, value_sum, key_sum)


def normed_grad_of(half_count, me_ref, first_ref, second_ref, cross_ref):
    tokens = second_ref.shape[0] // 4
    is_low = me_ref[0] < half_count
    far = jnp.where(is_low, cross_ref[:tokens, :].astype(jnp.float32), 0.0)
    first_float = first_ref[3 * tokens :, :].astype(jnp.float32) + far
    second_float = second_ref[3 * tokens :, :].astype(jnp.float32)
    return jnp.concatenate([first_float, second_float], axis=1)


def inner_kernel(half_count, me_ref, key_ref, rms_ref, *refs):
    cross_refs, first_refs, second_refs = [
        refs[place * half_count : (place + 1) * half_count] for place in range(3)
    ]
    out_ref = refs[3 * half_count]
    tokens, features = key_ref.shape
    width = features // half_count
    inside = me_ref[0] & (half_count - 1)
    total = jnp.zeros((tokens, width), jnp.float32)
    for distance in range(half_count):
        owner = inside ^ distance
        start = pl.multiple_of(owner * width, LANES)
        key_float = key_ref[:, pl.ds(start, width)].astype(jnp.float32)
        total = total + key_float * normed_grad_of(
            half_count, me_ref, first_refs[distance], second_refs[distance], cross_refs[distance]
        )
    column = jnp.sum(total, axis=1, keepdims=True) / column_of(rms_ref[...], 0, tokens)
    out_ref[...] = jnp.zeros_like(out_ref)
    store_as_rows(out_ref, 0, column)


def key_kernel(half_count, feature_total, me_ref, key_ref, rms_ref, inner_ref, *refs):
    cross_refs, first_refs, second_refs = [
        refs[place * half_count : (place + 1) * half_count] for place in range(3)
    ]
    key_out_ref = refs[3 * half_count]
    tokens, features = key_ref.shape
    width = features // half_count
    inside = me_ref[0] & (half_count - 1)
    rms = column_of(rms_ref[...], 0, tokens)
    inner = column_of(inner_ref[...], 0, tokens) / feature_total
    for distance in range(half_count):
        columns = pl.ds(pl.multiple_of((inside ^ distance) * width, LANES), width)
        normed_float = key_ref[:, columns].astype(jnp.float32) / rms
        grad_float = normed_grad_of(
            half_count, me_ref, first_refs[distance], second_refs[distance], cross_refs[distance]
        )
        key_out_ref[:, columns] = ((grad_float - normed_float * inner) / rms).astype(jnp.bfloat16)


def final_kernel(half_count, me_ref, *refs):
    cross_refs, first_refs, second_refs = [
        refs[place * half_count : (place + 1) * half_count] for place in range(3)
    ]
    attended_ref, query_ref, value_ref = refs[3 * half_count :]
    tokens, features = attended_ref.shape
    width = features // half_count
    single = width // 2
    is_high = me_ref[0] >= half_count
    inside = me_ref[0] & (half_count - 1)
    for distance in range(half_count):
        start = pl.multiple_of((inside ^ distance) * width, LANES)
        first = pl.ds(start, single)
        second = pl.ds(pl.multiple_of(start + single, LANES), single)
        cross_ref = cross_refs[distance]

        def block(refs, place):
            return refs[distance][place * tokens : (place + 1) * tokens, :]

        def joined(refs, place, far):
            whole = block(refs, place).astype(jnp.float32) + cross_ref[
                far * tokens : (far + 1) * tokens, :
            ].astype(jnp.float32)
            return whole.astype(jnp.bfloat16)

        attended_ref[:, first] = block(first_refs, 0)
        query_ref[:, first] = block(first_refs, 1)
        value_ref[:, second] = block(second_refs, 2)

        @pl.when(is_high)
        def _():
            attended_ref[:, second] = joined(second_refs, 0, 0)
            query_ref[:, second] = joined(second_refs, 1, 1)
            value_ref[:, first] = block(first_refs, 2)

        @pl.when(jnp.logical_not(is_high))
        def _():
            attended_ref[:, second] = block(second_refs, 0)
            query_ref[:, second] = block(second_refs, 1)
            value_ref[:, first] = joined(first_refs, 2, 1)


def lane_rows(vector, row_count):
    return jnp.pad(vector, (0, row_count * LANES - vector.shape[0])).reshape(row_count, LANES)


def half_array(rows, columns):
    return jax.ShapeDtypeStruct((rows, columns), jnp.bfloat16)


def call(kernel, out_shapes, scalars, arrays, scratch=(), in_hbm=0, out_hbm=False, flops=0):
    vmem, anywhere = pl.BlockSpec(memory_space=pltpu.VMEM), pl.BlockSpec(memory_space=pl.ANY)
    return pl.pallas_call(
        kernel,
        out_shape=out_shapes,
        in_specs=[pl.BlockSpec(memory_space=pltpu.SMEM)] * len(scalars)
        + [anywhere] * in_hbm
        + [vmem] * (len(arrays) - in_hbm),
        out_specs=jax.tree.map(lambda shape: anywhere if out_hbm else vmem, out_shapes),
        scratch_shapes=list(scratch),
        compiler_params=pltpu.CompilerParams(vmem_limit_bytes=PACK_VMEM_BYTES if in_hbm else VMEM_BYTES),
        cost_estimate=pl.CostEstimate(flops=flops, bytes_accessed=0, transcendentals=0) if flops else None,
    )(*scalars, *arrays)


def swap(block, distance):
    count = lax.axis_size("seq")
    return lax.ppermute(block, "seq", [(i, i ^ distance) for i in range(count)])


def swap_inside(blocks):
    return [blocks[0]] + [swap(block, d) for d, block in enumerate(blocks) if d]


def swap_across(blocks):
    return [swap(block, len(blocks) + d) for d, block in enumerate(blocks)]


def exchange_inside(rows, half_count):
    count = 2 * half_count
    groups = [list(range(half_count)), list(range(half_count, count))]
    parts = rows.reshape(half_count, -1, rows.shape[1])
    return lax.all_to_all(
        parts, "seq", split_axis=0, concat_axis=0, tiled=True, axis_index_groups=groups
    ).reshape(rows.shape)


def sum_over_head(block):
    count = lax.axis_size("head")
    if count & (count - 1):
        return lax.psum(block, "head")
    return block + sum(
        lax.ppermute(block, "head", [(i, i ^ d) for i in range(count)]) for d in range(1, count)
    )


def by_halves(queries, key_vectors, values, cotangent, cluster, block_pattern):
    count = lax.axis_size("seq")
    half_count = count // 2
    tokens, features = queries.shape
    width = features // half_count
    single = width // 2
    cluster_count, block_count, _ = block_pattern.shape
    half_len = half_count * tokens
    shape = (tokens, half_count, cluster_count, block_count)
    row_count = -(-tokens // (8 * LANES)) * 8
    stat_rows = -(-half_len // (8 * LANES)) * 8
    me = lax.axis_index("seq").astype(jnp.int32).reshape(1)
    packed_shape = half_array(half_count * 3 * tokens, width)
    packed = call(
        functools.partial(pack_kernel, half_count),
        packed_shape,
        [],
        [queries, values, cotangent],
        [
            pltpu.VMEM((3, tokens, features), jnp.bfloat16),
            pltpu.VMEM(packed_shape.shape, jnp.bfloat16),
            pltpu.SemaphoreType.DMA((3,)),
            pltpu.SemaphoreType.DMA((3 * half_count,)),
        ],
        in_hbm=3,
        out_hbm=True,
    )
    packed, key_vectors, cluster = lax.optimization_barrier((packed, key_vectors, cluster))
    packed = exchange_inside(packed, half_count)
    ids = lane_rows(cluster[:, 0], ID_ROWS).astype(jnp.bfloat16)
    key_float = key_vectors.astype(jnp.float32)
    square_sum = sum_over_head(lane_rows(jnp.sum(key_float * key_float, axis=1), row_count))
    feature_total = HEADS * HEAD_DIM
    key_rms = jnp.sqrt(square_sum / feature_total + EPSILON)
    sent = call(
        functools.partial(pack_keys_kernel, half_count),
        [half_array(tokens + ID_ROWS, width)] * half_count
        + [half_array(2 * tokens + ID_ROWS, single)] * half_count,
        [me],
        [queries, values, cotangent, key_vectors, key_rms, ids],
    )
    cross = swap_across(sent[half_count:])
    key_sent = list(sent[:half_count])
    key_sent[1], cross[0] = lax.optimization_barrier((key_sent[1], cross[0]))
    keys = swap_inside(key_sent)
    pattern_rows = block_pattern.transpose(1, 0, 2).reshape(block_count, -1).astype(jnp.float32)
    pattern_rows = jnp.pad(pattern_rows, ((0, 0), (0, LANES - cluster_count * block_count)))
    wide = pltpu.VMEM((half_len, 2 * HEAD_DIM), jnp.bfloat16)
    slim = pltpu.VMEM((half_len, HEAD_DIM), jnp.bfloat16)
    sums = pltpu.VMEM((half_len, HEAD_DIM), jnp.float32)
    turned = pltpu.VMEM((HEAD_DIM, half_len), jnp.bfloat16)
    ids_column = pltpu.VMEM((half_len, 1), jnp.float32)
    block_flops = 12 * half_len * half_len * single
    inputs = [pattern_rows, packed] + cross + keys[::-1]
    stats = call(
        functools.partial(stats_kernel, shape, stat_rows),
        jax.ShapeDtypeStruct((3 * stat_rows * (single // HEAD_DIM), LANES), jnp.float32),
        [me],
        inputs,
        [wide, wide, slim, slim, ids_column, ids_column],
        flops=block_flops // 3,
    )
    far_stats = swap(stats, half_count)
    firsts = call(
        functools.partial(first_kernel, shape),
        [half_array(4 * tokens, single)] * half_count
        + [half_array(2 * tokens, single)] * half_count
        + [
            half_array(2 * half_len, single),
            jax.ShapeDtypeStruct((2 * half_len, single), jnp.float32),
        ],
        [me],
        inputs + [stats],
        [wide, wide, slim, slim, wide, slim, ids_column, ids_column, slim, slim]
        + [sums, sums, sums, sums] + [turned] * 4,
        flops=block_flops + block_flops // 2,
    )
    *firsts, far_stats = lax.optimization_barrier((*firsts, far_stats))
    rest = firsts[half_count:]
    firsts = swap_inside(firsts[:half_count])
    results = call(
        functools.partial(second_head_kernel, shape, stat_rows),
        [half_array(4 * tokens, single)] * half_count
        + [half_array(2 * tokens, single)] * half_count,
        [me],
        inputs + [stats, far_stats] + rest[half_count:] + rest[:half_count],
        [wide, wide, slim, slim, wide, slim, ids_column, ids_column, slim, slim]
        + [sums, sums, slim, slim] + [turned] * 2,
        flops=block_flops,
    )
    far_sent, seconds = list(results[half_count:]), list(results[:half_count])
    near = half_count // 2
    far_parts = swap_across(far_sent)
    seconds[2:], firsts, far_parts[-1] = lax.optimization_barrier((seconds[2:], firsts, far_parts[-1]))
    seconds[1], far_parts[0] = lax.optimization_barrier((seconds[1], far_parts[0]))
    seconds = swap_inside(seconds)
    inner = call(
        functools.partial(inner_kernel, half_count),
        jax.ShapeDtypeStruct((row_count, LANES), jnp.float32),
        [me],
        [key_vectors, key_rms] + far_parts + firsts + seconds,
    )
    inner = sum_over_head(inner)
    attended, query_grad, value_grad = call(
        functools.partial(final_kernel, half_count),
        [half_array(tokens, features)] * 3,
        [me],
        far_parts + firsts + seconds,
    )
    key_grad = call(
        functools.partial(key_kernel, half_count, feature_total),
        half_array(tokens, features),
        [me],
        [key_vectors, key_rms, inner] + far_parts + firsts + seconds,
    )
    return attended, query_grad, key_grad, value_grad


def per_device_any(queries, key_vectors, values, cotangent, cluster, block_pattern):
    count = lax.axis_size("seq")
    tokens, features = queries.shape
    cluster_count, block_count, _ = block_pattern.shape
    fits = (
        count % 2 == 0
        and count & (count - 1) == 0
        and count >= 4
        and tokens <= ID_ROWS * LANES
        and features % (count * HEAD_DIM) == 0
        and tokens % ID_ROWS == 0
        and tokens * count % (2 * BLK) == 0
        and cluster_count * block_count <= LANES
    )
    chosen = by_halves if fits else per_device
    return chosen(queries, key_vectors, values, cotangent, cluster, block_pattern)


def solution(mesh):
    in_specs = (
        P("seq", "head"),
        P("seq", "head"),
        P("seq", "head"),
        P("seq", "head"),
        P("seq", None),
        P(),
    )
    out_specs = (P("seq", "head"), P("seq", "head"), P("seq", "head"), P("seq", "head"))
    return jax.shard_map(
        per_device_any, mesh=mesh, in_specs=in_specs, out_specs=out_specs, check_vma=False
    )
```

```python
import functools

import jax
import jax.numpy as jnp
from jax import lax
from jax.experimental import pallas as pl
from jax.experimental.pallas import tpu as pltpu
from jax.sharding import PartitionSpec as P

HEADS = 32
HEAD_DIM = 128
GS = 4
BLK = 128


NEG_FILL = -1e30
EPSILON = 1e-05
SCORE_SCALE = HEAD_DIM ** (-0.5)
EXPONENT_SCALE = SCORE_SCALE * 1.4426950408889634
LANES = 128
ID_ROWS = 16
QUERY_TILE = 256
STATS_TILE = 384
VMEM_BYTES = 32 << 20
PACK_VMEM_BYTES = 60 << 20


def contract_last(left_side, right_side):
    return lax.dot_general(
        left_side, right_side, (((1,), (1,)), ((), ())), preferred_element_type=jnp.float32
    )


def contract_first(left_side, right_side):
    return lax.dot_general(
        left_side, right_side, (((0,), (0,)), ((), ())), preferred_element_type=jnp.float32
    )


def visible_mask(pattern, query_pos, query_live, key_pos, key_live):
    pattern_rows = pattern[query_pos // BLK]
    allowed = jnp.take(pattern_rows, key_pos // BLK, axis=1) == 1
    causal = key_pos[None, :] <= query_pos[:, None]
    return allowed & causal & query_live[:, None] & key_live[None, :]


def cluster_ranks(table, cluster_index):
    source_count, tok_count = table.shape
    in_cluster = table == cluster_index
    token_iota = jnp.arange(tok_count, dtype=jnp.int32)
    earlier_table = (token_iota[:, None] < token_iota[None, :]).astype(jnp.bfloat16)
    earlier = jnp.dot(
        in_cluster.astype(jnp.bfloat16), earlier_table, preferred_element_type=jnp.float32
    ).astype(jnp.int32)
    global_pos = (
        jnp.arange(source_count, dtype=jnp.int32)[:, None] * tok_count + token_iota[None, :]
    )
    return (in_cluster, earlier, global_pos)


def code_positions(slot_code, global_pos, capacity):
    matches = slot_code[:, :, None] == jnp.arange(capacity, dtype=jnp.int32)[None, None, :]
    positions = jnp.sum(jnp.where(matches, global_pos[:, :, None], 0), axis=1)
    occupied = jnp.any(matches, axis=1)
    return (positions, occupied)


def rank_positions(table, cluster_index, capacity):
    in_cluster, earlier, global_pos = cluster_ranks(table, cluster_index)
    rank_code = jnp.where(in_cluster, earlier, -1)
    positions, occupied = code_positions(rank_code, global_pos, capacity)
    return (positions.reshape(-1), occupied.reshape(-1))


def dispatch_rows(outgoing):
    return lax.all_to_all(outgoing, "seq", split_axis=1, concat_axis=1, tiled=True)


def combine_rows(outgoing):
    return lax.all_to_all(outgoing, "seq", split_axis=1, concat_axis=1, tiled=True)


def forward_heads(query_slots, key_slots, value_slots, grad_slots, visible, score_scale):
    query_count, features = query_slots.shape
    key_count = key_slots.shape[0]
    head_count = features // HEAD_DIM
    attended = jnp.zeros((query_count, features), jnp.bfloat16)
    query_grad = jnp.zeros((query_count, features), jnp.bfloat16)
    side_result = jnp.zeros((2, key_count, features), jnp.float32)

    def one_head(head_index, running):
        attended_acc, query_acc, side_acc = running
        column_start = head_index * HEAD_DIM
        query_rows = lax.dynamic_slice_in_dim(query_slots, column_start, HEAD_DIM, 1)
        key_rows = lax.dynamic_slice_in_dim(key_slots, column_start, HEAD_DIM, 1)
        value_rows = lax.dynamic_slice_in_dim(value_slots, column_start, HEAD_DIM, 1)
        grad_rows = lax.dynamic_slice_in_dim(grad_slots, column_start, HEAD_DIM, 1)
        scores = jnp.where(visible, contract_last(query_rows, key_rows) * score_scale, NEG_FILL)
        row_max = jnp.max(scores, axis=1, keepdims=True)
        weights = jnp.where(visible, jnp.exp(scores - row_max), 0.0)
        row_total = jnp.maximum(jnp.sum(weights, axis=1, keepdims=True), 1.0)
        probabilities = weights / row_total
        prob_half = probabilities.astype(jnp.bfloat16)
        attended_head = jnp.dot(prob_half, value_rows, preferred_element_type=jnp.float32).astype(
            jnp.bfloat16
        )
        prob_grad = contract_last(grad_rows, value_rows)
        row_delta = jnp.sum(probabilities * prob_grad, axis=1, keepdims=True)
        score_grad = (probabilities * (prob_grad - row_delta)).astype(jnp.bfloat16)
        query_head = (
            jnp.dot(score_grad, key_rows, preferred_element_type=jnp.float32) * score_scale
        ).astype(jnp.bfloat16)
        attended_acc = lax.dynamic_update_slice_in_dim(attended_acc, attended_head, column_start, 1)
        query_acc = lax.dynamic_update_slice_in_dim(query_acc, query_head, column_start, 1)
        key_part = contract_first(score_grad, query_rows)
        value_part = contract_first(prob_half, grad_rows)
        side_acc = lax.dynamic_update_slice_in_dim(
            side_acc, jnp.stack([key_part, value_part]), column_start, 2
        )
        return (attended_acc, query_acc, side_acc)

    return lax.fori_loop(0, head_count, one_head, (attended, query_grad, side_result))


def per_device(queries, key_vectors, values, cotangent, cluster, block_pattern):
    seq_count = lax.axis_size("seq")
    tok_count, features = queries.shape
    slot_count = 2 * tok_count // seq_count
    group_count = seq_count // GS
    score_scale = HEAD_DIM ** (-0.5)
    my_index = lax.axis_index("seq")
    group_index = my_index // GS
    key_float = key_vectors.astype(jnp.float32)
    square_sum = lax.psum(jnp.sum(key_float * key_float, axis=1), "head")
    key_rms = jnp.sqrt(square_sum / (HEADS * HEAD_DIM) + EPSILON)[:, None]
    normed_float = key_float / key_rms
    normed = normed_float.astype(jnp.bfloat16)
    own_ids = cluster[:, 0]
    everyone = lax.all_gather(own_ids, "seq", axis=0, tiled=True)
    table = everyone.reshape(seq_count, tok_count)
    token_iota = jnp.arange(tok_count, dtype=jnp.int32)
    onehot_own = (own_ids[:, None] == jnp.arange(group_count, dtype=jnp.int32)[None, :]).astype(
        jnp.bfloat16
    )
    before_table = (token_iota[:, None] > token_iota[None, :]).astype(jnp.bfloat16)
    before = jnp.dot(before_table, onehot_own, preferred_element_type=jnp.float32)
    own_rank = jnp.sum(before * onehot_own.astype(jnp.float32), axis=1).astype(jnp.int32)
    pattern = lax.dynamic_index_in_dim(block_pattern, group_index, 0, keepdims=False)
    stacked_inputs = jnp.stack([queries, normed, values, cotangent])
    quarter = features // GS
    capacity = GS * slot_count
    split_inputs = stacked_inputs.reshape(4, tok_count, GS, quarter)
    placed = (
        jnp.zeros((4, group_count, capacity, GS, quarter), jnp.bfloat16)
        .at[:, own_ids, own_rank]
        .set(split_inputs)
    )
    outgoing = placed.transpose(0, 1, 3, 2, 4).reshape(4, seq_count * capacity, quarter)
    arrived = dispatch_rows(outgoing)
    flat_positions, flat_present = rank_positions(table, group_index, capacity)
    visible = visible_mask(pattern, flat_positions, flat_present, flat_positions, flat_present)
    attended, query_grad, both_terms = forward_heads(
        arrived[0], arrived[1], arrived[2], arrived[3], visible, score_scale
    )
    normed_grad = (both_terms[0] * score_scale).astype(jnp.bfloat16)
    value_slots = both_terms[1].astype(jnp.bfloat16)
    outgoing_back = jnp.stack([attended, query_grad, normed_grad, value_slots])
    returned = combine_rows(outgoing_back)
    arranged = returned.reshape(4, group_count, GS, capacity, quarter).transpose(1, 3, 0, 2, 4)
    home_rows = arranged[own_ids, own_rank].transpose(1, 0, 2, 3).reshape(4, tok_count, features)
    grad_float = home_rows[2].astype(jnp.float32)
    inner = lax.psum(jnp.sum(normed_float * grad_float, axis=1), "head")
    key_grad = (
        (grad_float - normed_float * (inner / (HEADS * HEAD_DIM))[:, None]) / key_rms
    ).astype(jnp.bfloat16)
    return (home_rows[0], home_rows[1], key_grad, home_rows[3])


def column_of(rows, first_row, count):
    turned = jnp.transpose(rows)
    pieces = []
    for start in range(0, count, LANES):
        place = first_row + start // LANES
        pieces.append(turned[: min(LANES, count - start), place : place + 1])
    return jnp.concatenate(pieces, axis=0)


def ids_of(ref, first_row, count):
    rows = ref[first_row : first_row + ID_ROWS, :LANES].astype(jnp.float32)
    return column_of(rows, 0, count)


def store_as_rows(out_ref, first_row, column):
    count = column.shape[0]
    for start in range(0, count, LANES):
        size = min(LANES, count - start)
        diagonal = lax.broadcasted_iota(jnp.int32, (size, LANES), 0) == lax.broadcasted_iota(
            jnp.int32, (size, LANES), 1
        )
        spread = jnp.where(diagonal, column[start : start + size], 0.0)
        row = first_row + start // LANES
        out_ref[row : row + 1, :] = jnp.sum(spread, axis=0, keepdims=True)


def block_rows(index, size):
    return pl.ds(pl.multiple_of(index * size, 16), size)


def pack_kernel(half_count, query_ref, value_ref, grad_ref, out_ref, held, sorted_rows, in_sems, out_sems):
    tokens, features = query_ref.shape
    width = features // half_count
    arrivals = [
        pltpu.make_async_copy(source_ref, held.at[place], in_sems.at[place])
        for place, source_ref in enumerate((query_ref, value_ref, grad_ref))
    ]
    for arrival in arrivals:
        arrival.start()
    copies = []
    for place, arrival in enumerate(arrivals):
        arrival.wait()
        for owner in range(half_count):
            rows = pl.ds((owner * 3 + place) * tokens, tokens)
            sorted_rows[rows, :] = held[place, :, owner * width : (owner + 1) * width]
            copy = pltpu.make_async_copy(
                sorted_rows.at[rows, :], out_ref.at[rows, :], out_sems.at[place * half_count + owner]
            )
            copy.start()
            copies.append(copy)
    for copy in copies:
        copy.wait()


def pack_keys_kernel(
    half_count, me_ref, query_ref, value_ref, grad_ref, key_ref, rms_ref, ids_ref, *out_refs
):
    tokens, features = key_ref.shape
    width = features // half_count
    single = width // 2
    is_high = me_ref[0] >= half_count
    inside = me_ref[0] & (half_count - 1)
    key_refs, cross_refs = out_refs[:half_count], out_refs[half_count:]
    rms = column_of(rms_ref[...], 0, tokens)

    def normed_columns(first, size):
        return (key_ref[:, pl.ds(first, size)].astype(jnp.float32) / rms).astype(jnp.bfloat16)

    for distance in range(half_count):
        first = pl.multiple_of((inside ^ distance) * width, LANES)
        cross_ref = cross_refs[distance]
        key_refs[distance][:tokens, :] = normed_columns(first, width)
        key_refs[distance][tokens:, :LANES] = ids_ref[...]
        key_refs[distance][tokens:, LANES:] = jnp.zeros((ID_ROWS, width - LANES), jnp.bfloat16)
        cross_ref[2 * tokens :, :LANES] = ids_ref[...]
        if single > LANES:
            cross_ref[2 * tokens :, LANES:] = jnp.zeros((ID_ROWS, single - LANES), jnp.bfloat16)

        @pl.when(is_high)
        def send_down():
            second = pl.multiple_of(first + single, LANES)
            cross_ref[:tokens, :] = query_ref[:, pl.ds(second, single)]
            cross_ref[tokens : 2 * tokens, :] = grad_ref[:, pl.ds(second, single)]

        @pl.when(jnp.logical_not(is_high))
        def send_up():
            cross_ref[:tokens, :] = normed_columns(first, single)
            cross_ref[tokens : 2 * tokens, :] = value_ref[:, pl.ds(first, single)]


class Slots:
    def __init__(self, shape, me_ref, pattern_ref, packed_ref, key_refs, cross_refs):
        self.tokens, self.half_count, self.cluster_count, self.block_count = shape
        self.half_len = self.tokens * self.half_count
        self.half_blocks = self.half_len // BLK
        self.is_high = me_ref[0] >= self.half_count
        self.inside = me_ref[0] & (self.half_count - 1)
        self.pattern_ref, self.packed_ref = pattern_ref, packed_ref
        self.key_refs, self.cross_refs = key_refs, cross_refs
        lane = lax.broadcasted_iota(jnp.int32, (1, LANES), 1)
        lane_cluster = jnp.zeros((1, LANES), jnp.int32)
        for index in range(1, self.cluster_count + 1):
            lane_cluster = lane_cluster + (lane >= index * self.block_count).astype(jnp.int32)
        self.lane_block = lane - lane_cluster * self.block_count
        self.lane_cluster = lane_cluster.astype(jnp.float32)

    def own_ids(self, ids_all):
        for distance in range(self.half_count):
            ids_all[block_rows(self.inside ^ distance, self.tokens), :] = ids_of(
                self.key_refs[distance], self.tokens, self.tokens
            )

    def cross_ids(self, ids_all):
        for distance in range(self.half_count):
            ids_all[block_rows(self.inside ^ distance, self.tokens), :] = ids_of(
                self.cross_refs[distance], 2 * self.tokens, self.tokens
            )

    def query_features(self, ids_all, target, high):
        for block in range(self.half_blocks):
            rows = slice(block * BLK, (block + 1) * BLK)
            place = block + high * self.half_blocks
            allowed = self.pattern_ref[pl.ds(place, 1), :] == 1.0
            same = ids_all[rows, :] == self.lane_cluster
            target[rows, HEAD_DIM:] = jnp.where(same & allowed, 0.0, NEG_FILL).astype(jnp.bfloat16)

    def key_features(self, ids_all, target, high):
        for block in range(self.half_blocks):
            rows = slice(block * BLK, (block + 1) * BLK)
            place = block + high * self.half_blocks
            same = ids_all[rows, :] == self.lane_cluster
            target[rows, HEAD_DIM:] = jnp.where(same & (self.lane_block == place), 1.0, 0.0).astype(
                jnp.bfloat16
            )

    def own(self, column, query_all, key_all, value_all, grad_all):
        columns = slice(column, column + HEAD_DIM)
        stride = 3 * self.tokens
        for source in range(self.half_count):
            rows = slice(source * self.tokens, (source + 1) * self.tokens)
            for place, target in enumerate((query_all, value_all, grad_all)):
                first = source * stride + place * self.tokens
                target[rows, :HEAD_DIM] = self.packed_ref[first : first + self.tokens, columns]
        for distance in range(self.half_count):
            rows = block_rows(self.inside ^ distance, self.tokens)
            key_all[rows, :HEAD_DIM] = self.key_refs[distance][: self.tokens, columns]

    def cross(self, column, first_all, second_all):
        columns = slice(column, column + HEAD_DIM)
        for distance in range(self.half_count):
            rows = block_rows(self.inside ^ distance, self.tokens)
            cross_ref = self.cross_refs[distance]
            first_all[rows, :HEAD_DIM] = cross_ref[: self.tokens, columns]
            second_all[rows, :] = cross_ref[self.tokens : 2 * self.tokens, columns]


class Keys:
    def __init__(self, key, value, key_turned=None, value_turned=None):
        self.key, self.value = key, value
        self.key_turned, self.value_turned = key_turned, value_turned

    def turn(self):
        self.key_turned[...] = jnp.transpose(self.key[:, :HEAD_DIM])
        self.value_turned[...] = jnp.transpose(self.value[...])


def tile_scores(query_tile, keys, limit, first):
    scores = contract_last(keys.key[:limit, :], query_tile)
    if first is not None:
        key_index = lax.broadcasted_iota(jnp.int32, scores.shape, 0)
        query_index = lax.broadcasted_iota(jnp.int32, scores.shape, 1) + first
        scores = jnp.where(key_index <= query_index, scores, NEG_FILL)
    return scores


def tile_stats(scores, prob_grads):
    row_max = functools.reduce(
        jnp.maximum, [jnp.max(part, axis=0, keepdims=True) for part in scores]
    )
    weights = [jnp.exp2((part - row_max) * EXPONENT_SCALE) for part in scores]
    row_total = sum(jnp.sum(part, axis=0, keepdims=True) for part in weights)
    row_delta = sum(
        jnp.sum(part * grad, axis=0, keepdims=True) for part, grad in zip(weights, prob_grads)
    )
    return weights, row_max, row_total, row_delta


def tile_products(query_tile, grad_tile, pieces):
    scores = [tile_scores(query_tile, *piece) for piece in pieces]
    return scores, [contract_last(keys.value[:limit, :], grad_tile) for keys, limit, _ in pieces]


def all_tiles(query_all, grad_all, half_len, pieces_of, sums, stats_of, keep, add=False):
    tiles = own_tiles(half_len)
    ready = None
    for index, (first, rows, limit) in enumerate(tiles):
        now = ready or tile_products(query_all[rows, :], grad_all[rows, :], pieces_of(first, limit))
        ready = None
        if index + 1 < len(tiles):
            later, later_rows, later_limit = tiles[index + 1]
            ready = tile_products(
                query_all[later_rows, :], grad_all[later_rows, :], pieces_of(later, later_limit)
            )
        keep(
            rows,
            *tile_backward(
                query_all[rows, :],
                grad_all[rows, :],
                pieces_of(first, limit),
                sums,
                stats_of(first, limit - first) if stats_of else None,
                first == 0 and not add,
                *now,
            ),
        )


def tile_backward(query_tile, grad_tile, pieces, sums, stats, is_first, scores, prob_grads):
    if stats is None:
        weights, _, row_total, row_delta = tile_stats(scores, prob_grads)
        inverse = 1.0 / jnp.maximum(row_total, 1.0)
        row_delta = row_delta * inverse
    else:
        row_max, inverse, row_delta = stats
        weights = [jnp.exp2((part - row_max) * EXPONENT_SCALE) for part in scores]
    attended, query_grad = 0.0, 0.0
    for index, (keys, limit, first) in enumerate(pieces):
        probabilities = weights[index] * inverse
        prob_half = probabilities.astype(jnp.bfloat16)
        score_grad = (probabilities * (prob_grads[index] - row_delta)).astype(jnp.bfloat16)
        attended += jnp.dot(
            keys.value_turned[:, :limit], prob_half, preferred_element_type=jnp.float32
        )
        query_grad += jnp.dot(
            keys.key_turned[:, :limit], score_grad, preferred_element_type=jnp.float32
        )
        key_part = jnp.dot(
            score_grad, query_tile[:, :HEAD_DIM], preferred_element_type=jnp.float32
        )
        value_part = jnp.dot(prob_half, grad_tile, preferred_element_type=jnp.float32)
        key_sum, value_sum = sums[index]
        fresh = 0 if is_first else (limit if first is None else first)
        if fresh:
            key_sum[:fresh, :] += key_part[:fresh]
            value_sum[:fresh, :] += value_part[:fresh]
        if fresh < limit:
            key_sum[fresh:limit, :] = key_part[fresh:]
            value_sum[fresh:limit, :] = value_part[fresh:]
    return (
        jnp.transpose(attended).astype(jnp.bfloat16),
        jnp.transpose(query_grad * SCORE_SCALE).astype(jnp.bfloat16),
    )


def own_tiles(half_len, tile=QUERY_TILE):
    tile = tile if half_len % tile == 0 else BLK
    return [(first, slice(first, first + tile), first + tile) for first in range(0, half_len, tile)]


def note_stats(out_ref, stat_rows, head, first, found):
    for place, column in enumerate(found[1:]):
        store_as_rows(out_ref, (3 * head + place) * stat_rows + first // LANES, column)


def stats_kernel(shape, stat_rows, me_ref, pattern_ref, packed_ref, *refs):
    half_count = shape[1]
    cross_refs, key_refs = refs[:half_count], refs[half_count : 2 * half_count][::-1]
    out_ref, query_all, key_all, value_all, grad_all, ids, other_ids = refs[2 * half_count :]
    slots = Slots(shape, me_ref, pattern_ref, packed_ref, key_refs, cross_refs)
    single = packed_ref.shape[1] // 2
    out_ref[...] = jnp.zeros_like(out_ref)
    slots.own_ids(ids)
    slots.key_features(ids, key_all, slots.is_high.astype(jnp.int32))

    @pl.when(slots.is_high)
    def _():
        slots.query_features(ids, query_all, 1)

    @pl.when(jnp.logical_not(slots.is_high))
    def _():
        slots.cross_ids(other_ids)
        slots.query_features(other_ids, query_all, 1)

    for head in range(single // HEAD_DIM):
        column = head * HEAD_DIM
        slots.own(single + column, query_all, key_all, value_all, grad_all)

        def note(first, rows, limit, causal_from):
            scores = tile_scores(query_all[rows, :], Keys(key_all, value_all), limit, causal_from)
            prob_grad = contract_last(value_all[:limit, :], grad_all[rows, :])
            for place, found in enumerate(tile_stats([scores], [prob_grad])[1:]):
                row = (3 * head + place) * stat_rows + first // LANES
                for start in range(0, found.shape[1], LANES):
                    out_ref[row + start // LANES : row + start // LANES + 1, :] = found[
                        :, start : start + LANES
                    ]

        @pl.when(slots.is_high)
        def _():
            for first, rows, limit in own_tiles(slots.half_len, STATS_TILE):
                note(first, rows, limit, first)

        @pl.when(jnp.logical_not(slots.is_high))
        def _():
            slots.cross(column, query_all, grad_all)
            for first, rows, _ in own_tiles(slots.half_len, STATS_TILE):
                note(first, rows, slots.half_len, None)


def store_own(slots, result_refs, column, attended, query_grad, value_sum, key_sum):
    tokens = slots.tokens
    columns = slice(column, column + HEAD_DIM)
    for distance, target in enumerate(result_refs):
        rows = block_rows(slots.inside ^ distance, tokens)
        target[:tokens, columns] = attended[rows, :]
        target[tokens : 2 * tokens, columns] = query_grad[rows, :]
        target[2 * tokens : 3 * tokens, columns] = value_sum[rows, :].astype(jnp.bfloat16)
        target[3 * tokens :, columns] = (key_sum[rows, :] * SCORE_SCALE).astype(jnp.bfloat16)


def first_kernel(shape, me_ref, pattern_ref, packed_ref, *refs):
    half_count = shape[1]
    cross_refs, key_refs = refs[:half_count], refs[half_count : 2 * half_count][::-1]
    refs = refs[2 * half_count + 1 :]
    result_refs, cross_out_refs = refs[:half_count], refs[half_count : 2 * half_count]
    second_ref, sums_ref = refs[2 * half_count : 2 * half_count + 2]
    (query_all, key_all, value_all, grad_all, other_key, other_value, ids, other_ids, attended,
     query_grad, key_sum, value_sum, other_key_sum, other_value_sum, *turned) = refs[
        2 * half_count + 2 :
    ]
    own, other = Keys(key_all, value_all, *turned[:2]), Keys(other_key, other_value, *turned[2:])
    slots = Slots(shape, me_ref, pattern_ref, packed_ref, key_refs, cross_refs)
    single = packed_ref.shape[1] // 2
    half_len = slots.half_len
    high = slots.is_high.astype(jnp.int32)
    slots.own_ids(ids)
    slots.key_features(ids, key_all, high)
    slots.query_features(ids, query_all, high)

    def run(others, other_sums, attended_out, query_grad_out, key_out, value_out):
        def keep(rows, attended_tile, query_grad_tile):
            attended_out[rows, :], query_grad_out[rows, :] = attended_tile, query_grad_tile

        all_tiles(
            query_all,
            grad_all,
            half_len,
            lambda first, limit: others + [(own, limit, first)],
            other_sums + [(key_out, value_out)],
            None,
            keep,
        )

    @pl.when(slots.is_high)
    def _():
        slots.cross_ids(other_ids)
        slots.key_features(other_ids, other_key, 0)

    for head in range(single // HEAD_DIM):
        column = head * HEAD_DIM
        columns = slice(column, column + HEAD_DIM)
        slots.own(column, query_all, key_all, value_all, grad_all)
        own.turn()

        @pl.when(slots.is_high)
        def _():
            slots.cross(column, other_key, other_value)
            other.turn()
            run(
                [(other, half_len, None)],
                [(other_key_sum, other_value_sum)],
                attended, query_grad, key_sum, value_sum,
            )
            for distance in range(half_count):
                rows = block_rows(slots.inside ^ distance, slots.tokens)
                target = cross_out_refs[distance]
                target[: slots.tokens, columns] = (other_key_sum[rows, :] * SCORE_SCALE).astype(
                    jnp.bfloat16
                )
                target[slots.tokens :, columns] = other_value_sum[rows, :].astype(jnp.bfloat16)

        @pl.when(jnp.logical_not(slots.is_high))
        def _():
            run([], [], attended, query_grad, key_sum, value_sum)

        store_own(slots, result_refs, column, attended, query_grad, value_sum, key_sum)

        @pl.when(jnp.logical_not(slots.is_high))
        def _():
            slots.own(single + column, query_all, key_all, value_all, grad_all)
            own.turn()
            run(
                [], [],
                second_ref.at[:half_len, columns],
                second_ref.at[half_len:, columns],
                sums_ref.at[:half_len, columns],
                sums_ref.at[half_len:, columns],
            )


def joint_rows(stat_rows, head, own_stats_ref, far_stats_ref):
    (own_max, own_total, own_delta), (far_max, far_total, far_delta) = [
        [
            ref[(3 * head + place) * stat_rows : (3 * head + place + 1) * stat_rows, :]
            for place in range(3)
        ]
        for ref in (own_stats_ref, far_stats_ref)
    ]
    row_max = jnp.maximum(own_max, far_max)
    own_part = jnp.exp2((own_max - row_max) * EXPONENT_SCALE)
    far_part = jnp.exp2((far_max - row_max) * EXPONENT_SCALE)
    inverse = 1.0 / jnp.maximum(own_total * own_part + far_total * far_part, 1.0)
    return row_max, inverse, (own_delta * own_part + far_delta * far_part) * inverse


def second_head_kernel(shape, stat_rows, me_ref, pattern_ref, packed_ref, *refs):
    half_count = shape[1]
    cross_refs, key_refs = refs[:half_count], refs[half_count : 2 * half_count][::-1]
    own_stats_ref, far_stats_ref, early_ref, sums_ref = refs[2 * half_count : 2 * half_count + 4]
    refs = refs[2 * half_count + 4 :]
    first_cross_refs, result_refs, cross_out_refs = [
        refs[place * half_count : (place + 1) * half_count] for place in range(3)
    ]
    (query_all, key_all, value_all, grad_all, other_query, other_grad, ids, other_ids, attended,
     query_grad, key_sum, value_sum, other_attended, other_query_grad, *turned) = refs[
        3 * half_count :
    ]
    own = Keys(key_all, value_all, *turned)
    slots = Slots(shape, me_ref, pattern_ref, packed_ref, key_refs, cross_refs)
    single = packed_ref.shape[1] // 2
    half_len, tokens = slots.half_len, slots.tokens
    slots.own_ids(ids)
    slots.key_features(ids, key_all, slots.is_high.astype(jnp.int32))

    @pl.when(slots.is_high)
    def _():
        slots.query_features(ids, query_all, 1)
        for distance in range(half_count):
            cross_out_refs[distance][...] = first_cross_refs[distance][...]

    @pl.when(jnp.logical_not(slots.is_high))
    def _():
        slots.cross_ids(other_ids)
        slots.query_features(other_ids, other_query, 1)

    for head in range(single // HEAD_DIM):
        column = head * HEAD_DIM
        columns = slice(column, column + HEAD_DIM)
        slots.own(single + column, query_all, key_all, value_all, grad_all)
        own.turn()
        joint_table = joint_rows(stat_rows, head, own_stats_ref, far_stats_ref)

        def joint_stats(first, size):
            places = range(first // LANES, (first + size) // LANES)
            return [
                jnp.concatenate([rows[place : place + 1, :] for place in places], axis=1)
                for rows in joint_table
            ]

        @pl.when(slots.is_high)
        def _():
            def keep(rows, attended_tile, query_grad_tile):
                attended[rows, :], query_grad[rows, :] = attended_tile, query_grad_tile

            all_tiles(
                query_all,
                grad_all,
                half_len,
                lambda first, limit: [(own, limit, first)],
                [(key_sum, value_sum)],
                joint_stats,
                keep,
            )

        @pl.when(jnp.logical_not(slots.is_high))
        def _():
            slots.cross(column, other_query, other_grad)
            attended[...] = early_ref[:half_len, columns]
            query_grad[...] = early_ref[half_len:, columns]
            key_sum[...] = sums_ref[:half_len, columns]
            value_sum[...] = sums_ref[half_len:, columns]

            def keep(rows, attended_tile, query_grad_tile):
                other_attended[rows, :], other_query_grad[rows, :] = attended_tile, query_grad_tile

            all_tiles(
                other_query,
                other_grad,
                half_len,
                lambda first, limit: [(own, half_len, None)],
                [(key_sum, value_sum)],
                joint_stats,
                keep,
                add=True,
            )
            for distance in range(half_count):
                rows = block_rows(slots.inside ^ distance, tokens)
                target = cross_out_refs[distance]
                target[:tokens, columns] = other_attended[rows, :]
                target[tokens:, columns] = other_query_grad[rows, :]

        store_own(slots, result_refs, column, attended, query_grad, value_sum, key_sum)


def normed_grad_of(half_count, me_ref, first_ref, second_ref, cross_ref):
    tokens = second_ref.shape[0] // 4
    is_low = me_ref[0] < half_count
    far = jnp.where(is_low, cross_ref[:tokens, :].astype(jnp.float32), 0.0)
    first_float = first_ref[3 * tokens :, :].astype(jnp.float32) + far
    second_float = second_ref[3 * tokens :, :].astype(jnp.float32)
    return jnp.concatenate([first_float, second_float], axis=1)


def inner_kernel(half_count, me_ref, key_ref, rms_ref, *refs):
    cross_refs, first_refs, second_refs = [
        refs[place * half_count : (place + 1) * half_count] for place in range(3)
    ]
    out_ref = refs[3 * half_count]
    tokens, features = key_ref.shape
    width = features // half_count
    inside = me_ref[0] & (half_count - 1)
    total = jnp.zeros((tokens, width), jnp.float32)
    for distance in range(half_count):
        owner = inside ^ distance
        start = pl.multiple_of(owner * width, LANES)
        key_float = key_ref[:, pl.ds(start, width)].astype(jnp.float32)
        total = total + key_float * normed_grad_of(
            half_count, me_ref, first_refs[distance], second_refs[distance], cross_refs[distance]
        )
    column = jnp.sum(total, axis=1, keepdims=True) / column_of(rms_ref[...], 0, tokens)
    out_ref[...] = jnp.zeros_like(out_ref)
    store_as_rows(out_ref, 0, column)


def key_kernel(half_count, feature_total, me_ref, key_ref, rms_ref, inner_ref, *refs):
    cross_refs, first_refs, second_refs = [
        refs[place * half_count : (place + 1) * half_count] for place in range(3)
    ]
    key_out_ref = refs[3 * half_count]
    tokens, features = key_ref.shape
    width = features // half_count
    inside = me_ref[0] & (half_count - 1)
    inverse = 1.0 / column_of(rms_ref[...], 0, tokens)
    inner = column_of(inner_ref[...], 0, tokens) * inverse / feature_total
    for distance in range(half_count):
        columns = pl.ds(pl.multiple_of((inside ^ distance) * width, LANES), width)
        key_float = key_ref[:, columns].astype(jnp.float32)
        grad_float = normed_grad_of(
            half_count, me_ref, first_refs[distance], second_refs[distance], cross_refs[distance]
        )
        key_out_ref[:, columns] = ((grad_float - key_float * inner) * inverse).astype(jnp.bfloat16)


def final_kernel(half_count, me_ref, *refs):
    cross_refs, first_refs, second_refs = [
        refs[place * half_count : (place + 1) * half_count] for place in range(3)
    ]
    attended_ref, query_ref, value_ref = refs[3 * half_count :]
    tokens, features = attended_ref.shape
    width = features // half_count
    single = width // 2
    is_high = me_ref[0] >= half_count
    inside = me_ref[0] & (half_count - 1)
    for distance in range(half_count):
        start = pl.multiple_of((inside ^ distance) * width, LANES)
        first = pl.ds(start, single)
        second = pl.ds(pl.multiple_of(start + single, LANES), single)
        cross_ref = cross_refs[distance]

        def block(refs, place):
            return refs[distance][place * tokens : (place + 1) * tokens, :]

        def joined(refs, place, far):
            whole = block(refs, place).astype(jnp.float32) + cross_ref[
                far * tokens : (far + 1) * tokens, :
            ].astype(jnp.float32)
            return whole.astype(jnp.bfloat16)

        attended_ref[:, first] = block(first_refs, 0)
        query_ref[:, first] = block(first_refs, 1)
        value_ref[:, second] = block(second_refs, 2)

        @pl.when(is_high)
        def _():
            attended_ref[:, second] = joined(second_refs, 0, 0)
            query_ref[:, second] = joined(second_refs, 1, 1)
            value_ref[:, first] = block(first_refs, 2)

        @pl.when(jnp.logical_not(is_high))
        def _():
            attended_ref[:, second] = block(second_refs, 0)
            query_ref[:, second] = block(second_refs, 1)
            value_ref[:, first] = joined(first_refs, 2, 1)


def lane_rows(vector, row_count):
    return jnp.pad(vector, (0, row_count * LANES - vector.shape[0])).reshape(row_count, LANES)


def half_array(rows, columns):
    return jax.ShapeDtypeStruct((rows, columns), jnp.bfloat16)


def call(kernel, out_shapes, scalars, arrays, scratch=(), in_hbm=0, out_hbm=False, flops=0):
    vmem, anywhere = pl.BlockSpec(memory_space=pltpu.VMEM), pl.BlockSpec(memory_space=pl.ANY)
    return pl.pallas_call(
        kernel,
        out_shape=out_shapes,
        in_specs=[pl.BlockSpec(memory_space=pltpu.SMEM)] * len(scalars)
        + [anywhere] * in_hbm
        + [vmem] * (len(arrays) - in_hbm),
        out_specs=jax.tree.map(lambda shape: anywhere if out_hbm else vmem, out_shapes),
        scratch_shapes=list(scratch),
        compiler_params=pltpu.CompilerParams(vmem_limit_bytes=PACK_VMEM_BYTES if in_hbm else VMEM_BYTES),
        cost_estimate=pl.CostEstimate(flops=flops, bytes_accessed=0, transcendentals=0) if flops else None,
    )(*scalars, *arrays)


def swap(block, distance):
    count = lax.axis_size("seq")
    return lax.ppermute(block, "seq", [(i, i ^ distance) for i in range(count)])


def swap_inside(blocks):
    return [blocks[0]] + [swap(block, d) for d, block in enumerate(blocks) if d]


def swap_across(blocks):
    return [swap(block, len(blocks) + d) for d, block in enumerate(blocks)]


def exchange_inside(rows, half_count):
    count = 2 * half_count
    groups = [list(range(half_count)), list(range(half_count, count))]
    parts = rows.reshape(half_count, -1, rows.shape[1])
    return lax.all_to_all(
        parts, "seq", split_axis=0, concat_axis=0, tiled=True, axis_index_groups=groups
    ).reshape(rows.shape)


def sum_over_head(block):
    count = lax.axis_size("head")
    if count & (count - 1):
        return lax.psum(block, "head")
    return block + sum(
        lax.ppermute(block, "head", [(i, i ^ d) for i in range(count)]) for d in range(1, count)
    )


def by_halves(queries, key_vectors, values, cotangent, cluster, block_pattern):
    count = lax.axis_size("seq")
    half_count = count // 2
    tokens, features = queries.shape
    width = features // half_count
    single = width // 2
    cluster_count, block_count, _ = block_pattern.shape
    half_len = half_count * tokens
    shape = (tokens, half_count, cluster_count, block_count)
    row_count = -(-tokens // (8 * LANES)) * 8
    stat_rows = -(-half_len // (8 * LANES)) * 8
    me = lax.axis_index("seq").astype(jnp.int32).reshape(1)
    packed_shape = half_array(half_count * 3 * tokens, width)
    packed = call(
        functools.partial(pack_kernel, half_count),
        packed_shape,
        [],
        [queries, values, cotangent],
        [
            pltpu.VMEM((3, tokens, features), jnp.bfloat16),
            pltpu.VMEM(packed_shape.shape, jnp.bfloat16),
            pltpu.SemaphoreType.DMA((3,)),
            pltpu.SemaphoreType.DMA((3 * half_count,)),
        ],
        in_hbm=3,
        out_hbm=True,
    )
    packed, key_vectors, cluster = lax.optimization_barrier((packed, key_vectors, cluster))
    packed = exchange_inside(packed, half_count)
    ids = lane_rows(cluster[:, 0], ID_ROWS).astype(jnp.bfloat16)
    key_float = key_vectors.astype(jnp.float32)
    square_sum = sum_over_head(lane_rows(jnp.sum(key_float * key_float, axis=1), row_count))
    feature_total = HEADS * HEAD_DIM
    key_rms = jnp.sqrt(square_sum / feature_total + EPSILON)
    sent = call(
        functools.partial(pack_keys_kernel, half_count),
        [half_array(tokens + ID_ROWS, width)] * half_count
        + [half_array(2 * tokens + ID_ROWS, single)] * half_count,
        [me],
        [queries, values, cotangent, key_vectors, key_rms, ids],
    )
    cross = swap_across(sent[half_count:])
    key_sent = list(sent[:half_count])
    key_sent[1], cross[0] = lax.optimization_barrier((key_sent[1], cross[0]))
    keys = swap_inside(key_sent)
    pattern_rows = block_pattern.transpose(1, 0, 2).reshape(block_count, -1).astype(jnp.float32)
    pattern_rows = jnp.pad(pattern_rows, ((0, 0), (0, LANES - cluster_count * block_count)))
    wide = pltpu.VMEM((half_len, 2 * HEAD_DIM), jnp.bfloat16)
    slim = pltpu.VMEM((half_len, HEAD_DIM), jnp.bfloat16)
    sums = pltpu.VMEM((half_len, HEAD_DIM), jnp.float32)
    turned = pltpu.VMEM((HEAD_DIM, half_len), jnp.bfloat16)
    ids_column = pltpu.VMEM((half_len, 1), jnp.float32)
    block_flops = 12 * half_len * half_len * single
    inputs = [pattern_rows, packed] + cross + keys[::-1]
    stats = call(
        functools.partial(stats_kernel, shape, stat_rows),
        jax.ShapeDtypeStruct((3 * stat_rows * (single // HEAD_DIM), LANES), jnp.float32),
        [me],
        inputs,
        [wide, wide, slim, slim, ids_column, ids_column],
        flops=block_flops // 3,
    )
    far_stats = swap(stats, half_count)
    firsts = call(
        functools.partial(first_kernel, shape),
        [half_array(4 * tokens, single)] * half_count
        + [half_array(2 * tokens, single)] * half_count
        + [
            half_array(2 * half_len, single),
            jax.ShapeDtypeStruct((2 * half_len, single), jnp.float32),
        ],
        [me],
        inputs + [stats],
        [wide, wide, slim, slim, wide, slim, ids_column, ids_column, slim, slim]
        + [sums, sums, sums, sums] + [turned] * 4,
        flops=block_flops + block_flops // 2,
    )
    *firsts, far_stats = lax.optimization_barrier((*firsts, far_stats))
    rest = firsts[half_count:]
    firsts = swap_inside(firsts[:half_count])
    results = call(
        functools.partial(second_head_kernel, shape, stat_rows),
        [half_array(4 * tokens, single)] * half_count
        + [half_array(2 * tokens, single)] * half_count,
        [me],
        inputs + [stats, far_stats] + rest[half_count:] + rest[:half_count],
        [wide, wide, slim, slim, wide, slim, ids_column, ids_column, slim, slim]
        + [sums, sums, slim, slim] + [turned] * 2,
        flops=block_flops,
    )
    far_sent, seconds = list(results[half_count:]), list(results[:half_count])
    near = half_count // 2
    far_parts = swap_across(far_sent)
    seconds[2:], firsts, far_parts[-1] = lax.optimization_barrier((seconds[2:], firsts, far_parts[-1]))
    seconds[1], far_parts[0] = lax.optimization_barrier((seconds[1], far_parts[0]))
    seconds = swap_inside(seconds)
    inner = call(
        functools.partial(inner_kernel, half_count),
        jax.ShapeDtypeStruct((row_count, LANES), jnp.float32),
        [me],
        [key_vectors, key_rms] + far_parts + firsts + seconds,
    )
    inner = sum_over_head(inner)
    attended, query_grad, value_grad = call(
        functools.partial(final_kernel, half_count),
        [half_array(tokens, features)] * 3,
        [me],
        far_parts + firsts + seconds,
    )
    key_grad = call(
        functools.partial(key_kernel, half_count, feature_total),
        half_array(tokens, features),
        [me],
        [key_vectors, key_rms, inner] + far_parts + firsts + seconds,
    )
    return attended, query_grad, key_grad, value_grad


def per_device_any(queries, key_vectors, values, cotangent, cluster, block_pattern):
    count = lax.axis_size("seq")
    tokens, features = queries.shape
    cluster_count, block_count, _ = block_pattern.shape
    fits = (
        count % 2 == 0
        and count & (count - 1) == 0
        and count >= 4
        and tokens <= ID_ROWS * LANES
        and features % (count * HEAD_DIM) == 0
        and tokens % ID_ROWS == 0
        and tokens * count % (2 * BLK) == 0
        and cluster_count * block_count <= LANES
    )
    chosen = by_halves if fits else per_device
    return chosen(queries, key_vectors, values, cotangent, cluster, block_pattern)


def solution(mesh):
    in_specs = (
        P("seq", "head"),
        P("seq", "head"),
        P("seq", "head"),
        P("seq", "head"),
        P("seq", None),
        P(),
    )
    out_specs = (P("seq", "head"), P("seq", "head"), P("seq", "head"), P("seq", "head"))
    return jax.shard_map(
        per_device_any, mesh=mesh, in_specs=in_specs, out_specs=out_specs, check_vma=False
    )
```

```python
import functools

import jax
import jax.numpy as jnp
from jax import lax
from jax.experimental import pallas as pl
from jax.experimental.pallas import tpu as pltpu
from jax.sharding import PartitionSpec as P

HEADS = 32
HEAD_DIM = 128
GS = 4
BLK = 128


NEG_FILL = -1e30
EPSILON = 1e-05
SCORE_SCALE = HEAD_DIM ** (-0.5)
EXPONENT_SCALE = SCORE_SCALE * 1.4426950408889634
LANES = 128
ID_ROWS = 16
QUERY_TILE = 256
STATS_TILE = 384
VMEM_BYTES = 32 << 20
PACK_VMEM_BYTES = 60 << 20


def contract_last(left_side, right_side):
    return lax.dot_general(
        left_side, right_side, (((1,), (1,)), ((), ())), preferred_element_type=jnp.float32
    )


def contract_first(left_side, right_side):
    return lax.dot_general(
        left_side, right_side, (((0,), (0,)), ((), ())), preferred_element_type=jnp.float32
    )


def visible_mask(pattern, query_pos, query_live, key_pos, key_live):
    pattern_rows = pattern[query_pos // BLK]
    allowed = jnp.take(pattern_rows, key_pos // BLK, axis=1) == 1
    causal = key_pos[None, :] <= query_pos[:, None]
    return allowed & causal & query_live[:, None] & key_live[None, :]


def cluster_ranks(table, cluster_index):
    source_count, tok_count = table.shape
    in_cluster = table == cluster_index
    token_iota = jnp.arange(tok_count, dtype=jnp.int32)
    earlier_table = (token_iota[:, None] < token_iota[None, :]).astype(jnp.bfloat16)
    earlier = jnp.dot(
        in_cluster.astype(jnp.bfloat16), earlier_table, preferred_element_type=jnp.float32
    ).astype(jnp.int32)
    global_pos = (
        jnp.arange(source_count, dtype=jnp.int32)[:, None] * tok_count + token_iota[None, :]
    )
    return (in_cluster, earlier, global_pos)


def code_positions(slot_code, global_pos, capacity):
    matches = slot_code[:, :, None] == jnp.arange(capacity, dtype=jnp.int32)[None, None, :]
    positions = jnp.sum(jnp.where(matches, global_pos[:, :, None], 0), axis=1)
    occupied = jnp.any(matches, axis=1)
    return (positions, occupied)


def rank_positions(table, cluster_index, capacity):
    in_cluster, earlier, global_pos = cluster_ranks(table, cluster_index)
    rank_code = jnp.where(in_cluster, earlier, -1)
    positions, occupied = code_positions(rank_code, global_pos, capacity)
    return (positions.reshape(-1), occupied.reshape(-1))


def dispatch_rows(outgoing):
    return lax.all_to_all(outgoing, "seq", split_axis=1, concat_axis=1, tiled=True)


def combine_rows(outgoing):
    return lax.all_to_all(outgoing, "seq", split_axis=1, concat_axis=1, tiled=True)


def forward_heads(query_slots, key_slots, value_slots, grad_slots, visible, score_scale):
    query_count, features = query_slots.shape
    key_count = key_slots.shape[0]
    head_count = features // HEAD_DIM
    attended = jnp.zeros((query_count, features), jnp.bfloat16)
    query_grad = jnp.zeros((query_count, features), jnp.bfloat16)
    side_result = jnp.zeros((2, key_count, features), jnp.float32)

    def one_head(head_index, running):
        attended_acc, query_acc, side_acc = running
        column_start = head_index * HEAD_DIM
        query_rows = lax.dynamic_slice_in_dim(query_slots, column_start, HEAD_DIM, 1)
        key_rows = lax.dynamic_slice_in_dim(key_slots, column_start, HEAD_DIM, 1)
        value_rows = lax.dynamic_slice_in_dim(value_slots, column_start, HEAD_DIM, 1)
        grad_rows = lax.dynamic_slice_in_dim(grad_slots, column_start, HEAD_DIM, 1)
        scores = jnp.where(visible, contract_last(query_rows, key_rows) * score_scale, NEG_FILL)
        row_max = jnp.max(scores, axis=1, keepdims=True)
        weights = jnp.where(visible, jnp.exp(scores - row_max), 0.0)
        row_total = jnp.maximum(jnp.sum(weights, axis=1, keepdims=True), 1.0)
        probabilities = weights / row_total
        prob_half = probabilities.astype(jnp.bfloat16)
        attended_head = jnp.dot(prob_half, value_rows, preferred_element_type=jnp.float32).astype(
            jnp.bfloat16
        )
        prob_grad = contract_last(grad_rows, value_rows)
        row_delta = jnp.sum(probabilities * prob_grad, axis=1, keepdims=True)
        score_grad = (probabilities * (prob_grad - row_delta)).astype(jnp.bfloat16)
        query_head = (
            jnp.dot(score_grad, key_rows, preferred_element_type=jnp.float32) * score_scale
        ).astype(jnp.bfloat16)
        attended_acc = lax.dynamic_update_slice_in_dim(attended_acc, attended_head, column_start, 1)
        query_acc = lax.dynamic_update_slice_in_dim(query_acc, query_head, column_start, 1)
        key_part = contract_first(score_grad, query_rows)
        value_part = contract_first(prob_half, grad_rows)
        side_acc = lax.dynamic_update_slice_in_dim(
            side_acc, jnp.stack([key_part, value_part]), column_start, 2
        )
        return (attended_acc, query_acc, side_acc)

    return lax.fori_loop(0, head_count, one_head, (attended, query_grad, side_result))


def per_device(queries, key_vectors, values, cotangent, cluster, block_pattern):
    seq_count = lax.axis_size("seq")
    tok_count, features = queries.shape
    slot_count = 2 * tok_count // seq_count
    group_count = seq_count // GS
    score_scale = HEAD_DIM ** (-0.5)
    my_index = lax.axis_index("seq")
    group_index = my_index // GS
    key_float = key_vectors.astype(jnp.float32)
    square_sum = lax.psum(jnp.sum(key_float * key_float, axis=1), "head")
    key_rms = jnp.sqrt(square_sum / (HEADS * HEAD_DIM) + EPSILON)[:, None]
    normed_float = key_float / key_rms
    normed = normed_float.astype(jnp.bfloat16)
    own_ids = cluster[:, 0]
    everyone = lax.all_gather(own_ids, "seq", axis=0, tiled=True)
    table = everyone.reshape(seq_count, tok_count)
    token_iota = jnp.arange(tok_count, dtype=jnp.int32)
    onehot_own = (own_ids[:, None] == jnp.arange(group_count, dtype=jnp.int32)[None, :]).astype(
        jnp.bfloat16
    )
    before_table = (token_iota[:, None] > token_iota[None, :]).astype(jnp.bfloat16)
    before = jnp.dot(before_table, onehot_own, preferred_element_type=jnp.float32)
    own_rank = jnp.sum(before * onehot_own.astype(jnp.float32), axis=1).astype(jnp.int32)
    pattern = lax.dynamic_index_in_dim(block_pattern, group_index, 0, keepdims=False)
    stacked_inputs = jnp.stack([queries, normed, values, cotangent])
    quarter = features // GS
    capacity = GS * slot_count
    split_inputs = stacked_inputs.reshape(4, tok_count, GS, quarter)
    placed = (
        jnp.zeros((4, group_count, capacity, GS, quarter), jnp.bfloat16)
        .at[:, own_ids, own_rank]
        .set(split_inputs)
    )
    outgoing = placed.transpose(0, 1, 3, 2, 4).reshape(4, seq_count * capacity, quarter)
    arrived = dispatch_rows(outgoing)
    flat_positions, flat_present = rank_positions(table, group_index, capacity)
    visible = visible_mask(pattern, flat_positions, flat_present, flat_positions, flat_present)
    attended, query_grad, both_terms = forward_heads(
        arrived[0], arrived[1], arrived[2], arrived[3], visible, score_scale
    )
    normed_grad = (both_terms[0] * score_scale).astype(jnp.bfloat16)
    value_slots = both_terms[1].astype(jnp.bfloat16)
    outgoing_back = jnp.stack([attended, query_grad, normed_grad, value_slots])
    returned = combine_rows(outgoing_back)
    arranged = returned.reshape(4, group_count, GS, capacity, quarter).transpose(1, 3, 0, 2, 4)
    home_rows = arranged[own_ids, own_rank].transpose(1, 0, 2, 3).reshape(4, tok_count, features)
    grad_float = home_rows[2].astype(jnp.float32)
    inner = lax.psum(jnp.sum(normed_float * grad_float, axis=1), "head")
    key_grad = (
        (grad_float - normed_float * (inner / (HEADS * HEAD_DIM))[:, None]) / key_rms
    ).astype(jnp.bfloat16)
    return (home_rows[0], home_rows[1], key_grad, home_rows[3])


def column_of(rows, first_row, count):
    turned = jnp.transpose(rows)
    pieces = []
    for start in range(0, count, LANES):
        place = first_row + start // LANES
        pieces.append(turned[: min(LANES, count - start), place : place + 1])
    return jnp.concatenate(pieces, axis=0)


def ids_of(ref, first_row, count):
    rows = ref[first_row : first_row + ID_ROWS, :LANES].astype(jnp.float32)
    return column_of(rows, 0, count)


def store_as_rows(out_ref, first_row, column):
    count = column.shape[0]
    for start in range(0, count, LANES):
        size = min(LANES, count - start)
        diagonal = lax.broadcasted_iota(jnp.int32, (size, LANES), 0) == lax.broadcasted_iota(
            jnp.int32, (size, LANES), 1
        )
        spread = jnp.where(diagonal, column[start : start + size], 0.0)
        row = first_row + start // LANES
        out_ref[row : row + 1, :] = jnp.sum(spread, axis=0, keepdims=True)


def block_rows(index, size):
    return pl.ds(pl.multiple_of(index * size, 16), size)


def pack_kernel(half_count, query_ref, value_ref, grad_ref, out_ref, held, sorted_rows, in_sems, out_sems):
    tokens, features = query_ref.shape
    width = features // half_count
    arrivals = [
        pltpu.make_async_copy(source_ref, held.at[place], in_sems.at[place])
        for place, source_ref in enumerate((query_ref, value_ref, grad_ref))
    ]
    for arrival in arrivals:
        arrival.start()
    copies = []
    for place, arrival in enumerate(arrivals):
        arrival.wait()
        for owner in range(half_count):
            rows = pl.ds((owner * 3 + place) * tokens, tokens)
            sorted_rows[rows, :] = held[place, :, owner * width : (owner + 1) * width]
            copy = pltpu.make_async_copy(
                sorted_rows.at[rows, :], out_ref.at[rows, :], out_sems.at[place * half_count + owner]
            )
            copy.start()
            copies.append(copy)
    for copy in copies:
        copy.wait()


def pack_keys_kernel(
    half_count, me_ref, query_ref, value_ref, grad_ref, key_ref, rms_ref, ids_ref, *out_refs
):
    tokens, features = key_ref.shape
    width = features // half_count
    single = width // 2
    is_high = me_ref[0] >= half_count
    inside = me_ref[0] & (half_count - 1)
    key_refs, cross_refs = out_refs[:half_count], out_refs[half_count:]
    rms = column_of(rms_ref[...], 0, tokens)

    def normed_columns(first, size):
        return (key_ref[:, pl.ds(first, size)].astype(jnp.float32) / rms).astype(jnp.bfloat16)

    for distance in range(half_count):
        first = pl.multiple_of((inside ^ distance) * width, LANES)
        cross_ref = cross_refs[distance]
        key_refs[distance][:tokens, :] = normed_columns(first, width)
        key_refs[distance][tokens:, :LANES] = ids_ref[...]
        key_refs[distance][tokens:, LANES:] = jnp.zeros((ID_ROWS, width - LANES), jnp.bfloat16)
        cross_ref[2 * tokens :, :LANES] = ids_ref[...]
        if single > LANES:
            cross_ref[2 * tokens :, LANES:] = jnp.zeros((ID_ROWS, single - LANES), jnp.bfloat16)

        @pl.when(is_high)
        def send_down():
            second = pl.multiple_of(first + single, LANES)
            cross_ref[:tokens, :] = query_ref[:, pl.ds(second, single)]
            cross_ref[tokens : 2 * tokens, :] = grad_ref[:, pl.ds(second, single)]

        @pl.when(jnp.logical_not(is_high))
        def send_up():
            cross_ref[:tokens, :] = normed_columns(first, single)
            cross_ref[tokens : 2 * tokens, :] = value_ref[:, pl.ds(first, single)]


class Slots:
    def __init__(self, shape, me_ref, pattern_ref, packed_ref, key_refs, cross_refs):
        self.tokens, self.half_count, self.cluster_count, self.block_count = shape
        self.half_len = self.tokens * self.half_count
        self.half_blocks = self.half_len // BLK
        self.is_high = me_ref[0] >= self.half_count
        self.inside = me_ref[0] & (self.half_count - 1)
        self.pattern_ref, self.packed_ref = pattern_ref, packed_ref
        self.key_refs, self.cross_refs = key_refs, cross_refs
        lane = lax.broadcasted_iota(jnp.int32, (1, LANES), 1)
        lane_cluster = jnp.zeros((1, LANES), jnp.int32)
        for index in range(1, self.cluster_count + 1):
            lane_cluster = lane_cluster + (lane >= index * self.block_count).astype(jnp.int32)
        self.lane_block = lane - lane_cluster * self.block_count
        self.lane_cluster = lane_cluster.astype(jnp.float32)

    def own_ids(self, ids_all):
        for distance in range(self.half_count):
            ids_all[block_rows(self.inside ^ distance, self.tokens), :] = ids_of(
                self.key_refs[distance], self.tokens, self.tokens
            )

    def cross_ids(self, ids_all):
        for distance in range(self.half_count):
            ids_all[block_rows(self.inside ^ distance, self.tokens), :] = ids_of(
                self.cross_refs[distance], 2 * self.tokens, self.tokens
            )

    def query_features(self, ids_all, target, high):
        for block in range(self.half_blocks):
            rows = slice(block * BLK, (block + 1) * BLK)
            place = block + high * self.half_blocks
            allowed = self.pattern_ref[pl.ds(place, 1), :] == 1.0
            same = ids_all[rows, :] == self.lane_cluster
            target[rows, HEAD_DIM:] = jnp.where(same & allowed, 0.0, NEG_FILL).astype(jnp.bfloat16)

    def key_features(self, ids_all, target, high):
        for block in range(self.half_blocks):
            rows = slice(block * BLK, (block + 1) * BLK)
            place = block + high * self.half_blocks
            same = ids_all[rows, :] == self.lane_cluster
            target[rows, HEAD_DIM:] = jnp.where(same & (self.lane_block == place), 1.0, 0.0).astype(
                jnp.bfloat16
            )

    def own(self, column, query_all, key_all, value_all, grad_all):
        columns = slice(column, column + HEAD_DIM)
        stride = 3 * self.tokens
        for source in range(self.half_count):
            rows = slice(source * self.tokens, (source + 1) * self.tokens)
            for place, target in enumerate((query_all, value_all, grad_all)):
                first = source * stride + place * self.tokens
                target[rows, :HEAD_DIM] = self.packed_ref[first : first + self.tokens, columns]
        for distance in range(self.half_count):
            rows = block_rows(self.inside ^ distance, self.tokens)
            key_all[rows, :HEAD_DIM] = self.key_refs[distance][: self.tokens, columns]

    def cross(self, column, first_all, second_all):
        columns = slice(column, column + HEAD_DIM)
        for distance in range(self.half_count):
            rows = block_rows(self.inside ^ distance, self.tokens)
            cross_ref = self.cross_refs[distance]
            first_all[rows, :HEAD_DIM] = cross_ref[: self.tokens, columns]
            second_all[rows, :] = cross_ref[self.tokens : 2 * self.tokens, columns]


class Keys:
    def __init__(self, key, value, key_turned=None, value_turned=None):
        self.key, self.value = key, value
        self.key_turned, self.value_turned = key_turned, value_turned

    def turn(self):
        self.key_turned[...] = jnp.transpose(self.key[:, :HEAD_DIM])
        self.value_turned[...] = jnp.transpose(self.value[...])


def tile_scores(query_tile, keys, limit, first):
    scores = contract_last(keys.key[:limit, :], query_tile)
    if first is not None:
        key_index = lax.broadcasted_iota(jnp.int32, scores.shape, 0)
        query_index = lax.broadcasted_iota(jnp.int32, scores.shape, 1) + first
        scores = jnp.where(key_index <= query_index, scores, NEG_FILL)
    return scores


def tile_stats(scores, prob_grads):
    row_max = functools.reduce(
        jnp.maximum, [jnp.max(part, axis=0, keepdims=True) for part in scores]
    )
    weights = [jnp.exp2((part - row_max) * EXPONENT_SCALE) for part in scores]
    row_total = sum(jnp.sum(part, axis=0, keepdims=True) for part in weights)
    row_delta = sum(
        jnp.sum(part * grad, axis=0, keepdims=True) for part, grad in zip(weights, prob_grads)
    )
    return weights, row_max, row_total, row_delta


def tile_products(query_tile, grad_tile, pieces):
    scores = [tile_scores(query_tile, *piece) for piece in pieces]
    return scores, [contract_last(keys.value[:limit, :], grad_tile) for keys, limit, _ in pieces]


def all_tiles(query_all, grad_all, half_len, pieces_of, sums, stats_of, keep, add=False):
    tiles = own_tiles(half_len)
    ready = None
    for index, (first, rows, limit) in enumerate(tiles):
        now = ready or tile_products(query_all[rows, :], grad_all[rows, :], pieces_of(first, limit))
        ready = None
        if index + 1 < len(tiles):
            later, later_rows, later_limit = tiles[index + 1]
            ready = tile_products(
                query_all[later_rows, :], grad_all[later_rows, :], pieces_of(later, later_limit)
            )
        keep(
            rows,
            *tile_backward(
                query_all[rows, :],
                grad_all[rows, :],
                pieces_of(first, limit),
                sums,
                stats_of(first, limit - first) if stats_of else None,
                first == 0 and not add,
                *now,
            ),
        )


def tile_backward(query_tile, grad_tile, pieces, sums, stats, is_first, scores, prob_grads):
    if stats is None:
        weights, _, row_total, row_delta = tile_stats(scores, prob_grads)
        inverse = 1.0 / jnp.maximum(row_total, 1.0)
        row_delta = row_delta * inverse
    else:
        row_max, inverse, row_delta = stats
        weights = [jnp.exp2((part - row_max) * EXPONENT_SCALE) for part in scores]
    attended, query_grad = 0.0, 0.0
    for index, (keys, limit, first) in enumerate(pieces):
        probabilities = weights[index] * inverse
        prob_half = probabilities.astype(jnp.bfloat16)
        score_grad = (probabilities * (prob_grads[index] - row_delta)).astype(jnp.bfloat16)
        attended += jnp.dot(
            keys.value_turned[:, :limit], prob_half, preferred_element_type=jnp.float32
        )
        query_grad += jnp.dot(
            keys.key_turned[:, :limit], score_grad, preferred_element_type=jnp.float32
        )
        key_part = jnp.dot(
            score_grad, query_tile[:, :HEAD_DIM], preferred_element_type=jnp.float32
        )
        value_part = jnp.dot(prob_half, grad_tile, preferred_element_type=jnp.float32)
        key_sum, value_sum = sums[index]
        fresh = 0 if is_first else (limit if first is None else first)
        if fresh:
            key_sum[:fresh, :] += key_part[:fresh]
            value_sum[:fresh, :] += value_part[:fresh]
        if fresh < limit:
            key_sum[fresh:limit, :] = key_part[fresh:]
            value_sum[fresh:limit, :] = value_part[fresh:]
    return (
        jnp.transpose(attended).astype(jnp.bfloat16),
        jnp.transpose(query_grad * SCORE_SCALE).astype(jnp.bfloat16),
    )


def own_tiles(half_len, tile=QUERY_TILE):
    tile = tile if half_len % tile == 0 else BLK
    return [(first, slice(first, first + tile), first + tile) for first in range(0, half_len, tile)]


def note_stats(out_ref, stat_rows, head, first, found):
    for place, column in enumerate(found[1:]):
        store_as_rows(out_ref, (3 * head + place) * stat_rows + first // LANES, column)


def stats_kernel(shape, stat_rows, me_ref, pattern_ref, packed_ref, *refs):
    half_count = shape[1]
    cross_refs, key_refs = refs[:half_count], refs[half_count : 2 * half_count][::-1]
    out_ref, query_all, key_all, value_all, grad_all, ids, other_ids = refs[2 * half_count :]
    slots = Slots(shape, me_ref, pattern_ref, packed_ref, key_refs, cross_refs)
    single = packed_ref.shape[1] // 2
    out_ref[...] = jnp.zeros_like(out_ref)
    slots.own_ids(ids)
    slots.key_features(ids, key_all, slots.is_high.astype(jnp.int32))

    @pl.when(slots.is_high)
    def _():
        slots.query_features(ids, query_all, 1)

    @pl.when(jnp.logical_not(slots.is_high))
    def _():
        slots.cross_ids(other_ids)
        slots.query_features(other_ids, query_all, 1)

    for head in range(single // HEAD_DIM):
        column = head * HEAD_DIM
        slots.own(single + column, query_all, key_all, value_all, grad_all)

        def note(first, rows, limit, causal_from):
            scores = tile_scores(query_all[rows, :], Keys(key_all, value_all), limit, causal_from)
            prob_grad = contract_last(value_all[:limit, :], grad_all[rows, :])
            for place, found in enumerate(tile_stats([scores], [prob_grad])[1:]):
                row = (3 * head + place) * stat_rows + first // LANES
                for start in range(0, found.shape[1], LANES):
                    out_ref[row + start // LANES : row + start // LANES + 1, :] = found[
                        :, start : start + LANES
                    ]

        @pl.when(slots.is_high)
        def _():
            for first, rows, limit in own_tiles(slots.half_len, STATS_TILE):
                note(first, rows, limit, first)

        @pl.when(jnp.logical_not(slots.is_high))
        def _():
            slots.cross(column, query_all, grad_all)
            for first, rows, _ in own_tiles(slots.half_len, STATS_TILE):
                note(first, rows, slots.half_len, None)


def store_own(slots, result_refs, column, attended, query_grad, value_sum, key_sum):
    tokens = slots.tokens
    columns = slice(column, column + HEAD_DIM)
    for distance, target in enumerate(result_refs):
        rows = block_rows(slots.inside ^ distance, tokens)
        target[:tokens, columns] = attended[rows, :]
        target[tokens : 2 * tokens, columns] = query_grad[rows, :]
        target[2 * tokens : 3 * tokens, columns] = value_sum[rows, :].astype(jnp.bfloat16)
        target[3 * tokens :, columns] = (key_sum[rows, :] * SCORE_SCALE).astype(jnp.bfloat16)


def first_kernel(shape, me_ref, pattern_ref, packed_ref, *refs):
    half_count = shape[1]
    cross_refs, key_refs = refs[:half_count], refs[half_count : 2 * half_count][::-1]
    refs = refs[2 * half_count + 1 :]
    result_refs, cross_out_refs = refs[:half_count], refs[half_count : 2 * half_count]
    second_ref, sums_ref = refs[2 * half_count : 2 * half_count + 2]
    (query_all, key_all, value_all, grad_all, other_key, other_value, ids, other_ids, attended,
     query_grad, key_sum, value_sum, other_key_sum, other_value_sum, *turned) = refs[
        2 * half_count + 2 :
    ]
    own, other = Keys(key_all, value_all, *turned[:2]), Keys(other_key, other_value, *turned[2:])
    slots = Slots(shape, me_ref, pattern_ref, packed_ref, key_refs, cross_refs)
    single = packed_ref.shape[1] // 2
    half_len = slots.half_len
    high = slots.is_high.astype(jnp.int32)
    slots.own_ids(ids)
    slots.key_features(ids, key_all, high)
    slots.query_features(ids, query_all, high)

    def run(others, other_sums, attended_out, query_grad_out, key_out, value_out):
        def keep(rows, attended_tile, query_grad_tile):
            attended_out[rows, :], query_grad_out[rows, :] = attended_tile, query_grad_tile

        all_tiles(
            query_all,
            grad_all,
            half_len,
            lambda first, limit: others + [(own, limit, first)],
            other_sums + [(key_out, value_out)],
            None,
            keep,
        )

    @pl.when(slots.is_high)
    def _():
        slots.cross_ids(other_ids)
        slots.key_features(other_ids, other_key, 0)

    for head in range(single // HEAD_DIM):
        column = head * HEAD_DIM
        columns = slice(column, column + HEAD_DIM)
        slots.own(column, query_all, key_all, value_all, grad_all)
        own.turn()

        @pl.when(slots.is_high)
        def _():
            slots.cross(column, other_key, other_value)
            other.turn()
            run(
                [(other, half_len, None)],
                [(other_key_sum, other_value_sum)],
                attended, query_grad, key_sum, value_sum,
            )
            for distance in range(half_count):
                rows = block_rows(slots.inside ^ distance, slots.tokens)
                target = cross_out_refs[distance]
                target[: slots.tokens, columns] = (other_key_sum[rows, :] * SCORE_SCALE).astype(
                    jnp.bfloat16
                )
                target[slots.tokens :, columns] = other_value_sum[rows, :].astype(jnp.bfloat16)

        @pl.when(jnp.logical_not(slots.is_high))
        def _():
            run([], [], attended, query_grad, key_sum, value_sum)

        store_own(slots, result_refs, column, attended, query_grad, value_sum, key_sum)

        @pl.when(jnp.logical_not(slots.is_high))
        def _():
            slots.own(single + column, query_all, key_all, value_all, grad_all)
            own.turn()
            run(
                [], [],
                second_ref.at[:half_len, columns],
                second_ref.at[half_len:, columns],
                sums_ref.at[:half_len, columns],
                sums_ref.at[half_len:, columns],
            )


def joint_rows(stat_rows, head, own_stats_ref, far_stats_ref):
    (own_max, own_total, own_delta), (far_max, far_total, far_delta) = [
        [
            ref[(3 * head + place) * stat_rows : (3 * head + place + 1) * stat_rows, :]
            for place in range(3)
        ]
        for ref in (own_stats_ref, far_stats_ref)
    ]
    row_max = jnp.maximum(own_max, far_max)
    own_part = jnp.exp2((own_max - row_max) * EXPONENT_SCALE)
    far_part = jnp.exp2((far_max - row_max) * EXPONENT_SCALE)
    inverse = 1.0 / jnp.maximum(own_total * own_part + far_total * far_part, 1.0)
    return row_max, inverse, (own_delta * own_part + far_delta * far_part) * inverse


def second_head_kernel(shape, stat_rows, me_ref, pattern_ref, packed_ref, *refs):
    half_count = shape[1]
    cross_refs, key_refs = refs[:half_count], refs[half_count : 2 * half_count][::-1]
    own_stats_ref, far_stats_ref, early_ref, sums_ref = refs[2 * half_count : 2 * half_count + 4]
    refs = refs[2 * half_count + 4 :]
    first_cross_refs, result_refs, cross_out_refs = [
        refs[place * half_count : (place + 1) * half_count] for place in range(3)
    ]
    (query_all, key_all, value_all, grad_all, other_query, other_grad, ids, other_ids, attended,
     query_grad, key_sum, value_sum, other_attended, other_query_grad, *turned) = refs[
        3 * half_count :
    ]
    own = Keys(key_all, value_all, *turned)
    slots = Slots(shape, me_ref, pattern_ref, packed_ref, key_refs, cross_refs)
    single = packed_ref.shape[1] // 2
    half_len, tokens = slots.half_len, slots.tokens
    slots.own_ids(ids)
    slots.key_features(ids, key_all, slots.is_high.astype(jnp.int32))

    @pl.when(slots.is_high)
    def _():
        slots.query_features(ids, query_all, 1)
        for distance in range(half_count):
            cross_out_refs[distance][...] = first_cross_refs[distance][...]

    @pl.when(jnp.logical_not(slots.is_high))
    def _():
        slots.cross_ids(other_ids)
        slots.query_features(other_ids, other_query, 1)

    for head in range(single // HEAD_DIM):
        column = head * HEAD_DIM
        columns = slice(column, column + HEAD_DIM)
        slots.own(single + column, query_all, key_all, value_all, grad_all)
        own.turn()
        joint_table = joint_rows(stat_rows, head, own_stats_ref, far_stats_ref)

        def joint_stats(first, size):
            places = range(first // LANES, (first + size) // LANES)
            return [
                jnp.concatenate([rows[place : place + 1, :] for place in places], axis=1)
                for rows in joint_table
            ]

        @pl.when(slots.is_high)
        def _():
            def keep(rows, attended_tile, query_grad_tile):
                attended[rows, :], query_grad[rows, :] = attended_tile, query_grad_tile

            all_tiles(
                query_all,
                grad_all,
                half_len,
                lambda first, limit: [(own, limit, first)],
                [(key_sum, value_sum)],
                joint_stats,
                keep,
            )

        @pl.when(jnp.logical_not(slots.is_high))
        def _():
            slots.cross(column, other_query, other_grad)
            attended[...] = early_ref[:half_len, columns]
            query_grad[...] = early_ref[half_len:, columns]
            key_sum[...] = sums_ref[:half_len, columns]
            value_sum[...] = sums_ref[half_len:, columns]

            def keep(rows, attended_tile, query_grad_tile):
                other_attended[rows, :], other_query_grad[rows, :] = attended_tile, query_grad_tile

            all_tiles(
                other_query,
                other_grad,
                half_len,
                lambda first, limit: [(own, half_len, None)],
                [(key_sum, value_sum)],
                joint_stats,
                keep,
                add=True,
            )
            for distance in range(half_count):
                rows = block_rows(slots.inside ^ distance, tokens)
                target = cross_out_refs[distance]
                target[:tokens, columns] = other_attended[rows, :]
                target[tokens:, columns] = other_query_grad[rows, :]

        store_own(slots, result_refs, column, attended, query_grad, value_sum, key_sum)


def normed_grad_of(half_count, me_ref, first_ref, second_ref, cross_ref):
    tokens = second_ref.shape[0] // 4
    is_low = me_ref[0] < half_count
    far = jnp.where(is_low, cross_ref[:tokens, :].astype(jnp.float32), 0.0)
    first_float = first_ref[3 * tokens :, :].astype(jnp.float32) + far
    second_float = second_ref[3 * tokens :, :].astype(jnp.float32)
    return jnp.concatenate([first_float, second_float], axis=1)


def inner_kernel(half_count, me_ref, key_ref, rms_ref, *refs):
    cross_refs, first_refs, second_refs = [
        refs[place * half_count : (place + 1) * half_count] for place in range(3)
    ]
    out_ref = refs[3 * half_count]
    tokens, features = key_ref.shape
    width = features // half_count
    inside = me_ref[0] & (half_count - 1)
    total = jnp.zeros((tokens, width), jnp.float32)
    for distance in range(half_count):
        owner = inside ^ distance
        start = pl.multiple_of(owner * width, LANES)
        key_float = key_ref[:, pl.ds(start, width)].astype(jnp.float32)
        total = total + key_float * normed_grad_of(
            half_count, me_ref, first_refs[distance], second_refs[distance], cross_refs[distance]
        )
    column = jnp.sum(total, axis=1, keepdims=True) / column_of(rms_ref[...], 0, tokens)
    out_ref[...] = jnp.zeros_like(out_ref)
    store_as_rows(out_ref, 0, column)


def key_kernel(half_count, feature_total, me_ref, key_ref, rms_ref, inner_ref, *refs):
    cross_refs, first_refs, second_refs = [
        refs[place * half_count : (place + 1) * half_count] for place in range(3)
    ]
    key_out_ref = refs[3 * half_count]
    tokens, features = key_ref.shape
    width = features // half_count
    inside = me_ref[0] & (half_count - 1)
    inverse = 1.0 / column_of(rms_ref[...], 0, tokens)
    inner = column_of(inner_ref[...], 0, tokens) * inverse / feature_total
    for distance in range(half_count):
        columns = pl.ds(pl.multiple_of((inside ^ distance) * width, LANES), width)
        key_float = key_ref[:, columns].astype(jnp.float32)
        grad_float = normed_grad_of(
            half_count, me_ref, first_refs[distance], second_refs[distance], cross_refs[distance]
        )
        key_out_ref[:, columns] = ((grad_float - key_float * inner) * inverse).astype(jnp.bfloat16)


def final_kernel(half_count, me_ref, *refs):
    cross_refs, first_refs, second_refs = [
        refs[place * half_count : (place + 1) * half_count] for place in range(3)
    ]
    attended_ref, query_ref, value_ref = refs[3 * half_count :]
    tokens, features = attended_ref.shape
    width = features // half_count
    single = width // 2
    is_high = me_ref[0] >= half_count
    inside = me_ref[0] & (half_count - 1)
    for distance in range(half_count):
        start = pl.multiple_of((inside ^ distance) * width, LANES)
        first = pl.ds(start, single)
        second = pl.ds(pl.multiple_of(start + single, LANES), single)
        cross_ref = cross_refs[distance]

        def block(refs, place):
            return refs[distance][place * tokens : (place + 1) * tokens, :]

        def joined(refs, place, far):
            whole = block(refs, place).astype(jnp.float32) + cross_ref[
                far * tokens : (far + 1) * tokens, :
            ].astype(jnp.float32)
            return whole.astype(jnp.bfloat16)

        attended_ref[:, first] = block(first_refs, 0)
        query_ref[:, first] = block(first_refs, 1)
        value_ref[:, second] = block(second_refs, 2)

        @pl.when(is_high)
        def _():
            attended_ref[:, second] = joined(second_refs, 0, 0)
            query_ref[:, second] = joined(second_refs, 1, 1)
            value_ref[:, first] = block(first_refs, 2)

        @pl.when(jnp.logical_not(is_high))
        def _():
            attended_ref[:, second] = block(second_refs, 0)
            query_ref[:, second] = block(second_refs, 1)
            value_ref[:, first] = joined(first_refs, 2, 1)


def lane_rows(vector, row_count):
    return jnp.pad(vector, (0, row_count * LANES - vector.shape[0])).reshape(row_count, LANES)


def half_array(rows, columns):
    return jax.ShapeDtypeStruct((rows, columns), jnp.bfloat16)


def call(kernel, out_shapes, scalars, arrays, scratch=(), in_hbm=0, out_hbm=False, flops=0):
    vmem, anywhere = pl.BlockSpec(memory_space=pltpu.VMEM), pl.BlockSpec(memory_space=pl.ANY)
    return pl.pallas_call(
        kernel,
        out_shape=out_shapes,
        in_specs=[pl.BlockSpec(memory_space=pltpu.SMEM)] * len(scalars)
        + [anywhere] * in_hbm
        + [vmem] * (len(arrays) - in_hbm),
        out_specs=jax.tree.map(lambda shape: anywhere if out_hbm else vmem, out_shapes),
        scratch_shapes=list(scratch),
        compiler_params=pltpu.CompilerParams(vmem_limit_bytes=PACK_VMEM_BYTES if in_hbm else VMEM_BYTES),
        cost_estimate=pl.CostEstimate(flops=flops, bytes_accessed=0, transcendentals=0) if flops else None,
    )(*scalars, *arrays)


def swap(block, distance):
    count = lax.axis_size("seq")
    return lax.ppermute(block, "seq", [(i, i ^ distance) for i in range(count)])


def swap_inside(blocks):
    return [blocks[0]] + [swap(block, d) for d, block in enumerate(blocks) if d]


def swap_across(blocks):
    return [swap(block, len(blocks) + d) for d, block in enumerate(blocks)]


def exchange_inside(rows, half_count):
    count = 2 * half_count
    groups = [list(range(half_count)), list(range(half_count, count))]
    parts = rows.reshape(half_count, -1, rows.shape[1])
    return lax.all_to_all(
        parts, "seq", split_axis=0, concat_axis=0, tiled=True, axis_index_groups=groups
    ).reshape(rows.shape)


def sum_over_head(block):
    count = lax.axis_size("head")
    if count & (count - 1):
        return lax.psum(block, "head")
    return block + sum(
        lax.ppermute(block, "head", [(i, i ^ d) for i in range(count)]) for d in range(1, count)
    )


def by_halves(queries, key_vectors, values, cotangent, cluster, block_pattern):
    count = lax.axis_size("seq")
    half_count = count // 2
    tokens, features = queries.shape
    width = features // half_count
    single = width // 2
    cluster_count, block_count, _ = block_pattern.shape
    half_len = half_count * tokens
    shape = (tokens, half_count, cluster_count, block_count)
    row_count = -(-tokens // (8 * LANES)) * 8
    stat_rows = -(-half_len // (8 * LANES)) * 8
    me = lax.axis_index("seq").astype(jnp.int32).reshape(1)
    packed_shape = half_array(half_count * 3 * tokens, width)
    packed = call(
        functools.partial(pack_kernel, half_count),
        packed_shape,
        [],
        [queries, values, cotangent],
        [
            pltpu.VMEM((3, tokens, features), jnp.bfloat16),
            pltpu.VMEM(packed_shape.shape, jnp.bfloat16),
            pltpu.SemaphoreType.DMA((3,)),
            pltpu.SemaphoreType.DMA((3 * half_count,)),
        ],
        in_hbm=3,
        out_hbm=True,
    )
    packed, key_vectors, cluster = lax.optimization_barrier((packed, key_vectors, cluster))
    packed = exchange_inside(packed, half_count)
    ids = lane_rows(cluster[:, 0], ID_ROWS).astype(jnp.bfloat16)
    key_float = key_vectors.astype(jnp.float32)
    square_sum = sum_over_head(lane_rows(jnp.sum(key_float * key_float, axis=1), row_count))
    feature_total = HEADS * HEAD_DIM
    key_rms = jnp.sqrt(square_sum / feature_total + EPSILON)
    sent = call(
        functools.partial(pack_keys_kernel, half_count),
        [half_array(tokens + ID_ROWS, width)] * half_count
        + [half_array(2 * tokens + ID_ROWS, single)] * half_count,
        [me],
        [queries, values, cotangent, key_vectors, key_rms, ids],
    )
    cross = swap_across(sent[half_count:])
    key_sent = list(sent[:half_count])
    key_sent[1], cross[0] = lax.optimization_barrier((key_sent[1], cross[0]))
    keys = swap_inside(key_sent)
    pattern_rows = block_pattern.transpose(1, 0, 2).reshape(block_count, -1).astype(jnp.float32)
    pattern_rows = jnp.pad(pattern_rows, ((0, 0), (0, LANES - cluster_count * block_count)))
    wide = pltpu.VMEM((half_len, 2 * HEAD_DIM), jnp.bfloat16)
    slim = pltpu.VMEM((half_len, HEAD_DIM), jnp.bfloat16)
    sums = pltpu.VMEM((half_len, HEAD_DIM), jnp.float32)
    turned = pltpu.VMEM((HEAD_DIM, half_len), jnp.bfloat16)
    ids_column = pltpu.VMEM((half_len, 1), jnp.float32)
    block_flops = 12 * half_len * half_len * single
    inputs = [pattern_rows, packed] + cross + keys[::-1]
    stats = call(
        functools.partial(stats_kernel, shape, stat_rows),
        jax.ShapeDtypeStruct((3 * stat_rows * (single // HEAD_DIM), LANES), jnp.float32),
        [me],
        inputs,
        [wide, wide, slim, slim, ids_column, ids_column],
        flops=block_flops // 3,
    )
    far_stats = swap(stats, half_count)
    firsts = call(
        functools.partial(first_kernel, shape),
        [half_array(4 * tokens, single)] * half_count
        + [half_array(2 * tokens, single)] * half_count
        + [
            half_array(2 * half_len, single),
            jax.ShapeDtypeStruct((2 * half_len, single), jnp.float32),
        ],
        [me],
        inputs + [stats],
        [wide, wide, slim, slim, wide, slim, ids_column, ids_column, slim, slim]
        + [sums, sums, sums, sums] + [turned] * 4,
        flops=block_flops + block_flops // 2,
    )
    *firsts, far_stats = lax.optimization_barrier((*firsts, far_stats))
    rest = firsts[half_count:]
    own_first, near_first, *rest_firsts = firsts[:half_count]
    rest_firsts = [swap(block, d) for d, block in enumerate(rest_firsts, 2)]
    results = call(
        functools.partial(second_head_kernel, shape, stat_rows),
        [half_array(4 * tokens, single)] * half_count
        + [half_array(2 * tokens, single)] * half_count,
        [me],
        inputs + [stats, far_stats] + rest[half_count:] + rest[:half_count],
        [wide, wide, slim, slim, wide, slim, ids_column, ids_column, slim, slim]
        + [sums, sums, slim, slim] + [turned] * 2,
        flops=block_flops,
    )
    far_sent, seconds = list(results[half_count:]), list(results[:half_count])
    near = half_count // 2
    far_parts = swap_across(far_sent)
    near_first, far_sent = lax.optimization_barrier((near_first, far_sent))
    firsts = [own_first, swap(near_first, 1)] + rest_firsts
    seconds[2:], rest_firsts, far_parts[-1] = lax.optimization_barrier(
        (seconds[2:], rest_firsts, far_parts[-1])
    )
    firsts[2:] = rest_firsts
    seconds[1], far_parts[0] = lax.optimization_barrier((seconds[1], far_parts[0]))
    seconds = swap_inside(seconds)
    inner = call(
        functools.partial(inner_kernel, half_count),
        jax.ShapeDtypeStruct((row_count, LANES), jnp.float32),
        [me],
        [key_vectors, key_rms] + far_parts + firsts + seconds,
    )
    inner = sum_over_head(inner)
    attended, query_grad, value_grad = call(
        functools.partial(final_kernel, half_count),
        [half_array(tokens, features)] * 3,
        [me],
        far_parts + firsts + seconds,
    )
    key_grad = call(
        functools.partial(key_kernel, half_count, feature_total),
        half_array(tokens, features),
        [me],
        [key_vectors, key_rms, inner] + far_parts + firsts + seconds,
    )
    return attended, query_grad, key_grad, value_grad


def per_device_any(queries, key_vectors, values, cotangent, cluster, block_pattern):
    count = lax.axis_size("seq")
    tokens, features = queries.shape
    cluster_count, block_count, _ = block_pattern.shape
    fits = (
        count % 2 == 0
        and count & (count - 1) == 0
        and count >= 4
        and tokens <= ID_ROWS * LANES
        and features % (count * HEAD_DIM) == 0
        and tokens % ID_ROWS == 0
        and tokens * count % (2 * BLK) == 0
        and cluster_count * block_count <= LANES
    )
    chosen = by_halves if fits else per_device
    return chosen(queries, key_vectors, values, cotangent, cluster, block_pattern)


def solution(mesh):
    in_specs = (
        P("seq", "head"),
        P("seq", "head"),
        P("seq", "head"),
        P("seq", "head"),
        P("seq", None),
        P(),
    )
    out_specs = (P("seq", "head"), P("seq", "head"), P("seq", "head"), P("seq", "head"))
    return jax.shard_map(
        per_device_any, mesh=mesh, in_specs=in_specs, out_specs=out_specs, check_vma=False
    )
```
